256 devices in a mesh: expert: 64 (over z, x, core), dp: 4 (over y).
Axes of the slice: x: 4, y: 4, z: 8, core: 2. Of those that a mesh axis runs over, the one named last changes fastest.
Arguments:
- features: bfloat16 [32768, 32, 64], P(('expert', 'dp')), may hold values from -1 to 1
- spacing: float32 [32768, 32], P(('expert', 'dp')), may hold values from 0.02 to 0.3
- targets: float32 [3, 32768], P(None, ('expert', 'dp')), may hold values from 0 to 1
- ray_length: int32 [32768], P(('expert', 'dp')), may hold values from 1 to 32, as said below
- cell_id: int32 [32768, 32], P(('expert', 'dp')), may hold values from 0 to 127, as said below
- slot_rank: int32 [32768, 32], P(('expert', 'dp')), may hold values from -1 to 47, as said below
- image_id: int32 [32768], P(('expert', 'dp')), may hold values from 0 to 4095, as said below
- params: float32 [128, 848, 256], P('expert'), may hold values from -5 to 5
- first_moment: float32 [128, 848, 256], P('expert'), may hold values from -0.75 to 0.75
- second_moment: float32 [128, 848, 256], P('expert'), may hold values from 1e-06 to 0.01
- code_table: float32 [4096, 64], P(('expert', 'dp')), may hold values from -6 to 6
- table_first: float32 [4096, 64], P(('expert', 'dp')), may hold values from -0.75 to 0.75
- table_second: float32 [4096, 64], P(('expert', 'dp')), may hold values from 1e-06 to 0.01
Outputs:
- ray_loss: float32 [32768], P(('expert', 'dp'))
- new_params: float32 [128, 848, 256], P('expert')
- new_first_moment: float32 [128, 848, 256], P('expert')
- new_second_moment: float32 [128, 848, 256], P('expert')
- new_code_table: float32 [4096, 64], P(('expert', 'dp'))
- new_table_first: float32 [4096, 64], P(('expert', 'dp'))
- new_table_second: float32 [4096, 64], P(('expert', 'dp'))
The draws below stay inside these ranges and needn't reach their ends.
Inputs may be any that keep to these rules, and one draw needn't show every extreme that they name: `ray_length`: rays form aligned blocks of 128, one a device, in the order of the axes expert then dp. In every block the lengths sum to 3072 and some ray has all 32 samples. `cell_id`: also given for samples at or beyond their ray's length, where it is unused. `slot_rank`: for a sample below its ray's length: its rank among the live samples of its block of 128 rays that have the same cell_id, counted ray by ray and along each ray; -1 for the other samples. No block has more than 48 live samples of one cell_id; in every block some cell_id has exactly 48, and one cell_id has 48 in every block. `image_id`: A ray of block b names an image from b * 16 to (b + 1) * 16 - 1.
All inputs are finite; a program needn't handle non-finite values.
Results may differ from the reference program's by a relative error of at most 0.0046.
Values may be sent and summed in bfloat16 or wider, within the bound.
No kernel may reach another device: no remote copies, remote signals or barrier semaphores. Data moves between devices by JAX's collectives and lax.ppermute only.
A program may use at most 128 MiB of HBM per device.

```python
import math
import jax
import jax.numpy as jnp
from jax import lax

NET_WIDTH = 256
CODE_WIDTH = 64
ENC_WIDTH = 64
LAYERS = 4
SAMPLES = 32
IMG_DEV = 16
RAY_DEV = 128
EXPERTS = 128
RAY_TOTAL = 32768
IMAGES = 4096
LIVE_DEV = 3072
CAPACITY = 48
PARAM_ROWS = 848


def sample_layout(key):
    blocks = RAY_TOTAL // RAY_DEV
    hot_all = jax.random.randint(jax.random.fold_in(key, 11), (), 0, EXPERTS)

    def one_block(block_number):
        subkeys = jax.random.split(jax.random.fold_in(key, block_number), 7)
        drop_units = RAY_DEV * (SAMPLES - 1)
        unit_ray = jnp.arange(drop_units, dtype=jnp.int32) // (SAMPLES - 1)
        full_ray = jax.random.randint(subkeys[0], (), 0, RAY_DEV)
        shuffled = jax.random.permutation(subkeys[1], drop_units).astype(jnp.int32)
        ranking = shuffled + jnp.where(unit_ray == full_ray, drop_units, 0).astype(jnp.int32)
        picked = jnp.argsort(ranking)[:RAY_DEV * SAMPLES // 4]
        dropped = jnp.zeros((RAY_DEV,), jnp.int32).at[unit_ray[picked]].add(1)
        lengths = (SAMPLES - dropped).astype(jnp.int32)
        pair_count = EXPERTS * CAPACITY
        pair_cell = jnp.arange(pair_count, dtype=jnp.int32) // CAPACITY
        own_hot = jax.random.randint(subkeys[2], (), 0, EXPERTS)
        cell_bias = jax.random.randint(subkeys[3], (EXPERTS,), 0, 4)
        cell_range = jnp.arange(EXPERTS, dtype=jnp.int32)
        cell_bias = jnp.where((cell_range == hot_all) | (cell_range == own_hot), 16, cell_bias).astype(jnp.int32)
        pair_score = cell_bias[pair_cell] * (pair_count // 4) + jax.random.permutation(subkeys[4], pair_count).astype(jnp.int32)
        chosen = pair_cell[jnp.argsort(-pair_score)[:LIVE_DEV]]
        chosen = chosen[jax.random.permutation(subkeys[5], LIVE_DEV)]
        position = jnp.arange(SAMPLES, dtype=jnp.int32)
        flat_live = (position[None, :] < lengths[:, None]).reshape(RAY_DEV * SAMPLES)
        rank_live = jnp.cumsum(flat_live.astype(jnp.int32)) - 1
        dead_cell = jax.random.randint(subkeys[6], (RAY_DEV * SAMPLES,), 0, EXPERTS)
        cell_ids = jnp.where(flat_live, chosen[jnp.clip(rank_live, 0, LIVE_DEV - 1)], dead_cell).astype(jnp.int32)
        onehot = (cell_ids[:, None] == cell_range[None, :]) & flat_live[:, None]
        counts = jnp.cumsum(onehot.astype(jnp.int32), axis=0) - 1
        slot_ranks = jnp.where(flat_live, jnp.take_along_axis(counts, cell_ids[:, None], axis=1)[:, 0], -1).astype(jnp.int32)
        return (lengths, cell_ids.reshape(RAY_DEV, SAMPLES), slot_ranks.reshape(RAY_DEV, SAMPLES))
    lengths, cell_ids, slot_ranks = lax.map(one_block, jnp.arange(blocks, dtype=jnp.int32))
    return (lengths.reshape(RAY_TOTAL), cell_ids.reshape(RAY_TOTAL, SAMPLES), slot_ranks.reshape(RAY_TOTAL, SAMPLES))


def draw_ray_length(key, part):
    return sample_layout(jax.random.fold_in(key, 5))[0]


def draw_cell_id(key, part):
    return sample_layout(jax.random.fold_in(key, 5))[1]


def draw_slot_rank(key, part):
    return sample_layout(jax.random.fold_in(key, 5))[2]


def draw_image_id(key, part):
    blocks = RAY_TOTAL // RAY_DEV
    local_ids = jax.random.randint(key, (blocks, RAY_DEV), 0, IMG_DEV)
    marked = jax.random.randint(jax.random.fold_in(key, 3), (blocks, 2), 0, RAY_DEV)
    row_number = jnp.arange(blocks, dtype=jnp.int32)
    local_ids = local_ids.at[row_number, marked[:, 1]].set(0)
    local_ids = local_ids.at[row_number, marked[:, 0]].set(IMG_DEV - 1)
    global_ids = local_ids + (row_number * IMG_DEV)[:, None]
    return global_ids.reshape(RAY_TOTAL).astype(jnp.int32)


def draw_params(key, part):
    head_row = ENC_WIDTH + (LAYERS - 1) * NET_WIDTH
    row_number = jnp.arange(PARAM_ROWS)
    row_scale = jnp.where(row_number < ENC_WIDTH, (2.0 / ENC_WIDTH) ** 0.5, (2.0 / NET_WIDTH) ** 0.5)
    row_scale = jnp.where(row_number >= head_row, NET_WIDTH ** (-0.5), row_scale)
    row_scale = jnp.where(row_number >= head_row + 4, 4.0 * CODE_WIDTH ** (-0.5), row_scale)
    row_scale = jnp.where(row_number >= head_row + 8, 0.3, row_scale)
    normals = jnp.clip(jax.random.normal(key, (EXPERTS, PARAM_ROWS, NET_WIDTH), jnp.float32), -5.0, 5.0)
    return normals * row_scale[None, :, None].astype(jnp.float32)


def levels(rng, shape, cuts, least, top_value):
    gain = 1.0
    for dim, parts in cuts:
        heights = jax.random.uniform(jax.random.fold_in(jax.random.fold_in(rng, 6), dim), (parts,), jnp.float32, least / len(cuts), top_value / len(cuts))
        gain = gain * jnp.repeat(jnp.exp(heights), shape[dim] // parts).reshape((-1,) + (1,) * (len(shape) - 1 - dim))
    return gain


def normal_values(stream_key, dims, deviation, limit, shards=(), kind=jnp.bfloat16):
    level = levels(stream_key, dims, shards, -0.22, 0.18) if shards else 1.0
    values = jax.random.normal(stream_key, dims, jnp.float32) * deviation * level
    return jnp.minimum(jnp.maximum(values, -limit), limit).astype(kind)


def setup_inputs(seed: int = 0) -> dict:
    key_list = jax.random.split(jax.random.key(seed), 14)
    return {
        "features": jnp.clip(jax.random.uniform(key_list[0], (RAY_TOTAL, SAMPLES, ENC_WIDTH), jnp.float32, -1.0, 1.0) * levels(key_list[0], (RAY_TOTAL, SAMPLES, ENC_WIDTH), ((0, 256),), -0.4, 0.0), -1.0, 1.0).astype(jnp.bfloat16),
        "spacing": jnp.clip(jnp.exp(math.log(0.3) - 2.7080503 * jax.random.uniform(key_list[1], (RAY_TOTAL, SAMPLES), jnp.float32) ** levels(key_list[1], (RAY_TOTAL, SAMPLES), ((0, 256),), -0.2, 0.2)), 0.02, 0.3),
        "targets": jnp.clip(1.0 * jax.random.uniform(key_list[2], (3, RAY_TOTAL), jnp.float32) ** levels(key_list[2], (3, RAY_TOTAL), ((1, 256),), -0.2, 0.2), 0.0, 1.0),
        "ray_length": draw_ray_length(jax.random.fold_in(key_list[13], 71), 0),
        "cell_id": draw_cell_id(jax.random.fold_in(key_list[13], 71), 0),
        "slot_rank": draw_slot_rank(jax.random.fold_in(key_list[13], 71), 0),
        "image_id": draw_image_id(jax.random.fold_in(key_list[13], 71), 0),
        "params": draw_params(jax.random.fold_in(key_list[13], 71), 0),
        "first_moment": normal_values(key_list[8], (EXPERTS, PARAM_ROWS, NET_WIDTH), 0.05, 0.75, ((0, 64),), jnp.float32),
        "second_moment": jnp.clip(jnp.exp(math.log(0.01) - 9.2103404 * jax.random.uniform(key_list[9], (EXPERTS, PARAM_ROWS, NET_WIDTH), jnp.float32) ** levels(key_list[9], (EXPERTS, PARAM_ROWS, NET_WIDTH), ((0, 64),), -0.2, 0.2)), 9.999999974752427e-07, 0.01),
        "code_table": normal_values(key_list[10], (IMAGES, CODE_WIDTH), 0.5, 6.0, ((0, 256),), jnp.float32),
        "table_first": normal_values(key_list[11], (IMAGES, CODE_WIDTH), 0.05, 0.75, ((0, 256),), jnp.float32),
        "table_second": jnp.clip(jnp.exp(math.log(0.01) - 9.2103404 * jax.random.uniform(key_list[12], (IMAGES, CODE_WIDTH), jnp.float32) ** levels(key_list[12], (IMAGES, CODE_WIDTH), ((0, 256),), -0.2, 0.2)), 9.999999974752427e-07, 0.01),
    }


BETA_ONE = 0.9
BETA_TWO = 0.999
LEARN_RATE = 0.001
ADAM_EPS = 1e-08
CORRECT_ONE = 1.0 - 0.9 ** 10
CORRECT_TWO = 1.0 - 0.999 ** 10

def adam_update(param_now, gradient, moment_one, moment_two):
    new_one = BETA_ONE * moment_one + (1.0 - BETA_ONE) * gradient
    new_two = BETA_TWO * moment_two + (1.0 - BETA_TWO) * gradient * gradient
    update = LEARN_RATE * (new_one / CORRECT_ONE) / (jnp.sqrt(new_two / CORRECT_TWO) + ADAM_EPS)
    return (param_now - update, new_one, new_two)

def composite(raw_out, spacing, live_mask, targets):
    density = jax.nn.softplus(raw_out[0])
    colors = jax.nn.sigmoid(raw_out[1:4])
    optical = density * spacing * live_mask
    before = jnp.cumsum(optical, axis=1) - optical
    weight = jnp.exp(-before) * (1.0 - jnp.exp(-optical))
    render = lax.optimization_barrier(jnp.sum(weight[None] * colors, axis=2))
    return 0.5 * lax.optimization_barrier(jnp.sum((render - targets) ** 2, axis=0))

def contract_first(left, right):
    return lax.dot_general(left.astype(jnp.float32), right.astype(jnp.float32), (((0,), (0,)), ((), ())))

def contract_last(left, right):
    return lax.dot_general(left.astype(jnp.float32), right.astype(jnp.float32), (((1,), (1,)), ((), ())))

def expert_forward(weights, inputs, code_rows):
    head_row = ENC_WIDTH + (LAYERS - 1) * NET_WIDTH
    activations = [inputs]
    preacts = []
    current = inputs
    row_start = 0
    row_count = ENC_WIDTH
    for layer_index in range(LAYERS):
        matrix = weights[row_start:row_start + row_count]
        preact = jnp.dot(current.astype(jnp.float32), matrix.astype(jnp.float32)) + weights[head_row + 9 + layer_index].astype(jnp.float32)
        current = jnp.maximum(preact, 0.0).astype(jnp.bfloat16)
        preacts.append(preact)
        activations.append(current)
        row_start = row_start + row_count
        row_count = NET_WIDTH
    hidden_part = contract_last(current, weights[head_row:head_row + 4])
    code_part = contract_last(code_rows, weights[head_row + 4:head_row + 8, :CODE_WIDTH])
    raw_out = hidden_part + code_part + weights[head_row + 8, :4].astype(jnp.float32)
    return (activations, preacts, raw_out)

def expert_backward(weights, activations, preacts, code_rows, cotangent):
    head_row = ENC_WIDTH + (LAYERS - 1) * NET_WIDTH
    hidden_head = contract_first(cotangent, activations[-1])
    code_head = contract_first(cotangent, code_rows)
    bias_head = lax.optimization_barrier(jnp.sum(cotangent.astype(jnp.float32), axis=0))
    code_grad = jnp.dot(cotangent.astype(jnp.float32), weights[head_row + 4:head_row + 8, :CODE_WIDTH].astype(jnp.float32))
    upstream = jnp.dot(cotangent.astype(jnp.float32), weights[head_row:head_row + 4].astype(jnp.float32))
    weight_grads = [None] * LAYERS
    bias_grads = [None] * LAYERS
    for layer_index in reversed(range(LAYERS)):
        pre_grad = jnp.where(preacts[layer_index] > 0, upstream, 0.0).astype(jnp.bfloat16)
        weight_grads[layer_index] = contract_first(activations[layer_index], pre_grad)
        bias_grads[layer_index] = lax.optimization_barrier(jnp.sum(pre_grad.astype(jnp.float32), axis=0))
        if layer_index > 0:
            row_start = ENC_WIDTH + (layer_index - 1) * NET_WIDTH
            upstream = contract_last(pre_grad, weights[row_start:row_start + NET_WIDTH])
    pieces = list(weight_grads) + [hidden_head, jnp.pad(code_head, ((0, 0), (0, NET_WIDTH - CODE_WIDTH))), jnp.pad(bias_head, (0, NET_WIDTH - 4))[None, :], jnp.stack(bias_grads, axis=0), jnp.zeros((7 - LAYERS, NET_WIDTH), jnp.float32)]
    return (jnp.concatenate(pieces, axis=0), code_grad)

def reference(features, spacing, targets, ray_length, cell_id, slot_rank, image_id, params, first_moment, second_moment, code_table, table_first, table_second):
    ray_total = features.shape[0]
    sample_count = ray_total * SAMPLES
    blocks = ray_total // RAY_DEV
    column_count = blocks * CAPACITY
    positions = features.reshape(sample_count, ENC_WIDTH)
    ray_code = code_table.astype(jnp.bfloat16)[image_id]
    sample_code = jnp.broadcast_to(ray_code[:, None, :], (ray_total, SAMPLES, CODE_WIDTH)).reshape(sample_count, CODE_WIDTH)
    flat_rank = slot_rank.reshape(sample_count)
    flat_cell = cell_id.reshape(sample_count)
    sample_numbers = jnp.arange(sample_count, dtype=jnp.int32)
    block_number = sample_numbers // (RAY_DEV * SAMPLES)
    column = jnp.where(flat_rank >= 0, block_number * CAPACITY + flat_rank, column_count).astype(jnp.int32)
    owner_ids = jnp.full((EXPERTS, column_count), -1, jnp.int32).at[flat_cell, column].set(sample_numbers, mode='drop')
    weights_bf = params.astype(jnp.bfloat16)

    def gather_rows(sample_ids):
        occupied = sample_ids >= 0
        safe_ids = jnp.maximum(sample_ids, 0)
        inputs = jnp.where(occupied[:, None], positions[safe_ids], jnp.zeros((), jnp.bfloat16))
        code_rows = jnp.where(occupied[:, None], sample_code[safe_ids], jnp.zeros((), jnp.bfloat16))
        return (occupied, safe_ids, inputs, code_rows)

    def forward_one(operands):
        weights, sample_ids = operands
        occupied, safe_ids, inputs, code_rows = gather_rows(sample_ids)
        return expert_forward(weights, inputs, code_rows)[2]
    raw_table = lax.map(forward_one, (weights_bf, owner_ids))
    live_flat = flat_rank >= 0
    raw_samples = raw_table[flat_cell, jnp.minimum(column, column_count - 1)]
    raw_samples = jnp.where(live_flat[:, None], raw_samples, 0.0)
    position = jnp.arange(SAMPLES, dtype=jnp.int32)
    live_mask = (position[None, :] < ray_length[:, None]).astype(jnp.float32)
    raw_grid = raw_samples.T.reshape(4, ray_total, SAMPLES)

    def loss_of(raw_in):
        return composite(raw_in, spacing, live_mask, targets)
    ray_loss, pullback = jax.vjp(loss_of, raw_grid)
    raw_grad, = pullback(jnp.ones_like(ray_loss))
    cotangent = raw_grad.reshape(4, sample_count).T.astype(jnp.bfloat16)

    def backward_one(code_sum, operands):
        weights, sample_ids = operands
        occupied, safe_ids, inputs, code_rows = gather_rows(sample_ids)
        upstream_rows = jnp.where(occupied[:, None], cotangent[safe_ids], jnp.zeros((), jnp.bfloat16))
        activations, preacts, raw_out = expert_forward(weights, inputs, code_rows)
        gradient, code_grad = expert_backward(weights, activations, preacts, code_rows, upstream_rows)
        code_sum = code_sum.at[safe_ids // SAMPLES].add(jnp.where(occupied[:, None], code_grad, 0.0))
        return (code_sum, gradient)
    ray_code_grad, param_grad = lax.scan(backward_one, jnp.zeros((ray_total, CODE_WIDTH), jnp.float32), (weights_bf, owner_ids))
    table_grad = jax.ops.segment_sum(ray_code_grad, image_id, num_segments=IMAGES)
    new_params, new_first, new_second = adam_update(params, param_grad, first_moment, second_moment)
    new_table, new_table_first, new_table_second = adam_update(code_table, table_grad, table_first, table_second)
    return (ray_loss, new_params, new_first, new_second, new_table, new_table_first, new_table_second)
```

```python
import jax
import jax.numpy as jnp
from jax import lax
from jax.experimental import pallas as pl
from jax.experimental.pallas import tpu as pltpu
from jax.sharding import PartitionSpec as P

NET_WIDTH = 256
CODE_WIDTH = 64
ENC_WIDTH = 64
LAYERS = 4
SAMPLES = 32
RAYS = 128
IMAGES_DEV = 16
CAPACITY = 48
DEPTH = 16
THIRDS = CAPACITY // DEPTH
HEAD_ROW = ENC_WIDTH + (LAYERS - 1) * NET_WIDTH
PARAM_ROWS = HEAD_ROW + 16

F32 = jnp.float32
BF16 = jnp.bfloat16

BETA_ONE = 0.9
BETA_TWO = 0.999
LEARN_RATE = 0.001
ADAM_EPS = 1e-08
CORRECT_ONE = 1.0 - 0.9**10
CORRECT_TWO = 1.0 - 0.999**10

NN = (((1,), (0,)), ((), ()))
NT = (((1,), (1,)), ((), ()))
TN = (((0,), (0,)), ((), ()))


def mul(left, right, dims=NN):
    return lax.dot_general(left, right, dims, preferred_element_type=F32)


def iota(shape, dim):
    return lax.broadcasted_iota(jnp.int32, shape, dim)


def three_parts(value):
    high = value.astype(BF16)
    rest = value - high.astype(F32)
    middle = rest.astype(BF16)
    low = (rest - middle.astype(F32)).astype(BF16)
    return [high, middle, low]


def adam_update(param_now, gradient, moment_one, moment_two):
    new_one = BETA_ONE * moment_one + (1.0 - BETA_ONE) * gradient
    new_two = BETA_TWO * moment_two + (1.0 - BETA_TWO) * gradient * gradient
    update = LEARN_RATE * (new_one / CORRECT_ONE) / (jnp.sqrt(new_two / CORRECT_TWO) + ADAM_EPS)
    return (param_now - update, new_one, new_two)


def dispatch_kernel(feat_ref, cell_ref, rank_ref, out_ref, hot_ref, rows_ref):
    places = out_ref.shape[0]
    for i in range(SAMPLES):
        cell = cell_ref[i : i + 1, :]
        rank = rank_ref[i : i + 1, :]
        place = jnp.where(rank >= 0, (cell >> 1) * DEPTH + (rank & (DEPTH - 1)), -1)
        inner = (rank >> 4) * 2 + (cell & 1)
        span = pl.ds(i * RAYS, RAYS)
        hot_ref[:, span] = jnp.where(iota((places, RAYS), 0) == place, 1.0, 0.0).astype(BF16)
        feat = feat_ref[i].astype(F32)
        for q in range(THIRDS * 2):
            rows_ref[q * ENC_WIDTH : (q + 1) * ENC_WIDTH, span] = jnp.where(
                inner == q, feat, 0.0
            ).astype(BF16)
    out_ref[...] = mul(hot_ref[...], rows_ref[...], NT).astype(BF16)


def depth_match(rows):
    return (iota((rows, 128), 0) & (DEPTH - 1)) == (iota((rows, 128), 1) & (DEPTH - 1))


def first_matrix(weights_ref, held):
    matrix = weights_ref[held, 0:ENC_WIDTH, :]
    blank = jnp.zeros_like(matrix)
    return jnp.concatenate([matrix, blank] if held == 0 else [blank, matrix], axis=0)


def hidden_matrix(weights_ref, held, layer):
    start = ENC_WIDTH + (layer - 1) * NET_WIDTH
    return weights_ref[held, start : start + NET_WIDTH, :]


def head_tile(head, held):
    rows = jnp.concatenate(
        [jnp.broadcast_to(head[c : c + 1, :], (DEPTH, NET_WIDTH)) for c in range(4)], axis=0
    )
    blank = jnp.zeros_like(rows)
    return jnp.concatenate([rows, blank] if held == 0 else [blank, rows], axis=0).astype(BF16)


def forward_kernel(x_ref, params_ref, acts_ref, out_ref, weights_ref):
    third = pl.program_id(0)
    groups = out_ref.shape[0]
    rows = x_ref.shape[0]

    @pl.when(third == 0)
    def _():
        weights_ref[...] = params_ref[...].astype(BF16)

    heads = [weights_ref[h, HEAD_ROW:PARAM_ROWS, :].astype(F32) for h in range(2)]

    @pl.when(third == 0)
    def _():
        for j in range(4):
            h, c = j // 2, (j % 2) * 2
            pair = jnp.concatenate(
                [heads[h][4 + c : 5 + c, :CODE_WIDTH], heads[h][5 + c : 6 + c, :CODE_WIDTH]], axis=1
            )
            out_ref[:, 3 + j, :] = jnp.broadcast_to(pair, (groups, 128))
        out_ref[:, 7, :] = jnp.zeros((groups, 128), F32)

    lane = iota((1, 128), 1)
    shift = jnp.zeros((1, 128), F32)
    total = jnp.zeros((rows, 128), F32)
    for h in range(2):
        current = x_ref[...]
        for k in range(LAYERS):
            matrix = first_matrix(weights_ref, h) if k == 0 else hidden_matrix(weights_ref, h, k)
            preact = mul(current, matrix) + heads[h][9 + k : 10 + k, :]
            current = jnp.maximum(preact, 0.0).astype(BF16)
            acts_ref[0, h, k] = current
        total = total + mul(current, head_tile(heads[h], h), NT)
        for c in range(4):
            shift = shift + jnp.where((lane >> 4) == h * 4 + c, heads[h][8:9, c : c + 1], 0.0)
    total = jnp.where(depth_match(rows), total + shift, 0.0)
    raw = jnp.sum(total.reshape(groups, DEPTH, 128), axis=1)
    for j in range(THIRDS):

        @pl.when(third == j)
        def _():
            out_ref[:, j, :] = raw


def one_sample_row(cell_ref, rank_ref, image, i, owners):
    cell = cell_ref[pl.ds(i, 1), :]
    rank = rank_ref[pl.ds(i, 1), :]
    live = rank >= 0
    owner = jnp.where(live, cell >> 1, -1)
    hot = jnp.where(iota((owners, RAYS), 0) == owner, 1.0, 0.0).astype(BF16)
    held = cell & 1
    slot = jnp.where(live, ((rank >> 4) * 2 + held) * DEPTH + (rank & (DEPTH - 1)), -1)
    code = jnp.where(live, held * IMAGES_DEV + image, -1)
    slot_mask = iota((THIRDS * 2 * DEPTH, RAYS), 0) == slot
    code_mask = iota((2 * IMAGES_DEV, RAYS), 0) == code
    masks = [slot_mask[q * DEPTH : (q + 1) * DEPTH] for q in range(THIRDS * 2)]
    masks += [code_mask[h * IMAGES_DEV : (h + 1) * IMAGES_DEV] for h in range(2)]
    return hot, masks


def running_sum(value):
    step = 1
    while step < SAMPLES:
        value = value + jnp.concatenate(
            [jnp.zeros((step, RAYS), F32), value[: SAMPLES - step]], axis=0
        )
        step *= 2
    return value


def running_sum_back(value):
    step = 1
    while step < SAMPLES:
        value = value + jnp.concatenate([value[step:], jnp.zeros((step, RAYS), F32)], axis=0)
        step *= 2
    return value


def ray_kernel(
    back_ref,
    cell_ref,
    rank_ref,
    image_ref,
    length_ref,
    spacing_ref,
    targets_ref,
    code_ref,
    first_ref,
    second_ref,
    out_ref,
    loss_ref,
    new_code_ref,
    new_first_ref,
    new_second_ref,
    table_ref,
    raw_ref,
):
    owners = back_ref.shape[0]
    image = image_ref[...] & (IMAGES_DEV - 1)
    code = code_ref[...].astype(BF16).astype(F32)
    tile = jnp.concatenate([code] * 8, axis=0)
    tile = jnp.concatenate([tile, tile], axis=1)
    block_row = iota((128, 128), 0) >> 4
    block_lane = iota((128, 128), 1) >> 6
    code_blocks = [
        jnp.where(block_row == 2 * j + block_lane, tile, 0.0).astype(BF16) for j in range(4)
    ]
    queries = [back_ref[:, 3 + j, :].astype(BF16) for j in range(4)]
    code_part = mul(queries[0], code_blocks[0], NT)
    for j in range(1, 4):
        code_part = code_part + mul(queries[j], code_blocks[j], NT)
    pieces = [back_ref[:, j, :] for j in range(THIRDS)] + [code_part]
    table = jnp.concatenate([piece.T for piece in pieces], axis=0)
    table_ref[...] = jnp.concatenate(three_parts(table), axis=1)

    def pick(i, carry):
        hot, masks = one_sample_row(cell_ref, rank_ref, image, i, owners)
        found = mul(table_ref[...], jnp.concatenate([hot] * 3, axis=0))
        for c in range(4):
            total = jnp.zeros((DEPTH, RAYS), F32)
            for q in range(THIRDS * 2 + 2):
                start = q * 64 + c * DEPTH
                total = total + jnp.where(masks[q], found[start : start + DEPTH], 0.0)
            raw_ref[c, pl.ds(i, 1), :] = jnp.sum(total, axis=0, keepdims=True)
        return carry

    lax.fori_loop(0, SAMPLES, pick, 0, unroll=4)

    spacing = spacing_ref[...]
    live = jnp.where(iota((SAMPLES, RAYS), 0) < length_ref[...], 1.0, 0.0)
    raw_density = raw_ref[0]
    small = jnp.exp(-jnp.abs(raw_density))
    density = jnp.maximum(raw_density, 0.0) + jnp.log1p(small)
    slope = jnp.where(raw_density >= 0, 1.0, small) / (1.0 + small)
    colors = []
    for c in range(3):
        raw_color = raw_ref[1 + c]
        tail = jnp.exp(-jnp.abs(raw_color))
        colors.append(jnp.where(raw_color >= 0, 1.0, tail) / (1.0 + tail))
    reach = spacing * live
    tau = density * reach
    before = running_sum(tau) - tau
    passed = jnp.exp(-before)
    kept = jnp.exp(-tau)
    weight = passed * (1.0 - kept)
    gaps = []
    loss = jnp.zeros((1, RAYS), F32)
    for c in range(3):
        gap = jnp.sum(weight * colors[c], axis=0, keepdims=True) - targets_ref[c : c + 1, :]
        gaps.append(gap)
        loss = loss + gap * gap
    loss_ref[...] = 0.5 * loss
    pull = gaps[0] * colors[0] + gaps[1] * colors[1] + gaps[2] * colors[2]
    behind = weight * pull
    tau_grad = pull * passed * kept - (running_sum_back(behind) - behind)
    raw_ref[0] = (tau_grad * reach * slope).astype(BF16).astype(F32)
    for c in range(3):
        raw_ref[1 + c] = (
            (weight * gaps[c] * (colors[c] * (1.0 - colors[c]))).astype(BF16).astype(F32)
        )

    def put(i, total):
        hots, rows = [], []
        for half in range(2):
            hot, masks = one_sample_row(cell_ref, rank_ref, image, 2 * i + half, owners)
            cots = [raw_ref[c, pl.ds(2 * i + half, 1), :] for c in range(4)]
            hots.append(hot)
            rows.append(
                jnp.concatenate(
                    [
                        jnp.where(masks[q], cots[c], 0.0)
                        for q in range(THIRDS * 2 + 2)
                        for c in range(4)
                    ],
                    axis=0,
                ).astype(BF16)
            )
        return total + mul(
            jnp.concatenate(rows, axis=1), jnp.concatenate(hots, axis=1), NT
        )

    placed = lax.fori_loop(
        0, SAMPLES // 2, put, jnp.zeros((512, owners), F32), unroll=2
    )
    for j in range(THIRDS):
        out_ref[:, j, :] = placed[j * 128 : (j + 1) * 128].T
    image_sums = placed[384:512]
    sums_parts = three_parts(image_sums)
    sums_wide = jnp.concatenate(sums_parts, axis=1)
    sums_flip = jnp.concatenate(three_parts(image_sums.T), axis=1)
    table_grad = jnp.zeros((IMAGES_DEV, CODE_WIDTH), F32)
    for j in range(4):
        out_ref[:, 3 + j, :] = mul(sums_flip, jnp.concatenate([code_blocks[j]] * 3, axis=0))
        product = mul(sums_wide, jnp.concatenate([queries[j]] * 3, axis=0))
        low = 2 * j * IMAGES_DEV
        table_grad = table_grad + product[low : low + IMAGES_DEV, :CODE_WIDTH]
        table_grad = table_grad + product[low + IMAGES_DEV : low + 2 * IMAGES_DEV, CODE_WIDTH:]
    out_ref[:, 7, :] = jnp.zeros((owners, 128), F32)
    new_code, new_first, new_second = adam_update(
        code_ref[...], table_grad, first_ref[...], second_ref[...]
    )
    new_code_ref[...] = new_code
    new_first_ref[...] = new_first
    new_second_ref[...] = new_second


def backward_kernel(x_ref, acts_ref, cot_ref, params_ref, grad_ref, weights_ref, total_ref):
    third = pl.program_id(0)
    groups = cot_ref.shape[0]
    rows = x_ref.shape[0]

    @pl.when(third == 0)
    def _():
        weights_ref[...] = params_ref[...].astype(BF16)
        total_ref[...] = jnp.zeros_like(total_ref)
        for h in range(2):
            lines = []
            for c in range(4):
                sums = jnp.sum(cot_ref[:, 3 + h * 2 + c // 2, :], axis=0, keepdims=True)
                start = (c % 2) * CODE_WIDTH
                line = sums[:, start : start + CODE_WIDTH]
                lines.append(
                    jnp.concatenate([line, jnp.zeros((1, NET_WIDTH - CODE_WIDTH), F32)], axis=1)
                )
            total_ref[h, HEAD_ROW:PARAM_ROWS, :] = jnp.concatenate(
                [jnp.zeros((4, NET_WIDTH), F32)] + lines + [jnp.zeros((8, NET_WIDTH), F32)], axis=0
            )

    cot = jnp.where(
        third == 0, cot_ref[:, 0, :], jnp.where(third == 1, cot_ref[:, 1, :], cot_ref[:, 2, :])
    )
    sums = jnp.sum(cot, axis=0, keepdims=True)
    spread = jnp.broadcast_to(cot[:, None, :], (groups, DEPTH, 128)).reshape(rows, 128)
    spread = jnp.where(depth_match(rows), spread, 0.0).astype(BF16)
    lane = iota((1, 128), 1)
    wide_lane = iota((1, NET_WIDTH), 1)
    for h in range(2):
        head = weights_ref[h, HEAD_ROW:PARAM_ROWS, :].astype(F32)
        last = acts_ref[0, h, LAYERS - 1]
        outer = mul(spread, last, TN)[h * 64 : (h + 1) * 64]
        head_grad = jnp.sum(outer.reshape(4, DEPTH, NET_WIDTH), axis=1)
        bias_head = jnp.zeros((1, NET_WIDTH), F32)
        for c in range(4):
            value = jnp.sum(
                jnp.where((lane >> 4) == h * 4 + c, sums, 0.0), axis=1, keepdims=True
            )
            bias_head = bias_head + jnp.where(wide_lane == c, value, 0.0)
        up = mul(spread, head_tile(head, h))
        bias_lines = [None] * LAYERS
        for k in reversed(range(LAYERS)):
            pre_grad = jnp.where(acts_ref[0, h, k].astype(F32) > 0, up, 0.0).astype(BF16)
            bias_lines[k] = jnp.sum(pre_grad.astype(F32), axis=0, keepdims=True)
            if k > 0:
                start = ENC_WIDTH + (k - 1) * NET_WIDTH
                total_ref[h, start : start + NET_WIDTH, :] += mul(
                    acts_ref[0, h, k - 1], pre_grad, TN
                )
                up = mul(pre_grad, hidden_matrix(weights_ref, h, k), NT)
            else:
                total_ref[h, 0:ENC_WIDTH, :] += mul(x_ref[...], pre_grad, TN)[
                    h * ENC_WIDTH : (h + 1) * ENC_WIDTH
                ]
        total_ref[h, HEAD_ROW:PARAM_ROWS, :] += jnp.concatenate(
            [head_grad, jnp.zeros((4, NET_WIDTH), F32), bias_head]
            + bias_lines
            + [jnp.zeros((3, NET_WIDTH), F32)],
            axis=0,
        )

    @pl.when(third == THIRDS - 1)
    def _():
        grad_ref[...] = total_ref[...].astype(BF16)


def limits(mib=48):
    return pltpu.CompilerParams(vmem_limit_bytes=mib * 1024 * 1024)


def shape_of(dims, kind):
    return jax.ShapeDtypeStruct(dims, kind)


def shards(
    features,
    spacing,
    targets,
    ray_length,
    cell_id,
    slot_rank,
    image_id,
    params,
    first_moment,
    second_moment,
    code_table,
    table_first,
    table_second,
):
    groups = lax.axis_size("expert")
    copies = lax.axis_size("dp")
    places = groups * DEPTH
    cell_rows = cell_id.T
    rank_rows = slot_rank.T
    outgoing = pl.pallas_call(
        dispatch_kernel,
        out_shape=shape_of((places, THIRDS * 128), BF16),
        scratch_shapes=[
            pltpu.VMEM((places, SAMPLES * RAYS), BF16),
            pltpu.VMEM((THIRDS * 128, SAMPLES * RAYS), BF16),
        ],
        compiler_params=limits(),
        name="dispatch",
    )(jnp.transpose(features, (1, 2, 0)), cell_rows, rank_rows)
    arrived = lax.all_to_all(outgoing, "expert", split_axis=0, concat_axis=0, tiled=True)

    whole = lambda *dims: pl.BlockSpec(dims, lambda i: (0,) * len(dims))
    third_rows = pl.BlockSpec((places, 128), lambda i: (0, i))
    third_acts = pl.BlockSpec((1, 2, LAYERS, places, NET_WIDTH), lambda i: (i, 0, 0, 0, 0))
    acts, raw_out = pl.pallas_call(
        forward_kernel,
        grid=(THIRDS,),
        in_specs=[third_rows, whole(2, PARAM_ROWS, NET_WIDTH)],
        out_specs=[third_acts, whole(groups, 8, 128)],
        out_shape=[
            shape_of((THIRDS, 2, LAYERS, places, NET_WIDTH), BF16),
            shape_of((groups, 8, 128), F32),
        ],
        scratch_shapes=[pltpu.VMEM((2, PARAM_ROWS, NET_WIDTH), BF16)],
        compiler_params=limits(),
        name="forward",
    )(arrived, params)
    returned = lax.all_to_all(raw_out, "expert", split_axis=0, concat_axis=0, tiled=True)

    table_shape = shape_of(code_table.shape, F32)
    cot_out, loss, new_table, new_table_first, new_table_second = pl.pallas_call(
        ray_kernel,
        out_shape=[
            shape_of((groups, 8, 128), F32),
            shape_of((1, RAYS), F32),
            table_shape,
            table_shape,
            table_shape,
        ],
        scratch_shapes=[
            pltpu.VMEM((512, 3 * groups), BF16),
            pltpu.VMEM((4, SAMPLES, RAYS), F32),
        ],
        compiler_params=limits(),
        name="rays",
    )(
        returned,
        cell_rows,
        rank_rows,
        image_id.reshape(1, RAYS),
        ray_length.reshape(1, RAYS),
        spacing.T,
        targets,
        code_table,
        table_first,
        table_second,
    )
    cot_in = lax.all_to_all(cot_out, "expert", split_axis=0, concat_axis=0, tiled=True)

    local_grad = pl.pallas_call(
        backward_kernel,
        grid=(THIRDS,),
        in_specs=[
            third_rows,
            third_acts,
            whole(groups, 8, 128),
            whole(2, PARAM_ROWS, NET_WIDTH),
        ],
        out_specs=whole(2, PARAM_ROWS, NET_WIDTH),
        out_shape=shape_of((2, PARAM_ROWS, NET_WIDTH), BF16),
        scratch_shapes=[
            pltpu.VMEM((2, PARAM_ROWS, NET_WIDTH), BF16),
            pltpu.VMEM((2, PARAM_ROWS, NET_WIDTH), F32),
        ],
        compiler_params=limits(),
        name="backward",
    )(arrived, acts, cot_in, params)

    quarter = 2 * PARAM_ROWS // copies
    shares = lax.all_to_all(
        local_grad.reshape(copies, quarter, NET_WIDTH), "dp", split_axis=0, concat_axis=0, tiled=True
    )
    share = jnp.sum(shares.astype(F32), axis=0).astype(BF16)
    param_grad = (
        lax.all_gather(share, "dp", axis=0, tiled=False)
        .reshape(2, PARAM_ROWS, NET_WIDTH)
        .astype(F32)
    )
    new_params, new_first, new_second = adam_update(params, param_grad, first_moment, second_moment)
    return (
        loss.reshape(RAYS),
        new_params,
        new_first,
        new_second,
        new_table,
        new_table_first,
        new_table_second,
    )


def solution(mesh):
    rays = ("expert", "dp")
    table = P(rays, None)
    block = P("expert", None, None)
    return jax.shard_map(
        shards,
        mesh=mesh,
        in_specs=(
            P(rays, None, None),
            P(rays, None),
            P(None, rays),
            P(rays),
            P(rays, None),
            P(rays, None),
            P(rays),
            block,
            block,
            block,
            table,
            table,
            table,
        ),
        out_specs=(P(rays), block, block, block, table, table, table),
        check_vma=False,
    )
```

```python
import jax
import jax.numpy as jnp
from jax import lax
from jax.experimental import pallas as pl
from jax.experimental.pallas import tpu as pltpu
from jax.sharding import PartitionSpec as P

NET_WIDTH = 256
CODE_WIDTH = 64
ENC_WIDTH = 64
LAYERS = 4
SAMPLES = 32
RAYS = 128
IMAGES_DEV = 16
CAPACITY = 48
DEPTH = 16
THIRDS = CAPACITY // DEPTH
HEAD_ROW = ENC_WIDTH + (LAYERS - 1) * NET_WIDTH
PARAM_ROWS = HEAD_ROW + 16

F32 = jnp.float32
BF16 = jnp.bfloat16

BETA_ONE = 0.9
BETA_TWO = 0.999
LEARN_RATE = 0.001
ADAM_EPS = 1e-08
CORRECT_ONE = 1.0 - 0.9**10
CORRECT_TWO = 1.0 - 0.999**10

NN = (((1,), (0,)), ((), ()))
NT = (((1,), (1,)), ((), ()))
TN = (((0,), (0,)), ((), ()))


def mul(left, right, dims=NN):
    return lax.dot_general(left, right, dims, preferred_element_type=F32)


def iota(shape, dim):
    return lax.broadcasted_iota(jnp.int32, shape, dim)


def three_parts(value):
    high = value.astype(BF16)
    rest = value - high.astype(F32)
    middle = rest.astype(BF16)
    low = (rest - middle.astype(F32)).astype(BF16)
    return [high, middle, low]


def adam_update(param_now, gradient, moment_one, moment_two):
    new_one = BETA_ONE * moment_one + (1.0 - BETA_ONE) * gradient
    new_two = BETA_TWO * moment_two + (1.0 - BETA_TWO) * gradient * gradient
    update = LEARN_RATE * (new_one / CORRECT_ONE) / (jnp.sqrt(new_two / CORRECT_TWO) + ADAM_EPS)
    return (param_now - update, new_one, new_two)


def dispatch_kernel(feat_ref, cell_ref, rank_ref, out_ref, hot_ref, rows_ref):
    places = out_ref.shape[0]
    for i in range(SAMPLES):
        cell = cell_ref[i : i + 1, :]
        rank = rank_ref[i : i + 1, :]
        place = jnp.where(rank >= 0, (cell >> 1) * DEPTH + (rank & (DEPTH - 1)), -1)
        inner = (rank >> 4) * 2 + (cell & 1)
        span = pl.ds(i * RAYS, RAYS)
        hot_ref[:, span] = jnp.where(iota((places, RAYS), 0) == place, 1.0, 0.0).astype(BF16)
        feat = feat_ref[i].astype(F32)
        for q in range(THIRDS * 2):
            rows_ref[q * ENC_WIDTH : (q + 1) * ENC_WIDTH, span] = jnp.where(
                inner == q, feat, 0.0
            ).astype(BF16)
    out_ref[...] = mul(hot_ref[...], rows_ref[...], NT).astype(BF16)


def depth_match(rows):
    return (iota((rows, 128), 0) & (DEPTH - 1)) == (iota((rows, 128), 1) & (DEPTH - 1))


def first_matrix(weights_ref, held):
    matrix = weights_ref[held, 0:ENC_WIDTH, :]
    blank = jnp.zeros_like(matrix)
    return jnp.concatenate([matrix, blank] if held == 0 else [blank, matrix], axis=0)


def hidden_matrix(weights_ref, held, layer):
    start = ENC_WIDTH + (layer - 1) * NET_WIDTH
    return weights_ref[held, start : start + NET_WIDTH, :]


def head_tile(head, held):
    rows = jnp.concatenate(
        [jnp.broadcast_to(head[c : c + 1, :], (DEPTH, NET_WIDTH)) for c in range(4)], axis=0
    )
    blank = jnp.zeros_like(rows)
    return jnp.concatenate([rows, blank] if held == 0 else [blank, rows], axis=0).astype(BF16)


def forward_kernel(x_ref, params_ref, acts_ref, out_ref, weights_ref):
    third = pl.program_id(0)
    groups = out_ref.shape[0]
    rows = x_ref.shape[0]

    @pl.when(third == 0)
    def _():
        weights_ref[...] = params_ref[...].astype(BF16)

    heads = [weights_ref[h, HEAD_ROW:PARAM_ROWS, :].astype(F32) for h in range(2)]

    @pl.when(third == 0)
    def _():
        for j in range(4):
            h, c = j // 2, (j % 2) * 2
            pair = jnp.concatenate(
                [heads[h][4 + c : 5 + c, :CODE_WIDTH], heads[h][5 + c : 6 + c, :CODE_WIDTH]], axis=1
            )
            out_ref[:, 3 + j, :] = jnp.broadcast_to(pair, (groups, 128))
        out_ref[:, 7, :] = jnp.zeros((groups, 128), F32)

    lane = iota((1, 128), 1)
    shift = jnp.zeros((1, 128), F32)
    total = jnp.zeros((rows, 128), F32)
    for h in range(2):
        current = x_ref[...]
        for k in range(LAYERS):
            matrix = first_matrix(weights_ref, h) if k == 0 else hidden_matrix(weights_ref, h, k)
            preact = mul(current, matrix) + heads[h][9 + k : 10 + k, :]
            current = jnp.maximum(preact, 0.0).astype(BF16)
            acts_ref[0, h, k] = current
        total = total + mul(current, head_tile(heads[h], h), NT)
        for c in range(4):
            shift = shift + jnp.where((lane >> 4) == h * 4 + c, heads[h][8:9, c : c + 1], 0.0)
    total = jnp.where(depth_match(rows), total + shift, 0.0)
    raw = jnp.sum(total.reshape(groups, DEPTH, 128), axis=1)
    for j in range(THIRDS):

        @pl.when(third == j)
        def _():
            out_ref[:, j, :] = raw


def one_sample_row(cell_ref, rank_ref, image, i, owners):
    cell = cell_ref[pl.ds(i, 1), :]
    rank = rank_ref[pl.ds(i, 1), :]
    live = rank >= 0
    owner = jnp.where(live, cell >> 1, -1)
    hot = jnp.where(iota((owners, RAYS), 0) == owner, 1.0, 0.0).astype(BF16)
    held = cell & 1
    slot = jnp.where(live, ((rank >> 4) * 2 + held) * DEPTH + (rank & (DEPTH - 1)), -1)
    code = jnp.where(live, held * IMAGES_DEV + image, -1)
    slot_mask = iota((THIRDS * 2 * DEPTH, RAYS), 0) == slot
    code_mask = iota((2 * IMAGES_DEV, RAYS), 0) == code
    masks = [slot_mask[q * DEPTH : (q + 1) * DEPTH] for q in range(THIRDS * 2)]
    masks += [code_mask[h * IMAGES_DEV : (h + 1) * IMAGES_DEV] for h in range(2)]
    return hot, masks


def running_sum(value):
    step = 1
    while step < SAMPLES:
        value = value + jnp.concatenate(
            [jnp.zeros((step, RAYS), F32), value[: SAMPLES - step]], axis=0
        )
        step *= 2
    return value


def running_sum_back(value):
    step = 1
    while step < SAMPLES:
        value = value + jnp.concatenate([value[step:], jnp.zeros((step, RAYS), F32)], axis=0)
        step *= 2
    return value


def ray_kernel(
    back_ref,
    cell_ref,
    rank_ref,
    image_ref,
    length_ref,
    spacing_ref,
    targets_ref,
    code_ref,
    first_ref,
    second_ref,
    out_ref,
    loss_ref,
    new_code_ref,
    new_first_ref,
    new_second_ref,
    table_ref,
    raw_ref,
    lines_ref,
):
    owners = back_ref.shape[0]
    image = image_ref[...] & (IMAGES_DEV - 1)
    code = code_ref[...].astype(BF16).astype(F32)
    tile = jnp.concatenate([code] * 8, axis=0)
    tile = jnp.concatenate([tile, tile], axis=1)
    block_row = iota((128, 128), 0) >> 4
    block_lane = iota((128, 128), 1) >> 6
    code_blocks = [
        jnp.where(block_row == 2 * j + block_lane, tile, 0.0).astype(BF16) for j in range(4)
    ]
    queries = [back_ref[:, 3 + j, :].astype(BF16) for j in range(4)]
    code_part = mul(queries[0], code_blocks[0], NT)
    for j in range(1, 4):
        code_part = code_part + mul(queries[j], code_blocks[j], NT)
    pieces = [back_ref[:, j, :] for j in range(THIRDS)] + [code_part]
    table = jnp.concatenate([piece.T for piece in pieces], axis=0)
    table_ref[...] = jnp.concatenate(three_parts(table), axis=1)

    def pick(i, carry):
        hot, masks = one_sample_row(cell_ref, rank_ref, image, i, owners)
        found = mul(table_ref[...], jnp.concatenate([hot] * 3, axis=0))
        for c in range(4):
            total = jnp.zeros((DEPTH, RAYS), F32)
            for q in range(THIRDS * 2 + 2):
                start = q * 64 + c * DEPTH
                total = total + jnp.where(masks[q], found[start : start + DEPTH], 0.0)
            raw_ref[c, pl.ds(i, 1), :] = jnp.sum(total, axis=0, keepdims=True)
        return carry

    lax.fori_loop(0, SAMPLES, pick, 0, unroll=4)

    spacing = spacing_ref[...]
    live = jnp.where(iota((SAMPLES, RAYS), 0) < length_ref[...], 1.0, 0.0)
    raw_density = raw_ref[0]
    small = jnp.exp(-jnp.abs(raw_density))
    density = jnp.maximum(raw_density, 0.0) + jnp.log1p(small)
    slope = jnp.where(raw_density >= 0, 1.0, small) / (1.0 + small)
    colors = []
    for c in range(3):
        raw_color = raw_ref[1 + c]
        tail = jnp.exp(-jnp.abs(raw_color))
        colors.append(jnp.where(raw_color >= 0, 1.0, tail) / (1.0 + tail))
    reach = spacing * live
    tau = density * reach
    before = running_sum(tau) - tau
    passed = jnp.exp(-before)
    kept = jnp.exp(-tau)
    weight = passed * (1.0 - kept)
    gaps = []
    loss = jnp.zeros((1, RAYS), F32)
    for c in range(3):
        gap = jnp.sum(weight * colors[c], axis=0, keepdims=True) - targets_ref[c : c + 1, :]
        gaps.append(gap)
        loss = loss + gap * gap
    loss_ref[...] = 0.5 * loss
    pull = gaps[0] * colors[0] + gaps[1] * colors[1] + gaps[2] * colors[2]
    behind = weight * pull
    tau_grad = pull * passed * kept - (running_sum_back(behind) - behind)
    raw_ref[0] = (tau_grad * reach * slope).astype(BF16).astype(F32)
    for c in range(3):
        raw_ref[1 + c] = (
            (weight * gaps[c] * (colors[c] * (1.0 - colors[c]))).astype(BF16).astype(F32)
        )

    def put(i, total):
        hots, rows = [], []
        for half in range(2):
            hot, masks = one_sample_row(cell_ref, rank_ref, image, 2 * i + half, owners)
            cots = [raw_ref[c, pl.ds(2 * i + half, 1), :] for c in range(4)]
            hots.append(hot)
            rows.append(
                jnp.concatenate(
                    [
                        jnp.where(masks[q], cots[c], 0.0)
                        for q in range(THIRDS * 2 + 2)
                        for c in range(4)
                    ],
                    axis=0,
                ).astype(BF16)
            )
        return total + mul(
            jnp.concatenate(rows, axis=1), jnp.concatenate(hots, axis=1), NT
        )

    placed = lax.fori_loop(
        0, SAMPLES // 2, put, jnp.zeros((512, owners), F32), unroll=2
    )
    for j in range(THIRDS):
        lines_ref[:, j, :] = placed[j * 128 : (j + 1) * 128].T
    image_sums = placed[384:512]
    sums_parts = three_parts(image_sums)
    sums_wide = jnp.concatenate(sums_parts, axis=1)
    sums_flip = jnp.concatenate(three_parts(image_sums.T), axis=1)
    table_grad = jnp.zeros((IMAGES_DEV, CODE_WIDTH), F32)
    for j in range(4):
        lines_ref[:, 3 + j, :] = mul(sums_flip, jnp.concatenate([code_blocks[j]] * 3, axis=0))
        product = mul(sums_wide, jnp.concatenate([queries[j]] * 3, axis=0))
        low = 2 * j * IMAGES_DEV
        table_grad = table_grad + product[low : low + IMAGES_DEV, :CODE_WIDTH]
        table_grad = table_grad + product[low + IMAGES_DEV : low + 2 * IMAGES_DEV, CODE_WIDTH:]
    lines_ref[:, 7, :] = jnp.zeros((owners, 128), F32)
    out_ref[...] = lines_ref[...].astype(BF16)
    new_code, new_first, new_second = adam_update(
        code_ref[...], table_grad, first_ref[...], second_ref[...]
    )
    new_code_ref[...] = new_code
    new_first_ref[...] = new_first
    new_second_ref[...] = new_second


def backward_kernel(
    order_ref,
    x_ref,
    acts_ref,
    cot_in_ref,
    params_ref,
    own_ref,
    first_ref,
    second_ref,
    third_ref,
    weights_ref,
    total_ref,
    cot_ref,
):
    third = pl.program_id(0)
    groups = cot_ref.shape[0]
    rows = x_ref.shape[0]

    @pl.when(third == 0)
    def _():
        weights_ref[...] = params_ref[...].astype(BF16)
        cot_ref[...] = cot_in_ref[...].astype(F32)
        total_ref[...] = jnp.zeros_like(total_ref)
        for h in range(2):
            lines = []
            for c in range(4):
                sums = jnp.sum(cot_ref[:, 3 + h * 2 + c // 2, :], axis=0, keepdims=True)
                start = (c % 2) * CODE_WIDTH
                line = sums[:, start : start + CODE_WIDTH]
                lines.append(
                    jnp.concatenate([line, jnp.zeros((1, NET_WIDTH - CODE_WIDTH), F32)], axis=1)
                )
            total_ref[h * PARAM_ROWS + HEAD_ROW : (h + 1) * PARAM_ROWS, :] = jnp.concatenate(
                [jnp.zeros((4, NET_WIDTH), F32)] + lines + [jnp.zeros((8, NET_WIDTH), F32)], axis=0
            )

    cot = jnp.where(
        third == 0, cot_ref[:, 0, :], jnp.where(third == 1, cot_ref[:, 1, :], cot_ref[:, 2, :])
    )
    sums = jnp.sum(cot, axis=0, keepdims=True)
    spread = jnp.broadcast_to(cot[:, None, :], (groups, DEPTH, 128)).reshape(rows, 128)
    spread = jnp.where(depth_match(rows), spread, 0.0).astype(BF16)
    lane = iota((1, 128), 1)
    wide_lane = iota((1, NET_WIDTH), 1)
    for h in range(2):
        head = weights_ref[h, HEAD_ROW:PARAM_ROWS, :].astype(F32)
        last = acts_ref[0, h, LAYERS - 1]
        outer = mul(spread, last, TN)[h * 64 : (h + 1) * 64]
        head_grad = jnp.sum(outer.reshape(4, DEPTH, NET_WIDTH), axis=1)
        bias_head = jnp.zeros((1, NET_WIDTH), F32)
        for c in range(4):
            value = jnp.sum(
                jnp.where((lane >> 4) == h * 4 + c, sums, 0.0), axis=1, keepdims=True
            )
            bias_head = bias_head + jnp.where(wide_lane == c, value, 0.0)
        up = mul(spread, head_tile(head, h))
        bias_lines = [None] * LAYERS
        for k in reversed(range(LAYERS)):
            pre_grad = jnp.where(acts_ref[0, h, k].astype(F32) > 0, up, 0.0).astype(BF16)
            bias_lines[k] = jnp.sum(pre_grad.astype(F32), axis=0, keepdims=True)
            if k > 0:
                start = h * PARAM_ROWS + ENC_WIDTH + (k - 1) * NET_WIDTH
                total_ref[start : start + NET_WIDTH, :] += mul(
                    acts_ref[0, h, k - 1], pre_grad, TN
                )
                up = mul(pre_grad, hidden_matrix(weights_ref, h, k), NT)
            else:
                start = h * PARAM_ROWS
                total_ref[start : start + ENC_WIDTH, :] += mul(x_ref[...], pre_grad, TN)[
                    h * ENC_WIDTH : (h + 1) * ENC_WIDTH
                ]
        total_ref[h * PARAM_ROWS + HEAD_ROW : (h + 1) * PARAM_ROWS, :] += jnp.concatenate(
            [head_grad, jnp.zeros((4, NET_WIDTH), F32), bias_head]
            + bias_lines
            + [jnp.zeros((3, NET_WIDTH), F32)],
            axis=0,
        )

    @pl.when(third == THIRDS - 1)
    def _():
        quarter = own_ref.shape[0]
        for k, share_ref in enumerate((own_ref, first_ref, second_ref, third_ref)):
            start = pl.multiple_of(order_ref[k] * quarter, 8)
            share_ref[...] = total_ref[pl.ds(start, quarter), :].astype(share_ref.dtype)


def adam_kernel(
    order_ref, own_ref, first_ref, second_ref, third_ref, *refs
):
    step = pl.program_id(0)
    param_ref, one_ref, two_ref, new_param_ref, new_one_ref, new_two_ref = refs
    for k, share_ref in enumerate((own_ref, first_ref, second_ref, third_ref)):

        @pl.when(step == k)
        def _():
            new_param, new_one, new_two = adam_update(
                param_ref[...], share_ref[...].astype(F32), one_ref[...], two_ref[...]
            )
            new_param_ref[...] = new_param
            new_one_ref[...] = new_one
            new_two_ref[...] = new_two


def limits(mib=48):
    return pltpu.CompilerParams(vmem_limit_bytes=mib * 1024 * 1024)


def shape_of(dims, kind):
    return jax.ShapeDtypeStruct(dims, kind)


def shards(
    features,
    spacing,
    targets,
    ray_length,
    cell_id,
    slot_rank,
    image_id,
    params,
    first_moment,
    second_moment,
    code_table,
    table_first,
    table_second,
):
    groups = lax.axis_size("expert")
    places = groups * DEPTH
    cell_rows = cell_id.T
    rank_rows = slot_rank.T
    outgoing = pl.pallas_call(
        dispatch_kernel,
        out_shape=shape_of((places, THIRDS * 128), BF16),
        scratch_shapes=[
            pltpu.VMEM((places, SAMPLES * RAYS), BF16),
            pltpu.VMEM((THIRDS * 128, SAMPLES * RAYS), BF16),
        ],
        compiler_params=limits(),
        name="dispatch",
    )(jnp.transpose(features, (1, 2, 0)), cell_rows, rank_rows)
    arrived = lax.all_to_all(outgoing, "expert", split_axis=0, concat_axis=0, tiled=True)

    whole = lambda *dims: pl.BlockSpec(dims, lambda i: (0,) * len(dims))
    third_rows = pl.BlockSpec((places, 128), lambda i: (0, i))
    third_acts = pl.BlockSpec((1, 2, LAYERS, places, NET_WIDTH), lambda i: (i, 0, 0, 0, 0))
    acts, raw_out = pl.pallas_call(
        forward_kernel,
        grid=(THIRDS,),
        in_specs=[third_rows, whole(2, PARAM_ROWS, NET_WIDTH)],
        out_specs=[third_acts, whole(groups, 8, 128)],
        out_shape=[
            shape_of((THIRDS, 2, LAYERS, places, NET_WIDTH), BF16),
            shape_of((groups, 8, 128), F32),
        ],
        scratch_shapes=[pltpu.VMEM((2, PARAM_ROWS, NET_WIDTH), BF16)],
        compiler_params=limits(),
        name="forward",
    )(arrived, params)
    returned = lax.all_to_all(raw_out, "expert", split_axis=0, concat_axis=0, tiled=True)

    table_shape = shape_of(code_table.shape, F32)
    cot_out, loss, new_table, new_table_first, new_table_second = pl.pallas_call(
        ray_kernel,
        out_shape=[
            shape_of((groups, 8, 128), BF16),
            shape_of((1, RAYS), F32),
            table_shape,
            table_shape,
            table_shape,
        ],
        scratch_shapes=[
            pltpu.VMEM((512, 3 * groups), BF16),
            pltpu.VMEM((4, SAMPLES, RAYS), F32),
            pltpu.VMEM((groups, 8, 128), F32),
        ],
        compiler_params=limits(),
        name="rays",
    )(
        returned,
        cell_rows,
        rank_rows,
        image_id.reshape(1, RAYS),
        ray_length.reshape(1, RAYS),
        spacing.T,
        targets,
        code_table,
        table_first,
        table_second,
    )
    cot_in = lax.all_to_all(cot_out, "expert", split_axis=0, concat_axis=0, tiled=True)

    copies = lax.axis_size("dp")
    quarter = 2 * PARAM_ROWS // copies
    turns = jnp.arange(copies, dtype=jnp.int32)
    position = lax.axis_index("dp")
    lent = lambda *dims: pl.BlockSpec(dims, lambda i, order: (0,) * len(dims))
    shares = pl.pallas_call(
        backward_kernel,
        grid_spec=pltpu.PrefetchScalarGridSpec(
            num_scalar_prefetch=1,
            grid=(THIRDS,),
            in_specs=[
                pl.BlockSpec((places, 128), lambda i, order: (0, i)),
                pl.BlockSpec(
                    (1, 2, LAYERS, places, NET_WIDTH), lambda i, order: (i, 0, 0, 0, 0)
                ),
                lent(groups, 8, 128),
                lent(2, PARAM_ROWS, NET_WIDTH),
            ],
            out_specs=[lent(quarter, NET_WIDTH)] * 4,
            scratch_shapes=[
                pltpu.VMEM((2, PARAM_ROWS, NET_WIDTH), BF16),
                pltpu.VMEM((2 * PARAM_ROWS, NET_WIDTH), F32),
                pltpu.VMEM((groups, 8, 128), F32),
            ],
        ),
        out_shape=[shape_of((quarter, NET_WIDTH), F32)]
        + [shape_of((quarter, NET_WIDTH), BF16)] * 3,
        compiler_params=limits(),
        name="backward",
    )((position + turns) % copies, arrived, acts, cot_in, params)

    def send(value, distance):
        return lax.ppermute(value, "dp", [(i, (i + distance) % copies) for i in range(copies)])

    share = shares[0]
    for k in (2, 1, 3):
        share = share + send(shares[k], k).astype(F32)
    share = share.astype(BF16)
    others = [None, None, None]
    for k in (2, 1, 3):
        others[k - 1] = send(share, k)
    flat = (2 * PARAM_ROWS, NET_WIDTH)
    by_order = pl.BlockSpec((quarter, NET_WIDTH), lambda i, order: (order[i], 0))
    new_params, new_first, new_second = pl.pallas_call(
        adam_kernel,
        grid_spec=pltpu.PrefetchScalarGridSpec(
            num_scalar_prefetch=1,
            grid=(copies,),
            in_specs=[lent(quarter, NET_WIDTH)] * 4 + [by_order] * 3,
            out_specs=[by_order] * 3,
        ),
        out_shape=[shape_of(flat, F32)] * 3,
        compiler_params=limits(),
        name="adam",
    )(
        (position - turns) % copies,
        share,
        *others,
        params.reshape(flat),
        first_moment.reshape(flat),
        second_moment.reshape(flat),
    )
    new_params, new_first, new_second = (
        value.reshape(params.shape) for value in (new_params, new_first, new_second)
    )
    return (
        loss.reshape(RAYS),
        new_params,
        new_first,
        new_second,
        new_table,
        new_table_first,
        new_table_second,
    )


def solution(mesh):
    rays = ("expert", "dp")
    table = P(rays, None)
    block = P("expert", None, None)
    return jax.shard_map(
        shards,
        mesh=mesh,
        in_specs=(
            P(rays, None, None),
            P(rays, None),
            P(None, rays),
            P(rays),
            P(rays, None),
            P(rays, None),
            P(rays),
            block,
            block,
            block,
            table,
            table,
            table,
        ),
        out_specs=(P(rays), block, block, block, table, table, table),
        check_vma=False,
    )
```

```python
import functools

import jax
import jax.numpy as jnp
from jax import lax
from jax.experimental import pallas as pl
from jax.experimental.pallas import tpu as pltpu
from jax.sharding import PartitionSpec as P

NET_WIDTH = 256
CODE_WIDTH = 64
ENC_WIDTH = 64
LAYERS = 4
SAMPLES = 32
RAYS = 128
IMAGES_DEV = 16
CAPACITY = 48
DEPTH = 16
THIRDS = CAPACITY // DEPTH
HEAD_ROW = ENC_WIDTH + (LAYERS - 1) * NET_WIDTH
PARAM_ROWS = HEAD_ROW + 16

F32 = jnp.float32
BF16 = jnp.bfloat16

BETA_ONE = 0.9
BETA_TWO = 0.999
LEARN_RATE = 0.001
ADAM_EPS = 1e-08
CORRECT_ONE = 1.0 - 0.9**10
CORRECT_TWO = 1.0 - 0.999**10

NN = (((1,), (0,)), ((), ()))
NT = (((1,), (1,)), ((), ()))
TN = (((0,), (0,)), ((), ()))


def mul(left, right, dims=NN):
    return lax.dot_general(left, right, dims, preferred_element_type=F32)


def iota(shape, dim):
    return lax.broadcasted_iota(jnp.int32, shape, dim)


def three_parts(value):
    high = value.astype(BF16)
    rest = value - high.astype(F32)
    middle = rest.astype(BF16)
    low = (rest - middle.astype(F32)).astype(BF16)
    return [high, middle, low]


def adam_update(param_now, gradient, moment_one, moment_two):
    new_one = BETA_ONE * moment_one + (1.0 - BETA_ONE) * gradient
    new_two = BETA_TWO * moment_two + (1.0 - BETA_TWO) * gradient * gradient
    update = LEARN_RATE * (new_one / CORRECT_ONE) / (jnp.sqrt(new_two / CORRECT_TWO) + ADAM_EPS)
    return (param_now - update, new_one, new_two)


def dispatch_kernel(feat_ref, cell_ref, rank_ref, out_ref, hot_ref, rows_ref):
    places = out_ref.shape[0]
    for i in range(SAMPLES):
        cell = cell_ref[i : i + 1, :]
        rank = rank_ref[i : i + 1, :]
        place = jnp.where(rank >= 0, (cell >> 1) * DEPTH + (rank & (DEPTH - 1)), -1)
        inner = (rank >> 4) * 2 + (cell & 1)
        span = pl.ds(i * RAYS, RAYS)
        hot_ref[:, span] = jnp.where(iota((places, RAYS), 0) == place, 1.0, 0.0).astype(BF16)
        feat = feat_ref[i].astype(F32)
        for q in range(THIRDS * 2):
            rows_ref[q * ENC_WIDTH : (q + 1) * ENC_WIDTH, span] = jnp.where(
                inner == q, feat, 0.0
            ).astype(BF16)
    out_ref[...] = mul(hot_ref[...], rows_ref[...], NT).astype(BF16)


def depth_match(rows):
    return (iota((rows, 128), 0) & (DEPTH - 1)) == (iota((rows, 128), 1) & (DEPTH - 1))


def first_matrix(weights_ref, held):
    matrix = weights_ref[held, 0:ENC_WIDTH, :]
    blank = jnp.zeros_like(matrix)
    return jnp.concatenate([matrix, blank] if held == 0 else [blank, matrix], axis=0)


def hidden_matrix(weights_ref, held, layer):
    start = ENC_WIDTH + (layer - 1) * NET_WIDTH
    return weights_ref[held, start : start + NET_WIDTH, :]


def head_tile(head, held):
    rows = jnp.concatenate(
        [jnp.broadcast_to(head[c : c + 1, :], (DEPTH, NET_WIDTH)) for c in range(4)], axis=0
    )
    blank = jnp.zeros_like(rows)
    return jnp.concatenate([rows, blank] if held == 0 else [blank, rows], axis=0).astype(BF16)


def forward_kernel(x_ref, params_ref, acts_ref, out_ref, weights_ref):
    third = pl.program_id(0)
    groups = out_ref.shape[0]
    rows = x_ref.shape[0]

    @pl.when(third == 0)
    def _():
        weights_ref[...] = params_ref[...].astype(BF16)

    heads = [weights_ref[h, HEAD_ROW:PARAM_ROWS, :].astype(F32) for h in range(2)]

    @pl.when(third == 0)
    def _():
        for j in range(4):
            h, c = j // 2, (j % 2) * 2
            pair = jnp.concatenate(
                [heads[h][4 + c : 5 + c, :CODE_WIDTH], heads[h][5 + c : 6 + c, :CODE_WIDTH]], axis=1
            )
            out_ref[:, 3 + j, :] = jnp.broadcast_to(pair, (groups, 128))
        out_ref[:, 7, :] = jnp.zeros((groups, 128), F32)

    lane = iota((1, 128), 1)
    shift = jnp.zeros((1, 128), F32)
    total = jnp.zeros((rows, 128), F32)
    for h in range(2):
        current = x_ref[...]
        for k in range(LAYERS):
            matrix = first_matrix(weights_ref, h) if k == 0 else hidden_matrix(weights_ref, h, k)
            preact = mul(current, matrix) + heads[h][9 + k : 10 + k, :]
            current = jnp.maximum(preact, 0.0).astype(BF16)
            acts_ref[0, h, k] = current
        total = total + mul(current, head_tile(heads[h], h), NT)
        for c in range(4):
            shift = shift + jnp.where((lane >> 4) == h * 4 + c, heads[h][8:9, c : c + 1], 0.0)
    total = jnp.where(depth_match(rows), total + shift, 0.0)
    raw = jnp.sum(total.reshape(groups, DEPTH, 128), axis=1)
    for j in range(THIRDS):

        @pl.when(third == j)
        def _():
            out_ref[:, j, :] = raw


def one_sample_row(cell_ref, rank_ref, image, i, owners):
    cell = cell_ref[pl.ds(i, 1), :]
    rank = rank_ref[pl.ds(i, 1), :]
    live = rank >= 0
    owner = jnp.where(live, cell >> 1, -1)
    hot = jnp.where(iota((owners, RAYS), 0) == owner, 1.0, 0.0).astype(BF16)
    held = cell & 1
    slot = jnp.where(live, ((rank >> 4) * 2 + held) * DEPTH + (rank & (DEPTH - 1)), -1)
    code = jnp.where(live, held * IMAGES_DEV + image, -1)
    slot_mask = iota((THIRDS * 2 * DEPTH, RAYS), 0) == slot
    code_mask = iota((2 * IMAGES_DEV, RAYS), 0) == code
    masks = [slot_mask[q * DEPTH : (q + 1) * DEPTH] for q in range(THIRDS * 2)]
    masks += [code_mask[h * IMAGES_DEV : (h + 1) * IMAGES_DEV] for h in range(2)]
    return hot, masks


def running_sum(value):
    step = 1
    while step < SAMPLES:
        value = value + jnp.concatenate(
            [jnp.zeros((step, RAYS), F32), value[: SAMPLES - step]], axis=0
        )
        step *= 2
    return value


def running_sum_back(value):
    step = 1
    while step < SAMPLES:
        value = value + jnp.concatenate([value[step:], jnp.zeros((step, RAYS), F32)], axis=0)
        step *= 2
    return value


def ray_kernel(
    back_ref,
    cell_ref,
    rank_ref,
    image_ref,
    length_ref,
    spacing_ref,
    targets_ref,
    code_ref,
    first_ref,
    second_ref,
    out_ref,
    loss_ref,
    new_code_ref,
    new_first_ref,
    new_second_ref,
    table_ref,
    raw_ref,
    lines_ref,
):
    owners = back_ref.shape[0]
    image = image_ref[...] & (IMAGES_DEV - 1)
    code = code_ref[...].astype(BF16).astype(F32)
    tile = jnp.concatenate([code] * 8, axis=0)
    tile = jnp.concatenate([tile, tile], axis=1)
    block_row = iota((128, 128), 0) >> 4
    block_lane = iota((128, 128), 1) >> 6
    code_blocks = [
        jnp.where(block_row == 2 * j + block_lane, tile, 0.0).astype(BF16) for j in range(4)
    ]
    queries = [back_ref[:, 3 + j, :].astype(BF16) for j in range(4)]
    code_part = mul(queries[0], code_blocks[0], NT)
    for j in range(1, 4):
        code_part = code_part + mul(queries[j], code_blocks[j], NT)
    pieces = [back_ref[:, j, :] for j in range(THIRDS)] + [code_part]
    table = jnp.concatenate([piece.T for piece in pieces], axis=0)
    table_ref[...] = jnp.concatenate(three_parts(table), axis=1)

    def pick(i, carry):
        hot, masks = one_sample_row(cell_ref, rank_ref, image, i, owners)
        found = mul(table_ref[...], jnp.concatenate([hot] * 3, axis=0))
        for c in range(4):
            total = jnp.zeros((DEPTH, RAYS), F32)
            for q in range(THIRDS * 2 + 2):
                start = q * 64 + c * DEPTH
                total = total + jnp.where(masks[q], found[start : start + DEPTH], 0.0)
            raw_ref[c, pl.ds(i, 1), :] = jnp.sum(total, axis=0, keepdims=True)
        return carry

    lax.fori_loop(0, SAMPLES, pick, 0, unroll=4)

    spacing = spacing_ref[...]
    live = jnp.where(iota((SAMPLES, RAYS), 0) < length_ref[...], 1.0, 0.0)
    raw_density = raw_ref[0]
    small = jnp.exp(-jnp.abs(raw_density))
    density = jnp.maximum(raw_density, 0.0) + jnp.log1p(small)
    slope = jnp.where(raw_density >= 0, 1.0, small) / (1.0 + small)
    colors = []
    for c in range(3):
        raw_color = raw_ref[1 + c]
        tail = jnp.exp(-jnp.abs(raw_color))
        colors.append(jnp.where(raw_color >= 0, 1.0, tail) / (1.0 + tail))
    reach = spacing * live
    tau = density * reach
    before = running_sum(tau) - tau
    passed = jnp.exp(-before)
    kept = jnp.exp(-tau)
    weight = passed * (1.0 - kept)
    gaps = []
    loss = jnp.zeros((1, RAYS), F32)
    for c in range(3):
        gap = jnp.sum(weight * colors[c], axis=0, keepdims=True) - targets_ref[c : c + 1, :]
        gaps.append(gap)
        loss = loss + gap * gap
    loss_ref[...] = 0.5 * loss
    pull = gaps[0] * colors[0] + gaps[1] * colors[1] + gaps[2] * colors[2]
    behind = weight * pull
    tau_grad = pull * passed * kept - (running_sum_back(behind) - behind)
    raw_ref[0] = (tau_grad * reach * slope).astype(BF16).astype(F32)
    for c in range(3):
        raw_ref[1 + c] = (
            (weight * gaps[c] * (colors[c] * (1.0 - colors[c]))).astype(BF16).astype(F32)
        )

    def put(i, total):
        hots, rows = [], []
        for half in range(2):
            hot, masks = one_sample_row(cell_ref, rank_ref, image, 2 * i + half, owners)
            cots = [raw_ref[c, pl.ds(2 * i + half, 1), :] for c in range(4)]
            hots.append(hot)
            rows.append(
                jnp.concatenate(
                    [
                        jnp.where(masks[q], cots[c], 0.0)
                        for q in range(THIRDS * 2 + 2)
                        for c in range(4)
                    ],
                    axis=0,
                ).astype(BF16)
            )
        return total + mul(
            jnp.concatenate(rows, axis=1), jnp.concatenate(hots, axis=1), NT
        )

    placed = lax.fori_loop(
        0, SAMPLES // 2, put, jnp.zeros((512, owners), F32), unroll=2
    )
    for j in range(THIRDS):
        lines_ref[:, j, :] = placed[j * 128 : (j + 1) * 128].T
    image_sums = placed[384:512]
    sums_parts = three_parts(image_sums)
    sums_wide = jnp.concatenate(sums_parts, axis=1)
    sums_flip = jnp.concatenate(three_parts(image_sums.T), axis=1)
    table_grad = jnp.zeros((IMAGES_DEV, CODE_WIDTH), F32)
    for j in range(4):
        lines_ref[:, 3 + j, :] = mul(sums_flip, jnp.concatenate([code_blocks[j]] * 3, axis=0))
        product = mul(sums_wide, jnp.concatenate([queries[j]] * 3, axis=0))
        low = 2 * j * IMAGES_DEV
        table_grad = table_grad + product[low : low + IMAGES_DEV, :CODE_WIDTH]
        table_grad = table_grad + product[low + IMAGES_DEV : low + 2 * IMAGES_DEV, CODE_WIDTH:]
    lines_ref[:, 7, :] = jnp.zeros((owners, 128), F32)
    out_ref[...] = lines_ref[...].astype(BF16)
    new_code, new_first, new_second = adam_update(
        code_ref[...], table_grad, first_ref[...], second_ref[...]
    )
    new_code_ref[...] = new_code
    new_first_ref[...] = new_first
    new_second_ref[...] = new_second


def backward_kernel(
    h,
    order_ref,
    x_ref,
    acts_ref,
    cot_in_ref,
    params_ref,
    own_ref,
    first_ref,
    second_ref,
    third_ref,
    weights_ref,
    total_ref,
    cot_ref,
):
    third = pl.program_id(0)
    groups = cot_ref.shape[0]
    rows = x_ref.shape[0]

    @pl.when(third == 0)
    def _():
        weights_ref[...] = params_ref[0].astype(BF16)
        cot_ref[...] = cot_in_ref[...].astype(F32)
        total_ref[...] = jnp.zeros_like(total_ref)
        lines = []
        for c in range(4):
            sums = jnp.sum(cot_ref[:, 3 + h * 2 + c // 2, :], axis=0, keepdims=True)
            start = (c % 2) * CODE_WIDTH
            line = sums[:, start : start + CODE_WIDTH]
            lines.append(
                jnp.concatenate([line, jnp.zeros((1, NET_WIDTH - CODE_WIDTH), F32)], axis=1)
            )
        total_ref[HEAD_ROW:PARAM_ROWS, :] = jnp.concatenate(
            [jnp.zeros((4, NET_WIDTH), F32)] + lines + [jnp.zeros((8, NET_WIDTH), F32)], axis=0
        )

    cot = jnp.where(
        third == 0, cot_ref[:, 0, :], jnp.where(third == 1, cot_ref[:, 1, :], cot_ref[:, 2, :])
    )
    sums = jnp.sum(cot, axis=0, keepdims=True)
    spread = jnp.broadcast_to(cot[:, None, :], (groups, DEPTH, 128)).reshape(rows, 128)
    spread = jnp.where(depth_match(rows), spread, 0.0).astype(BF16)
    lane = iota((1, 128), 1)
    wide_lane = iota((1, NET_WIDTH), 1)
    head = weights_ref[HEAD_ROW:PARAM_ROWS, :].astype(F32)
    outer = mul(spread, acts_ref[0, 0, LAYERS - 1], TN)[h * 64 : (h + 1) * 64]
    head_grad = jnp.sum(outer.reshape(4, DEPTH, NET_WIDTH), axis=1)
    bias_head = jnp.zeros((1, NET_WIDTH), F32)
    for c in range(4):
        value = jnp.sum(jnp.where((lane >> 4) == h * 4 + c, sums, 0.0), axis=1, keepdims=True)
        bias_head = bias_head + jnp.where(wide_lane == c, value, 0.0)
    up = mul(spread, head_tile(head, h))
    bias_lines = [None] * LAYERS
    for k in reversed(range(LAYERS)):
        pre_grad = jnp.where(acts_ref[0, 0, k].astype(F32) > 0, up, 0.0).astype(BF16)
        bias_lines[k] = jnp.sum(pre_grad.astype(F32), axis=0, keepdims=True)
        if k > 0:
            start = ENC_WIDTH + (k - 1) * NET_WIDTH
            total_ref[start : start + NET_WIDTH, :] += mul(acts_ref[0, 0, k - 1], pre_grad, TN)
            up = mul(pre_grad, weights_ref[start : start + NET_WIDTH, :], NT)
        else:
            total_ref[0:ENC_WIDTH, :] += mul(x_ref[...], pre_grad, TN)[
                h * ENC_WIDTH : (h + 1) * ENC_WIDTH
            ]
    total_ref[HEAD_ROW:PARAM_ROWS, :] += jnp.concatenate(
        [head_grad, jnp.zeros((4, NET_WIDTH), F32), bias_head]
        + bias_lines
        + [jnp.zeros((3, NET_WIDTH), F32)],
        axis=0,
    )

    @pl.when(third == THIRDS - 1)
    def _():
        quarter = own_ref.shape[0]
        for k, share_ref in enumerate((own_ref, first_ref, second_ref, third_ref)):
            start = pl.multiple_of(order_ref[k] * quarter, 8)
            share_ref[...] = total_ref[pl.ds(start, quarter), :].astype(share_ref.dtype)


def adam_kernel(
    order_ref,
    own_ref,
    first_ref,
    second_ref,
    third_ref,
    param_ref,
    one_ref,
    two_ref,
    *refs,
):
    step = pl.program_id(0)
    new_param_ref, new_one_ref, new_two_ref = refs[-3:]
    for k, share_ref in enumerate((own_ref, first_ref, second_ref, third_ref)):

        @pl.when(step == k)
        def _():
            new_param, new_one, new_two = adam_update(
                param_ref[0], share_ref[...].astype(F32), one_ref[0], two_ref[0]
            )
            new_param_ref[0] = new_param
            new_one_ref[0] = new_one
            new_two_ref[0] = new_two


def cost(micros):
    return pl.CostEstimate(
        flops=int(micros * 1e9), bytes_accessed=int(micros * 3e6), transcendentals=0
    )


def limits(mib=48):
    return pltpu.CompilerParams(vmem_limit_bytes=mib * 1024 * 1024)


def shape_of(dims, kind):
    return jax.ShapeDtypeStruct(dims, kind)


def shards(
    features,
    spacing,
    targets,
    ray_length,
    cell_id,
    slot_rank,
    image_id,
    params,
    first_moment,
    second_moment,
    code_table,
    table_first,
    table_second,
):
    groups = lax.axis_size("expert")
    places = groups * DEPTH
    cell_rows = cell_id.T
    rank_rows = slot_rank.T
    outgoing = pl.pallas_call(
        dispatch_kernel,
        out_shape=shape_of((places, THIRDS * 128), BF16),
        scratch_shapes=[
            pltpu.VMEM((places, SAMPLES * RAYS), BF16),
            pltpu.VMEM((THIRDS * 128, SAMPLES * RAYS), BF16),
        ],
        compiler_params=limits(),
        name="dispatch",
    )(jnp.transpose(features, (1, 2, 0)), cell_rows, rank_rows)
    arrived = lax.all_to_all(outgoing, "expert", split_axis=0, concat_axis=0, tiled=True)

    whole = lambda *dims: pl.BlockSpec(dims, lambda i: (0,) * len(dims))
    third_rows = pl.BlockSpec((places, 128), lambda i: (0, i))
    third_acts = pl.BlockSpec((1, 2, LAYERS, places, NET_WIDTH), lambda i: (i, 0, 0, 0, 0))
    acts, raw_out = pl.pallas_call(
        forward_kernel,
        grid=(THIRDS,),
        in_specs=[third_rows, whole(2, PARAM_ROWS, NET_WIDTH)],
        out_specs=[third_acts, whole(groups, 8, 128)],
        out_shape=[
            shape_of((THIRDS, 2, LAYERS, places, NET_WIDTH), BF16),
            shape_of((groups, 8, 128), F32),
        ],
        scratch_shapes=[pltpu.VMEM((2, PARAM_ROWS, NET_WIDTH), BF16)],
        compiler_params=limits(),
        name="forward",
    )(arrived, params)
    returned = lax.all_to_all(raw_out, "expert", split_axis=0, concat_axis=0, tiled=True)

    table_shape = shape_of(code_table.shape, F32)
    cot_out, loss, new_table, new_table_first, new_table_second = pl.pallas_call(
        ray_kernel,
        out_shape=[
            shape_of((groups, 8, 128), BF16),
            shape_of((1, RAYS), F32),
            table_shape,
            table_shape,
            table_shape,
        ],
        scratch_shapes=[
            pltpu.VMEM((512, 3 * groups), BF16),
            pltpu.VMEM((4, SAMPLES, RAYS), F32),
            pltpu.VMEM((groups, 8, 128), F32),
        ],
        compiler_params=limits(),
        name="rays",
    )(
        returned,
        cell_rows,
        rank_rows,
        image_id.reshape(1, RAYS),
        ray_length.reshape(1, RAYS),
        spacing.T,
        targets,
        code_table,
        table_first,
        table_second,
    )
    cot_in = lax.all_to_all(cot_out, "expert", split_axis=0, concat_axis=0, tiled=True)

    copies = lax.axis_size("dp")
    quarter = -(-PARAM_ROWS // (8 * copies)) * 8
    turns = jnp.arange(copies, dtype=jnp.int32)
    position = lax.axis_index("dp")
    lent = lambda *dims: pl.BlockSpec(dims, lambda i, order: (0,) * len(dims))

    def send(value, distance):
        return lax.ppermute(value, "dp", [(i, (i + distance) % copies) for i in range(copies)])

    def gradient(h):
        return pl.pallas_call(
            functools.partial(backward_kernel, h),
            grid_spec=pltpu.PrefetchScalarGridSpec(
                num_scalar_prefetch=1,
                grid=(THIRDS,),
                in_specs=[
                    pl.BlockSpec((places, 128), lambda i, order: (0, i)),
                    pl.BlockSpec(
                        (1, 1, LAYERS, places, NET_WIDTH), lambda i, order: (i, h, 0, 0, 0)
                    ),
                    lent(groups, 8, 128),
                    pl.BlockSpec((1, PARAM_ROWS, NET_WIDTH), lambda i, order: (h, 0, 0)),
                ],
                out_specs=[lent(quarter, NET_WIDTH)] * 4,
                scratch_shapes=[
                    pltpu.VMEM((PARAM_ROWS, NET_WIDTH), BF16),
                    pltpu.VMEM((copies * quarter, NET_WIDTH), F32),
                    pltpu.VMEM((groups, 8, 128), F32),
                ],
            ),
            out_shape=[shape_of((quarter, NET_WIDTH), F32)]
            + [shape_of((quarter, NET_WIDTH), BF16)] * 3,
            compiler_params=limits(),
            cost_estimate=cost(6.0),
            name="backward",
        )((position + turns) % copies, arrived, acts, cot_in, params)

    def collect(shares):
        share = shares[0]
        for k in (2, 1, 3):
            share = share + send(shares[k], k).astype(F32)
        share = share.astype(BF16)
        behind, ahead = send(share, 1), send(share, 3)
        return share, behind, send(ahead, 3), ahead

    def update(h, pieces, earlier):
        block = pl.BlockSpec((1, quarter, NET_WIDTH), lambda i, order: (h, order[i], 0))
        return pl.pallas_call(
            adam_kernel,
            grid_spec=pltpu.PrefetchScalarGridSpec(
                num_scalar_prefetch=1,
                grid=(copies,),
                in_specs=[lent(quarter, NET_WIDTH)] * 4
                + [block] * 3
                + [pl.BlockSpec(memory_space=pl.ANY)] * len(earlier),
                out_specs=[block] * 3,
            ),
            out_shape=[shape_of(params.shape, F32)] * 3,
            input_output_aliases={8 + i: i for i in range(len(earlier))},
            compiler_params=limits(),
            cost_estimate=cost(2.0),
            name="adam",
        )(
            (position - turns) % copies,
            *pieces,
            params,
            first_moment,
            second_moment,
            *earlier,
        )

    pieces = [collect(gradient(h)) for h in range(2)]
    updated = update(0, pieces[0], ())
    new_params, new_first, new_second = update(1, pieces[1], updated)
    return (
        loss.reshape(RAYS),
        new_params,
        new_first,
        new_second,
        new_table,
        new_table_first,
        new_table_second,
    )


def solution(mesh):
    rays = ("expert", "dp")
    table = P(rays, None)
    block = P("expert", None, None)
    return jax.shard_map(
        shards,
        mesh=mesh,
        in_specs=(
            P(rays, None, None),
            P(rays, None),
            P(None, rays),
            P(rays),
            P(rays, None),
            P(rays, None),
            P(rays),
            block,
            block,
            block,
            table,
            table,
            table,
        ),
        out_specs=(P(rays), block, block, block, table, table, table),
        check_vma=False,
    )
```

```python
import functools

import jax
import jax.numpy as jnp
from jax import lax
from jax.experimental import pallas as pl
from jax.experimental.pallas import tpu as pltpu
from jax.sharding import PartitionSpec as P

NET_WIDTH = 256
CODE_WIDTH = 64
ENC_WIDTH = 64
LAYERS = 4
SAMPLES = 32
RAYS = 128
IMAGES_DEV = 16
CAPACITY = 48
DEPTH = 16
THIRDS = CAPACITY // DEPTH
PARTS = 2
HEAD_ROW = ENC_WIDTH + (LAYERS - 1) * NET_WIDTH
PARAM_ROWS = HEAD_ROW + 16

F32 = jnp.float32
BF16 = jnp.bfloat16

BETA_ONE = 0.9
BETA_TWO = 0.999
LEARN_RATE = 0.001
ADAM_EPS = 1e-08
CORRECT_ONE = 1.0 - 0.9**10
CORRECT_TWO = 1.0 - 0.999**10

NN = (((1,), (0,)), ((), ()))
NT = (((1,), (1,)), ((), ()))
TN = (((0,), (0,)), ((), ()))


def mul(left, right, dims=NN):
    return lax.dot_general(left, right, dims, preferred_element_type=F32)


def iota(shape, dim):
    return lax.broadcasted_iota(jnp.int32, shape, dim)


def three_parts(value):
    high = value.astype(BF16)
    rest = value - high.astype(F32)
    middle = rest.astype(BF16)
    low = (rest - middle.astype(F32)).astype(BF16)
    return [high, middle, low]


def adam_update(param_now, gradient, moment_one, moment_two):
    new_one = BETA_ONE * moment_one + (1.0 - BETA_ONE) * gradient
    new_two = BETA_TWO * moment_two + (1.0 - BETA_TWO) * gradient * gradient
    update = LEARN_RATE * (new_one / CORRECT_ONE) / (jnp.sqrt(new_two / CORRECT_TWO) + ADAM_EPS)
    return (param_now - update, new_one, new_two)


def dispatch_kernel(
    feat_in, cell_in, rank_in, out_ref, hot_ref, rows_ref, feat_ref, cell_ref, rank_ref, sems
):
    places = out_ref.shape[0]
    moves = [
        pltpu.make_async_copy(source, target, sems.at[i])
        for i, (source, target) in enumerate(
            ((cell_in, cell_ref), (rank_in, rank_ref), (feat_in, feat_ref))
        )
    ]
    for move in moves:
        move.start()
    moves[0].wait()
    moves[1].wait()
    for i in range(SAMPLES):
        cell = cell_ref[i : i + 1, :]
        rank = rank_ref[i : i + 1, :]
        place = jnp.where(rank >= 0, (cell >> 1) * DEPTH + (rank & (DEPTH - 1)), -1)
        hot_ref[:, i * RAYS : (i + 1) * RAYS] = jnp.where(
            iota((places, RAYS), 0) == place, 1.0, 0.0
        ).astype(BF16)
    moves[2].wait()
    for i in range(SAMPLES):
        inner = (rank_ref[i : i + 1, :] >> 4) * 2 + (cell_ref[i : i + 1, :] & 1)
        feat = feat_ref[i].astype(F32)
        for q in range(THIRDS * 2):
            rows_ref[q * ENC_WIDTH : (q + 1) * ENC_WIDTH, i * RAYS : (i + 1) * RAYS] = jnp.where(
                inner == q, feat, 0.0
            ).astype(BF16)
    out_ref[...] = mul(hot_ref[...], rows_ref[...], NT).astype(BF16)


def depth_match(rows):
    return (iota((rows, 128), 0) & (DEPTH - 1)) == (iota((rows, 128), 1) & (DEPTH - 1))


def first_matrix(weights_ref, held):
    matrix = weights_ref[held, 0:ENC_WIDTH, :]
    blank = jnp.zeros_like(matrix)
    return jnp.concatenate([matrix, blank] if held == 0 else [blank, matrix], axis=0)


def hidden_matrix(weights_ref, held, layer):
    start = ENC_WIDTH + (layer - 1) * NET_WIDTH
    return weights_ref[held, start : start + NET_WIDTH, :]


def head_tile(head, held):
    rows = jnp.concatenate(
        [jnp.broadcast_to(head[c : c + 1, :], (DEPTH, NET_WIDTH)) for c in range(4)], axis=0
    )
    blank = jnp.zeros_like(rows)
    return jnp.concatenate([rows, blank] if held == 0 else [blank, rows], axis=0).astype(BF16)


def slot_rows(x_ref):
    return jnp.concatenate([x_ref[:, j * 128 : (j + 1) * 128] for j in range(THIRDS)], axis=0)


def forward_kernel(
    x_ref, params_ref, acts0_ref, acts1_ref, out_ref, weights_ref, lines_ref, held_ref, sems
):
    groups = out_ref.shape[0]
    rows = held_ref.shape[1]
    moves = []
    weights_ref[...] = params_ref[...].astype(BF16)
    heads = [weights_ref[h, HEAD_ROW:PARAM_ROWS, :].astype(F32) for h in range(2)]
    for j in range(4):
        h, c = j // 2, (j % 2) * 2
        pair = jnp.concatenate(
            [heads[h][4 + c : 5 + c, :CODE_WIDTH], heads[h][5 + c : 6 + c, :CODE_WIDTH]], axis=1
        )
        lines_ref[:, 3 + j, :] = jnp.broadcast_to(pair, (groups, 128))
    lane = iota((1, 128), 1)
    shift = jnp.zeros((1, 128), F32)
    total = jnp.zeros((rows, 128), F32)
    for h, acts_ref in enumerate((acts0_ref, acts1_ref)):
        current = slot_rows(x_ref)
        for k in range(LAYERS):
            matrix = first_matrix(weights_ref, h) if k == 0 else hidden_matrix(weights_ref, h, k)
            preact = mul(current, matrix) + heads[h][9 + k : 10 + k, :]
            current = jnp.maximum(preact, 0.0).astype(BF16)
            place = h * LAYERS + k
            held_ref[place] = current
            move = pltpu.make_async_copy(held_ref.at[place], acts_ref.at[k], sems.at[place])
            move.start()
            moves.append(move)
        total = total + mul(current, head_tile(heads[h], h), NT)
        for c in range(4):
            shift = shift + jnp.where((lane >> 4) == h * 4 + c, heads[h][8:9, c : c + 1], 0.0)
    total = jnp.where(depth_match(rows), total + shift, 0.0)
    raw = jnp.sum(total.reshape(THIRDS * groups, DEPTH, 128), axis=1)
    low = raw - raw.astype(BF16).astype(F32)
    density = []
    for j in range(THIRDS):
        span = slice(j * groups, (j + 1) * groups)
        lines_ref[:, j, :] = raw[span]
        density += [low[span, 0:DEPTH], low[span, 64 : 64 + DEPTH]]
    lines_ref[:, 7, :] = jnp.concatenate(density + [jnp.zeros((groups, 32), F32)], axis=1)
    out_ref[...] = lines_ref[...].astype(BF16)
    for move in moves:
        move.wait()


def one_sample_row(cell_ref, rank_ref, image, i, owners):
    cell = cell_ref[pl.ds(i, 1), :]
    rank = rank_ref[pl.ds(i, 1), :]
    live = rank >= 0
    owner = jnp.where(live, cell >> 1, -1)
    hot = jnp.where(iota((owners, RAYS), 0) == owner, 1.0, 0.0).astype(BF16)
    held = cell & 1
    slot = jnp.where(live, ((rank >> 4) * 2 + held) * DEPTH + (rank & (DEPTH - 1)), -1)
    code = jnp.where(live, held * IMAGES_DEV + image, -1)
    slot_mask = iota((THIRDS * 2 * DEPTH, RAYS), 0) == slot
    code_mask = iota((2 * IMAGES_DEV, RAYS), 0) == code
    masks = [slot_mask[q * DEPTH : (q + 1) * DEPTH] for q in range(THIRDS * 2)]
    masks += [code_mask[h * IMAGES_DEV : (h + 1) * IMAGES_DEV] for h in range(2)]
    return hot, masks


def running_sum(value):
    step = 1
    while step < SAMPLES:
        value = value + jnp.concatenate(
            [jnp.zeros((step, RAYS), F32), value[: SAMPLES - step]], axis=0
        )
        step *= 2
    return value


def running_sum_back(value):
    step = 1
    while step < SAMPLES:
        value = value + jnp.concatenate([value[step:], jnp.zeros((step, RAYS), F32)], axis=0)
        step *= 2
    return value


def ray_kernel(
    back_ref,
    cell_ref,
    rank_ref,
    image_ref,
    length_ref,
    spacing_ref,
    targets_ref,
    code_ref,
    first_ref,
    second_ref,
    out_ref,
    loss_ref,
    new_code_ref,
    new_first_ref,
    new_second_ref,
    table_ref,
    raw_ref,
    lines_ref,
):
    owners = back_ref.shape[0]
    image = image_ref[...] & (IMAGES_DEV - 1)
    code = code_ref[...].astype(BF16).astype(F32)
    tile = jnp.concatenate([code] * 8, axis=0)
    tile = jnp.concatenate([tile, tile], axis=1)
    block_row = iota((128, 128), 0) >> 4
    block_lane = iota((128, 128), 1) >> 6
    code_blocks = [
        jnp.where(block_row == 2 * j + block_lane, tile, 0.0).astype(BF16) for j in range(4)
    ]
    lines_ref[...] = back_ref[...].astype(F32)
    queries = [lines_ref[:, 3 + j, :].astype(BF16) for j in range(4)]
    code_part = mul(queries[0], code_blocks[0], NT)
    for j in range(1, 4):
        code_part = code_part + mul(queries[j], code_blocks[j], NT)
    code_parts = three_parts(code_part.T)
    lows = lines_ref[:, 7, :]
    blank = jnp.zeros((owners, 64 - DEPTH), F32)
    highs, rests = [], []
    for j in range(THIRDS):
        start = j * 2 * DEPTH
        rest = [lows[:, start : start + DEPTH], blank]
        rest += [lows[:, start + DEPTH : start + 2 * DEPTH], blank]
        highs.append(lines_ref[:, j, :].T.astype(BF16))
        rests.append(jnp.concatenate(rest, axis=1).T.astype(BF16))
    table_ref[...] = jnp.concatenate(
        [
            jnp.concatenate(highs + code_parts[0:1], axis=0),
            jnp.concatenate(rests + code_parts[1:2], axis=0),
        ],
        axis=1,
    )

    def pick(i, carry):
        sides = [one_sample_row(cell_ref, rank_ref, image, 2 * i + half, owners) for half in range(2)]
        hots = jnp.concatenate([side[0] for side in sides], axis=1)
        found = mul(table_ref[...], jnp.concatenate([hots] * PARTS, axis=0))
        for half in range(2):
            masks = sides[half][1]
            for c in range(4):
                total = jnp.zeros((DEPTH, RAYS), F32)
                for q in range(THIRDS * 2 + 2):
                    start = q * 64 + c * DEPTH
                    total = total + jnp.where(
                        masks[q], found[start : start + DEPTH, half * RAYS : (half + 1) * RAYS], 0.0
                    )
                raw_ref[c, pl.ds(2 * i + half, 1), :] = jnp.sum(total, axis=0, keepdims=True)
        return carry

    lax.fori_loop(0, SAMPLES // 2, pick, 0, unroll=True)

    spacing = spacing_ref[...]
    live = jnp.where(iota((SAMPLES, RAYS), 0) < length_ref[...], 1.0, 0.0)
    raw_density = raw_ref[0]
    small = jnp.exp(-jnp.abs(raw_density))
    density = jnp.maximum(raw_density, 0.0) + jnp.log1p(small)
    slope = jnp.where(raw_density >= 0, 1.0, small) / (1.0 + small)
    colors = []
    for c in range(3):
        raw_color = raw_ref[1 + c]
        tail = jnp.exp(-jnp.abs(raw_color))
        colors.append(jnp.where(raw_color >= 0, 1.0, tail) / (1.0 + tail))
    reach = spacing * live
    tau = density * reach
    before = running_sum(tau) - tau
    passed = jnp.exp(-before)
    kept = jnp.exp(-tau)
    weight = passed * (1.0 - kept)
    gaps = []
    loss = jnp.zeros((1, RAYS), F32)
    for c in range(3):
        gap = jnp.sum(weight * colors[c], axis=0, keepdims=True) - targets_ref[c : c + 1, :]
        gaps.append(gap)
        loss = loss + gap * gap
    loss_ref[...] = 0.5 * loss
    pull = gaps[0] * colors[0] + gaps[1] * colors[1] + gaps[2] * colors[2]
    behind = weight * pull
    tau_grad = pull * passed * kept - (running_sum_back(behind) - behind)
    raw_ref[0] = (tau_grad * reach * slope).astype(BF16).astype(F32)
    for c in range(3):
        raw_ref[1 + c] = (
            (weight * gaps[c] * (colors[c] * (1.0 - colors[c]))).astype(BF16).astype(F32)
        )

    def put(i, total):
        hots, rows = [], []
        for half in range(2):
            hot, masks = one_sample_row(cell_ref, rank_ref, image, 2 * i + half, owners)
            cots = [raw_ref[c, pl.ds(2 * i + half, 1), :] for c in range(4)]
            hots.append(hot)
            rows.append(
                jnp.concatenate(
                    [
                        jnp.where(masks[q], cots[c], 0.0)
                        for q in range(THIRDS * 2 + 2)
                        for c in range(4)
                    ],
                    axis=0,
                ).astype(BF16)
            )
        return total + mul(
            jnp.concatenate(rows, axis=1), jnp.concatenate(hots, axis=1), NT
        )

    placed = lax.fori_loop(
        0, SAMPLES // 2, put, jnp.zeros((512, owners), F32), unroll=True
    )
    for j in range(THIRDS):
        lines_ref[:, j, :] = placed[j * 128 : (j + 1) * 128].T
    image_sums = placed[384:512]
    sums_parts = three_parts(image_sums)
    sums_wide = jnp.concatenate(sums_parts, axis=1)
    sums_flip = jnp.concatenate(three_parts(image_sums.T), axis=1)
    table_grad = jnp.zeros((IMAGES_DEV, CODE_WIDTH), F32)
    for j in range(4):
        lines_ref[:, 3 + j, :] = mul(sums_flip, jnp.concatenate([code_blocks[j]] * 3, axis=0))
        product = mul(sums_wide, jnp.concatenate([queries[j]] * 3, axis=0))
        low = 2 * j * IMAGES_DEV
        table_grad = table_grad + product[low : low + IMAGES_DEV, :CODE_WIDTH]
        table_grad = table_grad + product[low + IMAGES_DEV : low + 2 * IMAGES_DEV, CODE_WIDTH:]
    lines_ref[:, 7, :] = jnp.zeros((owners, 128), F32)
    out_ref[...] = lines_ref[...].astype(BF16)
    new_code, new_first, new_second = adam_update(
        code_ref[...], table_grad, first_ref[...], second_ref[...]
    )
    new_code_ref[...] = new_code
    new_first_ref[...] = new_first
    new_second_ref[...] = new_second


def backward_kernel(
    h,
    order_ref,
    x_ref,
    acts_in,
    cot_in_ref,
    weights_ref,
    own_ref,
    first_ref,
    second_ref,
    third_ref,
    total_ref,
    cot_ref,
    acts_ref,
    sems,
):
    groups = cot_ref.shape[0]
    places = x_ref.shape[0]
    moves = [
        pltpu.make_async_copy(acts_in.at[k], acts_ref.at[k], sems.at[k]) for k in range(LAYERS)
    ]
    for k in reversed(range(LAYERS)):
        moves[k].start()
    cot_ref[...] = cot_in_ref[...].astype(F32)
    cots = [cot_ref[:, j, :] for j in range(THIRDS)]
    sums = jnp.sum(cots[0] + cots[1] + cots[2], axis=0, keepdims=True)
    spread = jnp.concatenate(
        [
            jnp.broadcast_to(cot[:, None, :], (groups, DEPTH, 128)).reshape(places, 128)
            for cot in cots
        ],
        axis=0,
    )
    spread = jnp.where(depth_match(THIRDS * places), spread, 0.0).astype(BF16)
    code_lines = []
    for c in range(4):
        line = jnp.sum(cot_ref[:, 3 + h * 2 + c // 2, :], axis=0, keepdims=True)
        start = (c % 2) * CODE_WIDTH
        line = line[:, start : start + CODE_WIDTH]
        code_lines.append(
            jnp.concatenate([line, jnp.zeros((1, NET_WIDTH - CODE_WIDTH), F32)], axis=1)
        )
    lane = iota((1, 128), 1)
    wide_lane = iota((1, NET_WIDTH), 1)
    head = weights_ref[h, HEAD_ROW:PARAM_ROWS, :].astype(F32)
    moves[LAYERS - 1].wait()
    outer = mul(spread, acts_ref[LAYERS - 1], TN)[h * 64 : (h + 1) * 64]
    head_grad = jnp.sum(outer.reshape(4, DEPTH, NET_WIDTH), axis=1)
    bias_head = jnp.zeros((1, NET_WIDTH), F32)
    for c in range(4):
        value = jnp.sum(jnp.where((lane >> 4) == h * 4 + c, sums, 0.0), axis=1, keepdims=True)
        bias_head = bias_head + jnp.where(wide_lane == c, value, 0.0)
    up = mul(spread, head_tile(head, h))
    bias_lines = [None] * LAYERS
    for k in reversed(range(LAYERS)):
        pre_grad = jnp.where(acts_ref[k].astype(F32) > 0, up, 0.0).astype(BF16)
        bias_lines[k] = jnp.sum(pre_grad.astype(F32), axis=0, keepdims=True)
        if k > 0:
            start = ENC_WIDTH + (k - 1) * NET_WIDTH
            up = mul(pre_grad, hidden_matrix(weights_ref, h, k), NT)
            moves[k - 1].wait()
            total_ref[start : start + NET_WIDTH, :] = mul(acts_ref[k - 1], pre_grad, TN)
        else:
            total_ref[0:ENC_WIDTH, :] = mul(slot_rows(x_ref), pre_grad, TN)[
                h * ENC_WIDTH : (h + 1) * ENC_WIDTH
            ]
    total_ref[HEAD_ROW:PARAM_ROWS, :] = jnp.concatenate(
        [head_grad] + code_lines + [bias_head] + bias_lines + [jnp.zeros((3, NET_WIDTH), F32)],
        axis=0,
    )
    spare = total_ref.shape[0] - PARAM_ROWS
    total_ref[PARAM_ROWS:, :] = jnp.zeros((spare, NET_WIDTH), F32)
    quarter = own_ref.shape[0]
    for k, share_ref in enumerate((own_ref, first_ref, second_ref, third_ref)):
        start = pl.multiple_of(order_ref[k] * quarter, 8)
        share_ref[...] = total_ref[pl.ds(start, quarter), :].astype(share_ref.dtype)


def adam_kernel(
    order_ref,
    own_ref,
    first_ref,
    second_ref,
    third_ref,
    param_ref,
    one_ref,
    two_ref,
    *refs,
):
    step = pl.program_id(0)
    new_param_ref, new_one_ref, new_two_ref = refs[-3:]
    for k, share_ref in enumerate((own_ref, first_ref, second_ref, third_ref)):

        @pl.when(step == k)
        def _():
            new_param, new_one, new_two = adam_update(
                param_ref[0], share_ref[...].astype(F32), one_ref[0], two_ref[0]
            )
            new_param_ref[0] = new_param
            new_one_ref[0] = new_one
            new_two_ref[0] = new_two


def cost(micros):
    return pl.CostEstimate(
        flops=int(micros * 1e9), bytes_accessed=int(micros * 3e6), transcendentals=0
    )


def limits(mib=48):
    return pltpu.CompilerParams(vmem_limit_bytes=mib * 1024 * 1024)


def shape_of(dims, kind):
    return jax.ShapeDtypeStruct(dims, kind)


def shards(
    features,
    spacing,
    targets,
    ray_length,
    cell_id,
    slot_rank,
    image_id,
    params,
    first_moment,
    second_moment,
    code_table,
    table_first,
    table_second,
):
    groups = lax.axis_size("expert")
    places = groups * DEPTH
    cell_rows = cell_id.T
    rank_rows = slot_rank.T
    outgoing = pl.pallas_call(
        dispatch_kernel,
        out_shape=shape_of((places, THIRDS * 128), BF16),
        in_specs=[pl.BlockSpec(memory_space=pl.ANY)] * 3,
        scratch_shapes=[
            pltpu.VMEM((places, SAMPLES * RAYS), BF16),
            pltpu.VMEM((THIRDS * 128, SAMPLES * RAYS), BF16),
            pltpu.VMEM((SAMPLES, ENC_WIDTH, RAYS), BF16),
            pltpu.VMEM((SAMPLES, RAYS), jnp.int32),
            pltpu.VMEM((SAMPLES, RAYS), jnp.int32),
            pltpu.SemaphoreType.DMA((3,)),
        ],
        compiler_params=limits(59),
        name="dispatch",
    )(jnp.transpose(features, (1, 2, 0)), cell_rows, rank_rows)
    arrived = lax.all_to_all(outgoing, "expert", split_axis=0, concat_axis=0, tiled=True)

    slots = THIRDS * places
    vmem = pl.BlockSpec(memory_space=pltpu.VMEM)
    anywhere = pl.BlockSpec(memory_space=pl.ANY)
    acts_shape = shape_of((LAYERS, slots, NET_WIDTH), BF16)
    *acts, raw_out, weights = pl.pallas_call(
        forward_kernel,
        out_shape=[
            acts_shape,
            acts_shape,
            shape_of((groups, 8, 128), BF16),
            shape_of((2, PARAM_ROWS, NET_WIDTH), BF16),
        ],
        out_specs=[anywhere, anywhere, vmem, vmem],
        scratch_shapes=[
            pltpu.VMEM((groups, 8, 128), F32),
            pltpu.VMEM((2 * LAYERS, slots, NET_WIDTH), BF16),
            pltpu.SemaphoreType.DMA((2 * LAYERS,)),
        ],
        compiler_params=limits(48),
        name="forward",
    )(arrived, params)
    returned = lax.all_to_all(raw_out, "expert", split_axis=0, concat_axis=0, tiled=True)

    table_shape = shape_of(code_table.shape, F32)
    cot_out, loss, new_table, new_table_first, new_table_second = pl.pallas_call(
        ray_kernel,
        out_shape=[
            shape_of((groups, 8, 128), BF16),
            shape_of((1, RAYS), F32),
            table_shape,
            table_shape,
            table_shape,
        ],
        scratch_shapes=[
            pltpu.VMEM((512, PARTS * groups), BF16),
            pltpu.VMEM((4, SAMPLES, RAYS), F32),
            pltpu.VMEM((groups, 8, 128), F32),
        ],
        compiler_params=limits(16),
        name="rays",
    )(
        returned,
        cell_rows,
        rank_rows,
        image_id.reshape(1, RAYS),
        ray_length.reshape(1, RAYS),
        spacing.T,
        targets,
        code_table,
        table_first,
        table_second,
    )
    cot_in = lax.all_to_all(cot_out, "expert", split_axis=0, concat_axis=0, tiled=True)

    copies = lax.axis_size("dp")
    quarter = -(-PARAM_ROWS // (8 * copies)) * 8
    turns = jnp.arange(copies, dtype=jnp.int32)
    position = lax.axis_index("dp")
    lent = lambda *dims: pl.BlockSpec(dims, lambda i, order: (0,) * len(dims))

    def send(value, distance):
        return lax.ppermute(value, "dp", [(i, (i + distance) % copies) for i in range(copies)])

    def gradient(h):
        return pl.pallas_call(
            functools.partial(backward_kernel, h),
            in_specs=[pl.BlockSpec(memory_space=pltpu.SMEM), vmem, anywhere, vmem, vmem],
            out_specs=[vmem] * 4,
            out_shape=[shape_of((quarter, NET_WIDTH), F32)]
            + [shape_of((quarter, NET_WIDTH), BF16)] * 3,
            scratch_shapes=[
                pltpu.VMEM((copies * quarter, NET_WIDTH), F32),
                pltpu.VMEM((groups, 8, 128), F32),
                pltpu.VMEM((LAYERS, slots, NET_WIDTH), BF16),
                pltpu.SemaphoreType.DMA((LAYERS,)),
            ],
            compiler_params=limits(48),
            cost_estimate=cost(6.0),
            name="backward",
        )((position + turns) % copies, arrived, acts[h], cot_in, weights)

    def collect(shares):
        share = shares[0]
        for k in (2, 1, 3):
            share = share + send(shares[k], k).astype(F32)
        share = share.astype(BF16)
        behind, ahead = send(share, 1), send(share, 3)
        return share, behind, send(ahead, 3), ahead

    def update(h, pieces, earlier):
        block = pl.BlockSpec((1, quarter, NET_WIDTH), lambda i, order: (h, order[i], 0))
        return pl.pallas_call(
            adam_kernel,
            grid_spec=pltpu.PrefetchScalarGridSpec(
                num_scalar_prefetch=1,
                grid=(copies,),
                in_specs=[lent(quarter, NET_WIDTH)] * 4
                + [block] * 3
                + [pl.BlockSpec(memory_space=pl.ANY)] * len(earlier),
                out_specs=[block] * 3,
            ),
            out_shape=[shape_of(params.shape, F32)] * 3,
            input_output_aliases={8 + i: i for i in range(len(earlier))},
            compiler_params=limits(12),
            cost_estimate=cost(2.0),
            name="adam",
        )(
            (position - turns) % copies,
            *pieces,
            params,
            first_moment,
            second_moment,
            *earlier,
        )

    pieces = [collect(gradient(h)) for h in range(2)]
    updated = update(0, pieces[0], ())
    new_params, new_first, new_second = update(1, pieces[1], updated)
    return (
        loss.reshape(RAYS),
        new_params,
        new_first,
        new_second,
        new_table,
        new_table_first,
        new_table_second,
    )


def solution(mesh):
    rays = ("expert", "dp")
    table = P(rays, None)
    block = P("expert", None, None)
    return jax.shard_map(
        shards,
        mesh=mesh,
        in_specs=(
            P(rays, None, None),
            P(rays, None),
            P(None, rays),
            P(rays),
            P(rays, None),
            P(rays, None),
            P(rays),
            block,
            block,
            block,
            table,
            table,
            table,
        ),
        out_specs=(P(rays), block, block, block, table, table, table),
        check_vma=False,
    )
```

```python
import functools

import jax
import jax.numpy as jnp
from jax import lax
from jax.experimental import pallas as pl
from jax.experimental.pallas import tpu as pltpu
from jax.sharding import PartitionSpec as P

NET_WIDTH = 256
CODE_WIDTH = 64
ENC_WIDTH = 64
LAYERS = 4
SAMPLES = 32
RAYS = 128
IMAGES_DEV = 16
CAPACITY = 48
DEPTH = 16
THIRDS = CAPACITY // DEPTH
PARTS = 2
HEAD_ROW = ENC_WIDTH + (LAYERS - 1) * NET_WIDTH
PARAM_ROWS = HEAD_ROW + 16

F32 = jnp.float32
BF16 = jnp.bfloat16

BETA_ONE = 0.9
BETA_TWO = 0.999
LEARN_RATE = 0.001
ADAM_EPS = 1e-08
CORRECT_ONE = 1.0 - 0.9**10
CORRECT_TWO = 1.0 - 0.999**10

NN = (((1,), (0,)), ((), ()))
NT = (((1,), (1,)), ((), ()))
TN = (((0,), (0,)), ((), ()))


def mul(left, right, dims=NN):
    return lax.dot_general(left, right, dims, preferred_element_type=F32)


def iota(shape, dim):
    return lax.broadcasted_iota(jnp.int32, shape, dim)


def three_parts(value):
    high = value.astype(BF16)
    rest = value - high.astype(F32)
    middle = rest.astype(BF16)
    low = (rest - middle.astype(F32)).astype(BF16)
    return [high, middle, low]


def adam_update(param_now, gradient, moment_one, moment_two):
    new_one = BETA_ONE * moment_one + (1.0 - BETA_ONE) * gradient
    new_two = BETA_TWO * moment_two + (1.0 - BETA_TWO) * gradient * gradient
    update = LEARN_RATE * (new_one / CORRECT_ONE) / (jnp.sqrt(new_two / CORRECT_TWO) + ADAM_EPS)
    return (param_now - update, new_one, new_two)


def dispatch_kernel(
    feat_in, cell_in, rank_in, out_ref, hot_ref, rows_ref, feat_ref, cell_ref, rank_ref, sems
):
    places = out_ref.shape[0]
    moves = [
        pltpu.make_async_copy(source, target, sems.at[i])
        for i, (source, target) in enumerate(
            ((cell_in, cell_ref), (rank_in, rank_ref), (feat_in, feat_ref))
        )
    ]
    for move in moves:
        move.start()
    for move in moves:
        move.wait()
    for i in range(SAMPLES):
        cell = cell_ref[i : i + 1, :]
        rank = rank_ref[i : i + 1, :]
        place = jnp.where(rank >= 0, (cell >> 1) * DEPTH + (rank & (DEPTH - 1)), -1)
        inner = (rank >> 4) * 2 + (cell & 1)
        span = slice(i * RAYS, (i + 1) * RAYS)
        hot_ref[:, span] = jnp.where(iota((places, RAYS), 0) == place, 1.0, 0.0).astype(BF16)
        feat = feat_ref[i].astype(F32)
        for q in range(THIRDS * 2):
            rows_ref[q * ENC_WIDTH : (q + 1) * ENC_WIDTH, span] = jnp.where(
                inner == q, feat, 0.0
            ).astype(BF16)
    out_ref[...] = mul(hot_ref[...], rows_ref[...], NT).astype(BF16)


def depth_match(rows):
    return (iota((rows, 128), 0) & (DEPTH - 1)) == (iota((rows, 128), 1) & (DEPTH - 1))


def first_matrix(weights_ref, held):
    matrix = weights_ref[held, 0:ENC_WIDTH, :]
    blank = jnp.zeros_like(matrix)
    return jnp.concatenate([matrix, blank] if held == 0 else [blank, matrix], axis=0)


def hidden_matrix(weights_ref, held, layer):
    start = ENC_WIDTH + (layer - 1) * NET_WIDTH
    return weights_ref[held, start : start + NET_WIDTH, :]


def head_tile(head, held):
    rows = jnp.concatenate(
        [jnp.broadcast_to(head[c : c + 1, :], (DEPTH, NET_WIDTH)) for c in range(4)], axis=0
    )
    blank = jnp.zeros_like(rows)
    return jnp.concatenate([rows, blank] if held == 0 else [blank, rows], axis=0).astype(BF16)


def slot_rows(x_ref):
    return jnp.concatenate([x_ref[:, j * 128 : (j + 1) * 128] for j in range(THIRDS)], axis=0)


def forward_kernel(
    x_ref, params_ref, acts0_ref, acts1_ref, out_ref, weights_ref, lines_ref, held_ref, sems
):
    groups = out_ref.shape[0]
    rows = held_ref.shape[1]
    moves = []
    weights_ref[...] = params_ref[...].astype(BF16)
    heads = [weights_ref[h, HEAD_ROW:PARAM_ROWS, :].astype(F32) for h in range(2)]
    for j in range(4):
        h, c = j // 2, (j % 2) * 2
        pair = jnp.concatenate(
            [heads[h][4 + c : 5 + c, :CODE_WIDTH], heads[h][5 + c : 6 + c, :CODE_WIDTH]], axis=1
        )
        lines_ref[:, 3 + j, :] = jnp.broadcast_to(pair, (groups, 128))
    lane = iota((1, 128), 1)
    shift = jnp.zeros((1, 128), F32)
    total = jnp.zeros((rows, 128), F32)
    for h, acts_ref in enumerate((acts0_ref, acts1_ref)):
        current = slot_rows(x_ref)
        for k in range(LAYERS):
            matrix = first_matrix(weights_ref, h) if k == 0 else hidden_matrix(weights_ref, h, k)
            preact = mul(current, matrix) + heads[h][9 + k : 10 + k, :]
            current = jnp.maximum(preact, 0.0).astype(BF16)
            place = h * LAYERS + k
            held_ref[place] = current
            move = pltpu.make_async_copy(held_ref.at[place], acts_ref.at[k], sems.at[place])
            move.start()
            moves.append(move)
        total = total + mul(current, head_tile(heads[h], h), NT)
        for c in range(4):
            shift = shift + jnp.where((lane >> 4) == h * 4 + c, heads[h][8:9, c : c + 1], 0.0)
    total = jnp.where(depth_match(rows), total + shift, 0.0)
    raw = jnp.sum(total.reshape(THIRDS * groups, DEPTH, 128), axis=1)
    low = raw - raw.astype(BF16).astype(F32)
    density = []
    for j in range(THIRDS):
        span = slice(j * groups, (j + 1) * groups)
        lines_ref[:, j, :] = raw[span]
        density += [low[span, 0:DEPTH], low[span, 64 : 64 + DEPTH]]
    lines_ref[:, 7, :] = jnp.concatenate(density + [jnp.zeros((groups, 32), F32)], axis=1)
    out_ref[...] = lines_ref[...].astype(BF16)
    for move in moves:
        move.wait()


def one_sample_row(cell_ref, rank_ref, image, i, owners):
    cell = cell_ref[pl.ds(i, 1), :]
    rank = rank_ref[pl.ds(i, 1), :]
    live = rank >= 0
    owner = jnp.where(live, cell >> 1, -1)
    hot = jnp.where(iota((owners, RAYS), 0) == owner, 1.0, 0.0).astype(BF16)
    held = cell & 1
    slot = jnp.where(live, ((rank >> 4) * 2 + held) * DEPTH + (rank & (DEPTH - 1)), -1)
    code = jnp.where(live, held * IMAGES_DEV + image, -1)
    slot_mask = iota((THIRDS * 2 * DEPTH, RAYS), 0) == slot
    code_mask = iota((2 * IMAGES_DEV, RAYS), 0) == code
    masks = [slot_mask[q * DEPTH : (q + 1) * DEPTH] for q in range(THIRDS * 2)]
    masks += [code_mask[h * IMAGES_DEV : (h + 1) * IMAGES_DEV] for h in range(2)]
    return hot, masks


def running_sum(value):
    step = 1
    while step < SAMPLES:
        value = value + jnp.concatenate(
            [jnp.zeros((step, RAYS), F32), value[: SAMPLES - step]], axis=0
        )
        step *= 2
    return value


def running_sum_back(value):
    step = 1
    while step < SAMPLES:
        value = value + jnp.concatenate([value[step:], jnp.zeros((step, RAYS), F32)], axis=0)
        step *= 2
    return value


def ray_kernel(
    back_ref,
    cell_ref,
    rank_ref,
    image_ref,
    length_ref,
    spacing_ref,
    targets_ref,
    code_ref,
    first_ref,
    second_ref,
    out_ref,
    loss_ref,
    new_code_ref,
    new_first_ref,
    new_second_ref,
    table_ref,
    raw_ref,
    lines_ref,
):
    owners = back_ref.shape[0]
    image = image_ref[...] & (IMAGES_DEV - 1)
    code = code_ref[...].astype(BF16).astype(F32)
    tile = jnp.concatenate([code] * 8, axis=0)
    tile = jnp.concatenate([tile, tile], axis=1)
    block_row = iota((128, 128), 0) >> 4
    block_lane = iota((128, 128), 1) >> 6
    code_blocks = [
        jnp.where(block_row == 2 * j + block_lane, tile, 0.0).astype(BF16) for j in range(4)
    ]
    lines_ref[...] = back_ref[...].astype(F32)
    queries = [lines_ref[:, 3 + j, :].astype(BF16) for j in range(4)]
    code_part = mul(queries[0], code_blocks[0], NT)
    for j in range(1, 4):
        code_part = code_part + mul(queries[j], code_blocks[j], NT)
    code_parts = three_parts(code_part.T)
    lows = lines_ref[:, 7, :]
    blank = jnp.zeros((owners, 64 - DEPTH), F32)
    highs, rests = [], []
    for j in range(THIRDS):
        start = j * 2 * DEPTH
        rest = [lows[:, start : start + DEPTH], blank]
        rest += [lows[:, start + DEPTH : start + 2 * DEPTH], blank]
        highs.append(lines_ref[:, j, :].T.astype(BF16))
        rests.append(jnp.concatenate(rest, axis=1).T.astype(BF16))
    table_ref[...] = jnp.concatenate(
        [
            jnp.concatenate(highs + code_parts[0:1], axis=0),
            jnp.concatenate(rests + code_parts[1:2], axis=0),
        ],
        axis=1,
    )

    def pick(i, carry):
        sides = [one_sample_row(cell_ref, rank_ref, image, 2 * i + half, owners) for half in range(2)]
        hots = jnp.concatenate([side[0] for side in sides], axis=1)
        found = mul(table_ref[...], jnp.concatenate([hots] * PARTS, axis=0))
        for half in range(2):
            masks = sides[half][1]
            for c in range(4):
                total = jnp.zeros((DEPTH, RAYS), F32)
                for q in range(THIRDS * 2 + 2):
                    start = q * 64 + c * DEPTH
                    total = total + jnp.where(
                        masks[q], found[start : start + DEPTH, half * RAYS : (half + 1) * RAYS], 0.0
                    )
                raw_ref[c, pl.ds(2 * i + half, 1), :] = jnp.sum(total, axis=0, keepdims=True)
        return carry

    lax.fori_loop(0, SAMPLES // 2, pick, 0, unroll=4)

    spacing = spacing_ref[...]
    live = jnp.where(iota((SAMPLES, RAYS), 0) < length_ref[...], 1.0, 0.0)
    raw_density = raw_ref[0]
    small = jnp.exp(-jnp.abs(raw_density))
    density = jnp.maximum(raw_density, 0.0) + jnp.log1p(small)
    slope = jnp.where(raw_density >= 0, 1.0, small) / (1.0 + small)
    colors = []
    for c in range(3):
        raw_color = raw_ref[1 + c]
        tail = jnp.exp(-jnp.abs(raw_color))
        colors.append(jnp.where(raw_color >= 0, 1.0, tail) / (1.0 + tail))
    reach = spacing * live
    tau = density * reach
    before = running_sum(tau) - tau
    passed = jnp.exp(-before)
    kept = jnp.exp(-tau)
    weight = passed * (1.0 - kept)
    gaps = []
    loss = jnp.zeros((1, RAYS), F32)
    for c in range(3):
        gap = jnp.sum(weight * colors[c], axis=0, keepdims=True) - targets_ref[c : c + 1, :]
        gaps.append(gap)
        loss = loss + gap * gap
    loss_ref[...] = 0.5 * loss
    pull = gaps[0] * colors[0] + gaps[1] * colors[1] + gaps[2] * colors[2]
    behind = weight * pull
    tau_grad = pull * passed * kept - (running_sum_back(behind) - behind)
    raw_ref[0] = (tau_grad * reach * slope).astype(BF16).astype(F32)
    for c in range(3):
        raw_ref[1 + c] = (
            (weight * gaps[c] * (colors[c] * (1.0 - colors[c]))).astype(BF16).astype(F32)
        )

    def put(i, total):
        hots, rows = [], []
        for half in range(2):
            hot, masks = one_sample_row(cell_ref, rank_ref, image, 2 * i + half, owners)
            cots = [raw_ref[c, pl.ds(2 * i + half, 1), :] for c in range(4)]
            hots.append(hot)
            rows.append(
                jnp.concatenate(
                    [
                        jnp.where(masks[q], cots[c], 0.0)
                        for q in range(THIRDS * 2 + 2)
                        for c in range(4)
                    ],
                    axis=0,
                ).astype(BF16)
            )
        return total + mul(
            jnp.concatenate(rows, axis=1), jnp.concatenate(hots, axis=1), NT
        )

    placed = lax.fori_loop(
        0, SAMPLES // 2, put, jnp.zeros((512, owners), F32), unroll=4
    )
    for j in range(THIRDS):
        lines_ref[:, j, :] = placed[j * 128 : (j + 1) * 128].T
    image_sums = placed[384:512]
    sums_parts = three_parts(image_sums)
    sums_wide = jnp.concatenate(sums_parts, axis=1)
    sums_flip = jnp.concatenate(three_parts(image_sums.T), axis=1)
    table_grad = jnp.zeros((IMAGES_DEV, CODE_WIDTH), F32)
    for j in range(4):
        lines_ref[:, 3 + j, :] = mul(sums_flip, jnp.concatenate([code_blocks[j]] * 3, axis=0))
        product = mul(sums_wide, jnp.concatenate([queries[j]] * 3, axis=0))
        low = 2 * j * IMAGES_DEV
        table_grad = table_grad + product[low : low + IMAGES_DEV, :CODE_WIDTH]
        table_grad = table_grad + product[low + IMAGES_DEV : low + 2 * IMAGES_DEV, CODE_WIDTH:]
    lines_ref[:, 7, :] = jnp.zeros((owners, 128), F32)
    out_ref[...] = lines_ref[...].astype(BF16)
    new_code, new_first, new_second = adam_update(
        code_ref[...], table_grad, first_ref[...], second_ref[...]
    )
    new_code_ref[...] = new_code
    new_first_ref[...] = new_first
    new_second_ref[...] = new_second


def backward_kernel(
    h,
    order_ref,
    x_ref,
    acts_ref,
    cot_in_ref,
    weights_ref,
    own_ref,
    first_ref,
    second_ref,
    third_ref,
    total_ref,
    cot_ref,
):
    third = pl.program_id(0)
    groups = cot_ref.shape[0]
    rows = x_ref.shape[0]

    @pl.when(third == 0)
    def _():
        cot_ref[...] = cot_in_ref[...].astype(F32)
        total_ref[...] = jnp.zeros_like(total_ref)
        lines = []
        for c in range(4):
            sums = jnp.sum(cot_ref[:, 3 + h * 2 + c // 2, :], axis=0, keepdims=True)
            start = (c % 2) * CODE_WIDTH
            line = sums[:, start : start + CODE_WIDTH]
            lines.append(
                jnp.concatenate([line, jnp.zeros((1, NET_WIDTH - CODE_WIDTH), F32)], axis=1)
            )
        total_ref[HEAD_ROW:PARAM_ROWS, :] = jnp.concatenate(
            [jnp.zeros((4, NET_WIDTH), F32)] + lines + [jnp.zeros((8, NET_WIDTH), F32)], axis=0
        )

    cot = jnp.where(
        third == 0, cot_ref[:, 0, :], jnp.where(third == 1, cot_ref[:, 1, :], cot_ref[:, 2, :])
    )
    sums = jnp.sum(cot, axis=0, keepdims=True)
    spread = jnp.broadcast_to(cot[:, None, :], (groups, DEPTH, 128)).reshape(rows, 128)
    spread = jnp.where(depth_match(rows), spread, 0.0).astype(BF16)
    lane = iota((1, 128), 1)
    wide_lane = iota((1, NET_WIDTH), 1)
    head = weights_ref[0, HEAD_ROW:PARAM_ROWS, :].astype(F32)
    outer = mul(spread, acts_ref[LAYERS - 1], TN)[h * 64 : (h + 1) * 64]
    head_grad = jnp.sum(outer.reshape(4, DEPTH, NET_WIDTH), axis=1)
    bias_head = jnp.zeros((1, NET_WIDTH), F32)
    for c in range(4):
        value = jnp.sum(jnp.where((lane >> 4) == h * 4 + c, sums, 0.0), axis=1, keepdims=True)
        bias_head = bias_head + jnp.where(wide_lane == c, value, 0.0)
    up = mul(spread, head_tile(head, h))
    bias_lines = [None] * LAYERS
    for k in reversed(range(LAYERS)):
        pre_grad = jnp.where(acts_ref[k].astype(F32) > 0, up, 0.0).astype(BF16)
        bias_lines[k] = jnp.sum(pre_grad.astype(F32), axis=0, keepdims=True)
        if k > 0:
            start = ENC_WIDTH + (k - 1) * NET_WIDTH
            total_ref[start : start + NET_WIDTH, :] += mul(acts_ref[k - 1], pre_grad, TN)
            up = mul(pre_grad, weights_ref[0, start : start + NET_WIDTH, :], NT)
        else:
            total_ref[0:ENC_WIDTH, :] += mul(x_ref[...], pre_grad, TN)[
                h * ENC_WIDTH : (h + 1) * ENC_WIDTH
            ]
    total_ref[HEAD_ROW:PARAM_ROWS, :] += jnp.concatenate(
        [head_grad, jnp.zeros((4, NET_WIDTH), F32), bias_head]
        + bias_lines
        + [jnp.zeros((3, NET_WIDTH), F32)],
        axis=0,
    )

    @pl.when(third == THIRDS - 1)
    def _():
        quarter = own_ref.shape[0]
        for k, share_ref in enumerate((own_ref, first_ref, second_ref, third_ref)):
            start = pl.multiple_of(order_ref[k] * quarter, 8)
            share_ref[...] = total_ref[pl.ds(start, quarter), :].astype(share_ref.dtype)


def adam_kernel(
    order_ref,
    own_ref,
    first_ref,
    second_ref,
    third_ref,
    param_ref,
    one_ref,
    two_ref,
    *refs,
):
    step = pl.program_id(0)
    new_param_ref, new_one_ref, new_two_ref = refs[-3:]
    for k, share_ref in enumerate((own_ref, first_ref, second_ref, third_ref)):

        @pl.when(step == k)
        def _():
            new_param, new_one, new_two = adam_update(
                param_ref[0], share_ref[...].astype(F32), one_ref[0], two_ref[0]
            )
            new_param_ref[0] = new_param
            new_one_ref[0] = new_one
            new_two_ref[0] = new_two


def cost(micros):
    return pl.CostEstimate(
        flops=int(micros * 1e9), bytes_accessed=int(micros * 3e6), transcendentals=0
    )


def limits(mib=48):
    return pltpu.CompilerParams(vmem_limit_bytes=mib * 1024 * 1024)


def shape_of(dims, kind):
    return jax.ShapeDtypeStruct(dims, kind)


def shards(
    features,
    spacing,
    targets,
    ray_length,
    cell_id,
    slot_rank,
    image_id,
    params,
    first_moment,
    second_moment,
    code_table,
    table_first,
    table_second,
):
    groups = lax.axis_size("expert")
    places = groups * DEPTH
    cell_rows = cell_id.T
    rank_rows = slot_rank.T
    outgoing = pl.pallas_call(
        dispatch_kernel,
        out_shape=shape_of((places, THIRDS * 128), BF16),
        in_specs=[pl.BlockSpec(memory_space=pl.ANY)] * 3,
        scratch_shapes=[
            pltpu.VMEM((places, SAMPLES * RAYS), BF16),
            pltpu.VMEM((THIRDS * 128, SAMPLES * RAYS), BF16),
            pltpu.VMEM((SAMPLES, ENC_WIDTH, RAYS), BF16),
            pltpu.VMEM((SAMPLES, RAYS), jnp.int32),
            pltpu.VMEM((SAMPLES, RAYS), jnp.int32),
            pltpu.SemaphoreType.DMA((3,)),
        ],
        compiler_params=limits(59),
        name="dispatch",
    )(jnp.transpose(features, (1, 2, 0)), cell_rows, rank_rows)
    arrived = lax.all_to_all(outgoing, "expert", split_axis=0, concat_axis=0, tiled=True)

    slots = THIRDS * places
    vmem = pl.BlockSpec(memory_space=pltpu.VMEM)
    anywhere = pl.BlockSpec(memory_space=pl.ANY)
    acts_shape = shape_of((LAYERS, slots, NET_WIDTH), BF16)
    *acts, raw_out, weights = pl.pallas_call(
        forward_kernel,
        out_shape=[
            acts_shape,
            acts_shape,
            shape_of((groups, 8, 128), BF16),
            shape_of((2, PARAM_ROWS, NET_WIDTH), BF16),
        ],
        out_specs=[anywhere, anywhere, vmem, vmem],
        scratch_shapes=[
            pltpu.VMEM((groups, 8, 128), F32),
            pltpu.VMEM((2 * LAYERS, slots, NET_WIDTH), BF16),
            pltpu.SemaphoreType.DMA((2 * LAYERS,)),
        ],
        compiler_params=limits(48),
        name="forward",
    )(arrived, params)
    returned = lax.all_to_all(raw_out, "expert", split_axis=0, concat_axis=0, tiled=True)

    table_shape = shape_of(code_table.shape, F32)
    cot_out, loss, new_table, new_table_first, new_table_second = pl.pallas_call(
        ray_kernel,
        out_shape=[
            shape_of((groups, 8, 128), BF16),
            shape_of((1, RAYS), F32),
            table_shape,
            table_shape,
            table_shape,
        ],
        scratch_shapes=[
            pltpu.VMEM((512, PARTS * groups), BF16),
            pltpu.VMEM((4, SAMPLES, RAYS), F32),
            pltpu.VMEM((groups, 8, 128), F32),
        ],
        compiler_params=limits(16),
        name="rays",
    )(
        returned,
        cell_rows,
        rank_rows,
        image_id.reshape(1, RAYS),
        ray_length.reshape(1, RAYS),
        spacing.T,
        targets,
        code_table,
        table_first,
        table_second,
    )
    cot_in = lax.all_to_all(cot_out, "expert", split_axis=0, concat_axis=0, tiled=True)

    copies = lax.axis_size("dp")
    quarter = -(-PARAM_ROWS // (8 * copies)) * 8
    turns = jnp.arange(copies, dtype=jnp.int32)
    position = lax.axis_index("dp")
    lent = lambda *dims: pl.BlockSpec(dims, lambda i, order: (0,) * len(dims))

    def send(value, distance):
        return lax.ppermute(value, "dp", [(i, (i + distance) % copies) for i in range(copies)])

    def gradient(h):
        return pl.pallas_call(
            functools.partial(backward_kernel, h),
            grid_spec=pltpu.PrefetchScalarGridSpec(
                num_scalar_prefetch=1,
                grid=(THIRDS,),
                in_specs=[
                    pl.BlockSpec((places, 128), lambda i, order: (0, i)),
                    pl.BlockSpec((LAYERS, places, NET_WIDTH), lambda i, order: (0, i, 0)),
                    lent(groups, 8, 128),
                    pl.BlockSpec((1, PARAM_ROWS, NET_WIDTH), lambda i, order: (h, 0, 0)),
                ],
                out_specs=[lent(quarter, NET_WIDTH)] * 4,
                scratch_shapes=[
                    pltpu.VMEM((copies * quarter, NET_WIDTH), F32),
                    pltpu.VMEM((groups, 8, 128), F32),
                ],
            ),
            out_shape=[shape_of((quarter, NET_WIDTH), F32)]
            + [shape_of((quarter, NET_WIDTH), BF16)] * 3,
            compiler_params=limits(48),
            cost_estimate=cost(6.0),
            name="backward",
        )((position + turns) % copies, arrived, acts[h], cot_in, weights)

    def collect(shares):
        share = shares[0]
        for k in (2, 1, 3):
            share = share + send(shares[k], k).astype(F32)
        share = share.astype(BF16)
        behind, ahead = send(share, 1), send(share, 3)
        return share, behind, send(ahead, 3), ahead

    def update(h, pieces, earlier):
        block = pl.BlockSpec((1, quarter, NET_WIDTH), lambda i, order: (h, order[i], 0))
        return pl.pallas_call(
            adam_kernel,
            grid_spec=pltpu.PrefetchScalarGridSpec(
                num_scalar_prefetch=1,
                grid=(copies,),
                in_specs=[lent(quarter, NET_WIDTH)] * 4
                + [block] * 3
                + [pl.BlockSpec(memory_space=pl.ANY)] * len(earlier),
                out_specs=[block] * 3,
            ),
            out_shape=[shape_of(params.shape, F32)] * 3,
            input_output_aliases={8 + i: i for i in range(len(earlier))},
            compiler_params=limits(12),
            cost_estimate=cost(2.0),
            name="adam",
        )(
            (position - turns) % copies,
            *pieces,
            params,
            first_moment,
            second_moment,
            *earlier,
        )

    pieces = [collect(gradient(h)) for h in range(2)]
    updated = update(0, pieces[0], ())
    new_params, new_first, new_second = update(1, pieces[1], updated)
    return (
        loss.reshape(RAYS),
        new_params,
        new_first,
        new_second,
        new_table,
        new_table_first,
        new_table_second,
    )


def solution(mesh):
    rays = ("expert", "dp")
    table = P(rays, None)
    block = P("expert", None, None)
    return jax.shard_map(
        shards,
        mesh=mesh,
        in_specs=(
            P(rays, None, None),
            P(rays, None),
            P(None, rays),
            P(rays),
            P(rays, None),
            P(rays, None),
            P(rays),
            block,
            block,
            block,
            table,
            table,
            table,
        ),
        out_specs=(P(rays), block, block, block, table, table, table),
        check_vma=False,
    )
```

```python
import functools

import jax
import jax.numpy as jnp
from jax import lax
from jax.experimental import pallas as pl
from jax.experimental.pallas import tpu as pltpu
from jax.sharding import PartitionSpec as P

NET_WIDTH = 256
CODE_WIDTH = 64
ENC_WIDTH = 64
LAYERS = 4
SAMPLES = 32
RAYS = 128
IMAGES_DEV = 16
CAPACITY = 48
DEPTH = 16
THIRDS = CAPACITY // DEPTH
PARTS = 2
HEAD_ROW = ENC_WIDTH + (LAYERS - 1) * NET_WIDTH
PARAM_ROWS = HEAD_ROW + 16

F32 = jnp.float32
BF16 = jnp.bfloat16

BETA_ONE = 0.9
BETA_TWO = 0.999
LEARN_RATE = 0.001
ADAM_EPS = 1e-08
CORRECT_ONE = 1.0 - 0.9**10
CORRECT_TWO = 1.0 - 0.999**10

NN = (((1,), (0,)), ((), ()))
NT = (((1,), (1,)), ((), ()))
TN = (((0,), (0,)), ((), ()))


def mul(left, right, dims=NN):
    return lax.dot_general(left, right, dims, preferred_element_type=F32)


def iota(shape, dim):
    return lax.broadcasted_iota(jnp.int32, shape, dim)


def three_parts(value):
    high = value.astype(BF16)
    rest = value - high.astype(F32)
    middle = rest.astype(BF16)
    low = (rest - middle.astype(F32)).astype(BF16)
    return [high, middle, low]


def adam_update(param_now, gradient, moment_one, moment_two):
    new_one = BETA_ONE * moment_one + (1.0 - BETA_ONE) * gradient
    new_two = BETA_TWO * moment_two + (1.0 - BETA_TWO) * gradient * gradient
    update = LEARN_RATE * (new_one / CORRECT_ONE) / (jnp.sqrt(new_two / CORRECT_TWO) + ADAM_EPS)
    return (param_now - update, new_one, new_two)


def dispatch_kernel(
    feat_in, cell_in, rank_in, out_ref, hot_ref, rows_ref, feat_ref, cell_ref, rank_ref, sems
):
    places = out_ref.shape[0]
    moves = [
        pltpu.make_async_copy(source, target, sems.at[i])
        for i, (source, target) in enumerate(
            ((cell_in, cell_ref), (rank_in, rank_ref), (feat_in, feat_ref))
        )
    ]
    for move in moves:
        move.start()
    for move in moves:
        move.wait()
    for i in range(SAMPLES):
        cell = cell_ref[i : i + 1, :]
        rank = rank_ref[i : i + 1, :]
        place = jnp.where(rank >= 0, (cell >> 1) * DEPTH + (rank & (DEPTH - 1)), -1)
        inner = (rank >> 4) * 2 + (cell & 1)
        span = slice(i * RAYS, (i + 1) * RAYS)
        hot_ref[:, span] = jnp.where(iota((places, RAYS), 0) == place, 1.0, 0.0).astype(BF16)
        feat = feat_ref[i].astype(F32)
        for q in range(THIRDS * 2):
            rows_ref[q * ENC_WIDTH : (q + 1) * ENC_WIDTH, span] = jnp.where(
                inner == q, feat, 0.0
            ).astype(BF16)
    out_ref[...] = mul(hot_ref[...], rows_ref[...], NT).astype(BF16)


def depth_match(rows):
    return (iota((rows, 128), 0) & (DEPTH - 1)) == (iota((rows, 128), 1) & (DEPTH - 1))


def first_matrix(weights_ref, held):
    matrix = weights_ref[held, 0:ENC_WIDTH, :]
    blank = jnp.zeros_like(matrix)
    return jnp.concatenate([matrix, blank] if held == 0 else [blank, matrix], axis=0)


def hidden_matrix(weights_ref, held, layer):
    start = ENC_WIDTH + (layer - 1) * NET_WIDTH
    return weights_ref[held, start : start + NET_WIDTH, :]


def head_tile(head, held):
    rows = jnp.concatenate(
        [jnp.broadcast_to(head[c : c + 1, :], (DEPTH, NET_WIDTH)) for c in range(4)], axis=0
    )
    blank = jnp.zeros_like(rows)
    return jnp.concatenate([rows, blank] if held == 0 else [blank, rows], axis=0).astype(BF16)


def slot_rows(x_ref):
    return jnp.concatenate([x_ref[:, j * 128 : (j + 1) * 128] for j in range(THIRDS)], axis=0)


def forward_kernel(
    x_ref, params_ref, acts0_ref, acts1_ref, out_ref, weights_ref, lines_ref, held_ref, sems
):
    groups = out_ref.shape[0]
    rows = held_ref.shape[1]
    moves = []
    weights_ref[...] = params_ref[...].astype(BF16)
    heads = [weights_ref[h, HEAD_ROW:PARAM_ROWS, :].astype(F32) for h in range(2)]
    for j in range(4):
        h, c = j // 2, (j % 2) * 2
        pair = jnp.concatenate(
            [heads[h][4 + c : 5 + c, :CODE_WIDTH], heads[h][5 + c : 6 + c, :CODE_WIDTH]], axis=1
        )
        lines_ref[:, 3 + j, :] = jnp.broadcast_to(pair, (groups, 128))
    lane = iota((1, 128), 1)
    shift = jnp.zeros((1, 128), F32)
    total = jnp.zeros((rows, 128), F32)
    for h, acts_ref in enumerate((acts0_ref, acts1_ref)):
        current = slot_rows(x_ref)
        for k in range(LAYERS):
            matrix = first_matrix(weights_ref, h) if k == 0 else hidden_matrix(weights_ref, h, k)
            preact = mul(current, matrix) + heads[h][9 + k : 10 + k, :]
            current = jnp.maximum(preact, 0.0).astype(BF16)
            place = h * LAYERS + k
            held_ref[place] = current
            move = pltpu.make_async_copy(held_ref.at[place], acts_ref.at[k], sems.at[place])
            move.start()
            moves.append(move)
        total = total + mul(current, head_tile(heads[h], h), NT)
        for c in range(4):
            shift = shift + jnp.where((lane >> 4) == h * 4 + c, heads[h][8:9, c : c + 1], 0.0)
    total = jnp.where(depth_match(rows), total + shift, 0.0)
    raw = jnp.sum(total.reshape(THIRDS * groups, DEPTH, 128), axis=1)
    low = raw - raw.astype(BF16).astype(F32)
    density = []
    for j in range(THIRDS):
        span = slice(j * groups, (j + 1) * groups)
        lines_ref[:, j, :] = raw[span]
        density += [low[span, 0:DEPTH], low[span, 64 : 64 + DEPTH]]
    lines_ref[:, 7, :] = jnp.concatenate(density + [jnp.zeros((groups, 32), F32)], axis=1)
    out_ref[...] = lines_ref[...].astype(BF16)
    for move in moves:
        move.wait()


def one_sample_row(cell_ref, rank_ref, image, i, owners):
    cell = cell_ref[pl.ds(i, 1), :]
    rank = rank_ref[pl.ds(i, 1), :]
    live = rank >= 0
    owner = jnp.where(live, cell >> 1, -1)
    hot = jnp.where(iota((owners, RAYS), 0) == owner, 1.0, 0.0).astype(BF16)
    held = cell & 1
    slot = jnp.where(live, ((rank >> 4) * 2 + held) * DEPTH + (rank & (DEPTH - 1)), -1)
    code = jnp.where(live, held * IMAGES_DEV + image, -1)
    slot_mask = iota((THIRDS * 2 * DEPTH, RAYS), 0) == slot
    code_mask = iota((2 * IMAGES_DEV, RAYS), 0) == code
    masks = [slot_mask[q * DEPTH : (q + 1) * DEPTH] for q in range(THIRDS * 2)]
    masks += [code_mask[h * IMAGES_DEV : (h + 1) * IMAGES_DEV] for h in range(2)]
    return hot, masks


def running_sum(value):
    step = 1
    while step < SAMPLES:
        value = value + jnp.concatenate(
            [jnp.zeros((step, RAYS), F32), value[: SAMPLES - step]], axis=0
        )
        step *= 2
    return value


def running_sum_back(value):
    step = 1
    while step < SAMPLES:
        value = value + jnp.concatenate([value[step:], jnp.zeros((step, RAYS), F32)], axis=0)
        step *= 2
    return value


def ray_kernel(
    back_ref,
    cell_ref,
    rank_ref,
    image_ref,
    length_ref,
    spacing_ref,
    targets_ref,
    code_ref,
    first_ref,
    second_ref,
    out_ref,
    loss_ref,
    new_code_ref,
    new_first_ref,
    new_second_ref,
    table_ref,
    raw_ref,
    lines_ref,
):
    owners = back_ref.shape[0]
    image = image_ref[...] & (IMAGES_DEV - 1)
    code = code_ref[...].astype(BF16).astype(F32)
    tile = jnp.concatenate([code] * 8, axis=0)
    tile = jnp.concatenate([tile, tile], axis=1)
    block_row = iota((128, 128), 0) >> 4
    block_lane = iota((128, 128), 1) >> 6
    code_blocks = [
        jnp.where(block_row == 2 * j + block_lane, tile, 0.0).astype(BF16) for j in range(4)
    ]
    lines_ref[...] = back_ref[...].astype(F32)
    queries = [lines_ref[:, 3 + j, :].astype(BF16) for j in range(4)]
    code_part = mul(queries[0], code_blocks[0], NT)
    for j in range(1, 4):
        code_part = code_part + mul(queries[j], code_blocks[j], NT)
    code_parts = three_parts(code_part.T)
    lows = lines_ref[:, 7, :]
    blank = jnp.zeros((owners, 64 - DEPTH), F32)
    highs, rests = [], []
    for j in range(THIRDS):
        start = j * 2 * DEPTH
        rest = [lows[:, start : start + DEPTH], blank]
        rest += [lows[:, start + DEPTH : start + 2 * DEPTH], blank]
        highs.append(lines_ref[:, j, :].T.astype(BF16))
        rests.append(jnp.concatenate(rest, axis=1).T.astype(BF16))
    table_ref[...] = jnp.concatenate(
        [
            jnp.concatenate(highs + code_parts[0:1], axis=0),
            jnp.concatenate(rests + code_parts[1:2], axis=0),
        ],
        axis=1,
    )

    def pick(i, carry):
        sides = [one_sample_row(cell_ref, rank_ref, image, 2 * i + half, owners) for half in range(2)]
        hots = jnp.concatenate([side[0] for side in sides], axis=1)
        found = mul(table_ref[...], jnp.concatenate([hots] * PARTS, axis=0))
        for half in range(2):
            masks = sides[half][1]
            for c in range(4):
                total = jnp.zeros((DEPTH, RAYS), F32)
                for q in range(THIRDS * 2 + 2):
                    start = q * 64 + c * DEPTH
                    total = total + jnp.where(
                        masks[q], found[start : start + DEPTH, half * RAYS : (half + 1) * RAYS], 0.0
                    )
                raw_ref[c, pl.ds(2 * i + half, 1), :] = jnp.sum(total, axis=0, keepdims=True)
        return carry

    lax.fori_loop(0, SAMPLES // 2, pick, 0, unroll=4)

    spacing = spacing_ref[...]
    live = jnp.where(iota((SAMPLES, RAYS), 0) < length_ref[...], 1.0, 0.0)
    raw_density = raw_ref[0]
    small = jnp.exp(-jnp.abs(raw_density))
    density = jnp.maximum(raw_density, 0.0) + jnp.log1p(small)
    slope = jnp.where(raw_density >= 0, 1.0, small) / (1.0 + small)
    colors = []
    for c in range(3):
        raw_color = raw_ref[1 + c]
        tail = jnp.exp(-jnp.abs(raw_color))
        colors.append(jnp.where(raw_color >= 0, 1.0, tail) / (1.0 + tail))
    reach = spacing * live
    tau = density * reach
    before = running_sum(tau) - tau
    passed = jnp.exp(-before)
    kept = jnp.exp(-tau)
    weight = passed * (1.0 - kept)
    gaps = []
    loss = jnp.zeros((1, RAYS), F32)
    for c in range(3):
        gap = jnp.sum(weight * colors[c], axis=0, keepdims=True) - targets_ref[c : c + 1, :]
        gaps.append(gap)
        loss = loss + gap * gap
    loss_ref[...] = 0.5 * loss
    pull = gaps[0] * colors[0] + gaps[1] * colors[1] + gaps[2] * colors[2]
    behind = weight * pull
    tau_grad = pull * passed * kept - (running_sum_back(behind) - behind)
    raw_ref[0] = (tau_grad * reach * slope).astype(BF16).astype(F32)
    for c in range(3):
        raw_ref[1 + c] = (
            (weight * gaps[c] * (colors[c] * (1.0 - colors[c]))).astype(BF16).astype(F32)
        )

    def put(i, total):
        hots, rows = [], []
        for half in range(2):
            hot, masks = one_sample_row(cell_ref, rank_ref, image, 2 * i + half, owners)
            cots = [raw_ref[c, pl.ds(2 * i + half, 1), :] for c in range(4)]
            hots.append(hot)
            rows.append(
                jnp.concatenate(
                    [
                        jnp.where(masks[q], cots[c], 0.0)
                        for q in range(THIRDS * 2 + 2)
                        for c in range(4)
                    ],
                    axis=0,
                ).astype(BF16)
            )
        return total + mul(
            jnp.concatenate(rows, axis=1), jnp.concatenate(hots, axis=1), NT
        )

    placed = lax.fori_loop(
        0, SAMPLES // 2, put, jnp.zeros((512, owners), F32), unroll=4
    )
    for j in range(THIRDS):
        lines_ref[:, j, :] = placed[j * 128 : (j + 1) * 128].T
    image_sums = placed[384:512]
    sums_parts = three_parts(image_sums)
    sums_wide = jnp.concatenate(sums_parts, axis=1)
    sums_flip = jnp.concatenate(three_parts(image_sums.T), axis=1)
    table_grad = jnp.zeros((IMAGES_DEV, CODE_WIDTH), F32)
    for j in range(4):
        lines_ref[:, 3 + j, :] = mul(sums_flip, jnp.concatenate([code_blocks[j]] * 3, axis=0))
        product = mul(sums_wide, jnp.concatenate([queries[j]] * 3, axis=0))
        low = 2 * j * IMAGES_DEV
        table_grad = table_grad + product[low : low + IMAGES_DEV, :CODE_WIDTH]
        table_grad = table_grad + product[low + IMAGES_DEV : low + 2 * IMAGES_DEV, CODE_WIDTH:]
    lines_ref[:, 7, :] = jnp.zeros((owners, 128), F32)
    out_ref[...] = lines_ref[...].astype(BF16)
    new_code, new_first, new_second = adam_update(
        code_ref[...], table_grad, first_ref[...], second_ref[...]
    )
    new_code_ref[...] = new_code
    new_first_ref[...] = new_first
    new_second_ref[...] = new_second


def backward_kernel(
    h,
    order_ref,
    x_ref,
    acts_in,
    cot_in_ref,
    weights_ref,
    own_ref,
    first_ref,
    second_ref,
    third_ref,
    total_ref,
    cot_ref,
    acts_ref,
    sems,
):
    third = pl.program_id(0)
    groups = cot_ref.shape[0]
    rows = x_ref.shape[0]

    def move(j, k):
        source = acts_in.at[k, pl.ds(j * rows, rows), :]
        return pltpu.make_async_copy(source, acts_ref.at[j, k], sems.at[j, k])

    @pl.when(third == 0)
    def _():
        for j in range(THIRDS):
            for k in reversed(range(LAYERS)):
                move(j, k).start()
        cot_ref[...] = cot_in_ref[...].astype(F32)
        total_ref[...] = jnp.zeros_like(total_ref)
        lines = []
        for c in range(4):
            sums = jnp.sum(cot_ref[:, 3 + h * 2 + c // 2, :], axis=0, keepdims=True)
            start = (c % 2) * CODE_WIDTH
            line = sums[:, start : start + CODE_WIDTH]
            lines.append(
                jnp.concatenate([line, jnp.zeros((1, NET_WIDTH - CODE_WIDTH), F32)], axis=1)
            )
        total_ref[HEAD_ROW:PARAM_ROWS, :] = jnp.concatenate(
            [jnp.zeros((4, NET_WIDTH), F32)] + lines + [jnp.zeros((8, NET_WIDTH), F32)], axis=0
        )

    cot = jnp.where(
        third == 0, cot_ref[:, 0, :], jnp.where(third == 1, cot_ref[:, 1, :], cot_ref[:, 2, :])
    )
    sums = jnp.sum(cot, axis=0, keepdims=True)
    spread = jnp.broadcast_to(cot[:, None, :], (groups, DEPTH, 128)).reshape(rows, 128)
    spread = jnp.where(depth_match(rows), spread, 0.0).astype(BF16)
    lane = iota((1, 128), 1)
    wide_lane = iota((1, NET_WIDTH), 1)
    head = weights_ref[0, HEAD_ROW:PARAM_ROWS, :].astype(F32)
    move(third, LAYERS - 1).wait()
    outer = mul(spread, acts_ref[third, LAYERS - 1], TN)[h * 64 : (h + 1) * 64]
    head_grad = jnp.sum(outer.reshape(4, DEPTH, NET_WIDTH), axis=1)
    bias_head = jnp.zeros((1, NET_WIDTH), F32)
    for c in range(4):
        value = jnp.sum(jnp.where((lane >> 4) == h * 4 + c, sums, 0.0), axis=1, keepdims=True)
        bias_head = bias_head + jnp.where(wide_lane == c, value, 0.0)
    up = mul(spread, head_tile(head, h))
    bias_lines = [None] * LAYERS
    for k in reversed(range(LAYERS)):
        pre_grad = jnp.where(acts_ref[third, k].astype(F32) > 0, up, 0.0).astype(BF16)
        bias_lines[k] = jnp.sum(pre_grad.astype(F32), axis=0, keepdims=True)
        if k > 0:
            start = ENC_WIDTH + (k - 1) * NET_WIDTH
            up = mul(pre_grad, weights_ref[0, start : start + NET_WIDTH, :], NT)
            move(third, k - 1).wait()
            total_ref[start : start + NET_WIDTH, :] += mul(
                acts_ref[third, k - 1], pre_grad, TN
            )
        else:
            total_ref[0:ENC_WIDTH, :] += mul(x_ref[...], pre_grad, TN)[
                h * ENC_WIDTH : (h + 1) * ENC_WIDTH
            ]
    total_ref[HEAD_ROW:PARAM_ROWS, :] += jnp.concatenate(
        [head_grad, jnp.zeros((4, NET_WIDTH), F32), bias_head]
        + bias_lines
        + [jnp.zeros((3, NET_WIDTH), F32)],
        axis=0,
    )

    @pl.when(third == THIRDS - 1)
    def _():
        quarter = own_ref.shape[0]
        for k, share_ref in enumerate((own_ref, first_ref, second_ref, third_ref)):
            start = pl.multiple_of(order_ref[k] * quarter, 8)
            share_ref[...] = total_ref[pl.ds(start, quarter), :].astype(share_ref.dtype)


def adam_kernel(h, order_ref, own_ref, first_ref, second_ref, third_ref, *refs):
    olds, outs = refs[:3], refs[-8:-5]
    grad_ref, *new_refs = refs[-5:-1]
    sems = refs[-1]
    quarter = own_ref.shape[0]
    for k, share_ref in enumerate((own_ref, first_ref, second_ref, third_ref)):
        start = pl.multiple_of(order_ref[k] * quarter, 8)
        grad_ref[pl.ds(start, quarter), :] = share_ref[...].astype(F32)
    moves = []
    size = PARAM_ROWS // 2
    for part in range(2):
        span = slice(part * size, (part + 1) * size)
        values = adam_update(
            olds[0][h, span, :], grad_ref[span, :], olds[1][h, span, :], olds[2][h, span, :]
        )
        for i in range(3):
            new_refs[i][span, :] = values[i]
            move = pltpu.make_async_copy(
                new_refs[i].at[span], outs[i].at[h, span], sems.at[i, part]
            )
            move.start()
            moves.append(move)
    for move in moves:
        move.wait()


def cost(micros):
    return pl.CostEstimate(
        flops=int(micros * 1e9), bytes_accessed=int(micros * 3e6), transcendentals=0
    )


def limits(mib=48):
    return pltpu.CompilerParams(vmem_limit_bytes=mib * 1024 * 1024)


def shape_of(dims, kind):
    return jax.ShapeDtypeStruct(dims, kind)


def shards(
    features,
    spacing,
    targets,
    ray_length,
    cell_id,
    slot_rank,
    image_id,
    params,
    first_moment,
    second_moment,
    code_table,
    table_first,
    table_second,
):
    groups = lax.axis_size("expert")
    places = groups * DEPTH
    cell_rows = cell_id.T
    rank_rows = slot_rank.T
    outgoing = pl.pallas_call(
        dispatch_kernel,
        out_shape=shape_of((places, THIRDS * 128), BF16),
        in_specs=[pl.BlockSpec(memory_space=pl.ANY)] * 3,
        scratch_shapes=[
            pltpu.VMEM((places, SAMPLES * RAYS), BF16),
            pltpu.VMEM((THIRDS * 128, SAMPLES * RAYS), BF16),
            pltpu.VMEM((SAMPLES, ENC_WIDTH, RAYS), BF16),
            pltpu.VMEM((SAMPLES, RAYS), jnp.int32),
            pltpu.VMEM((SAMPLES, RAYS), jnp.int32),
            pltpu.SemaphoreType.DMA((3,)),
        ],
        compiler_params=limits(59),
        name="dispatch",
    )(jnp.transpose(features, (1, 2, 0)), cell_rows, rank_rows)
    arrived = lax.all_to_all(outgoing, "expert", split_axis=0, concat_axis=0, tiled=True)

    slots = THIRDS * places
    vmem = pl.BlockSpec(memory_space=pltpu.VMEM)
    anywhere = pl.BlockSpec(memory_space=pl.ANY)
    acts_shape = shape_of((LAYERS, slots, NET_WIDTH), BF16)
    *acts, raw_out, weights = pl.pallas_call(
        forward_kernel,
        out_shape=[
            acts_shape,
            acts_shape,
            shape_of((groups, 8, 128), BF16),
            shape_of((2, PARAM_ROWS, NET_WIDTH), BF16),
        ],
        out_specs=[anywhere, anywhere, vmem, vmem],
        scratch_shapes=[
            pltpu.VMEM((groups, 8, 128), F32),
            pltpu.VMEM((2 * LAYERS, slots, NET_WIDTH), BF16),
            pltpu.SemaphoreType.DMA((2 * LAYERS,)),
        ],
        compiler_params=limits(48),
        name="forward",
    )(arrived, params)
    returned = lax.all_to_all(raw_out, "expert", split_axis=0, concat_axis=0, tiled=True)

    table_shape = shape_of(code_table.shape, F32)
    cot_out, loss, new_table, new_table_first, new_table_second = pl.pallas_call(
        ray_kernel,
        out_shape=[
            shape_of((groups, 8, 128), BF16),
            shape_of((1, RAYS), F32),
            table_shape,
            table_shape,
            table_shape,
        ],
        scratch_shapes=[
            pltpu.VMEM((512, PARTS * groups), BF16),
            pltpu.VMEM((4, SAMPLES, RAYS), F32),
            pltpu.VMEM((groups, 8, 128), F32),
        ],
        compiler_params=limits(16),
        name="rays",
    )(
        returned,
        cell_rows,
        rank_rows,
        image_id.reshape(1, RAYS),
        ray_length.reshape(1, RAYS),
        spacing.T,
        targets,
        code_table,
        table_first,
        table_second,
    )
    cot_in = lax.all_to_all(cot_out, "expert", split_axis=0, concat_axis=0, tiled=True)

    copies = lax.axis_size("dp")
    quarter = -(-PARAM_ROWS // (8 * copies)) * 8
    turns = jnp.arange(copies, dtype=jnp.int32)
    position = lax.axis_index("dp")
    lent = lambda *dims: pl.BlockSpec(dims, lambda i, order: (0,) * len(dims))

    def send(value, distance):
        return lax.ppermute(value, "dp", [(i, (i + distance) % copies) for i in range(copies)])

    def gradient(h):
        return pl.pallas_call(
            functools.partial(backward_kernel, h),
            grid_spec=pltpu.PrefetchScalarGridSpec(
                num_scalar_prefetch=1,
                grid=(THIRDS,),
                in_specs=[
                    pl.BlockSpec((places, 128), lambda i, order: (0, i)),
                    anywhere,
                    lent(groups, 8, 128),
                    pl.BlockSpec((1, PARAM_ROWS, NET_WIDTH), lambda i, order: (h, 0, 0)),
                ],
                out_specs=[lent(quarter, NET_WIDTH)] * 4,
                scratch_shapes=[
                    pltpu.VMEM((copies * quarter, NET_WIDTH), F32),
                    pltpu.VMEM((groups, 8, 128), F32),
                    pltpu.VMEM((THIRDS, LAYERS, places, NET_WIDTH), BF16),
                    pltpu.SemaphoreType.DMA((THIRDS, LAYERS)),
                ],
            ),
            out_shape=[shape_of((quarter, NET_WIDTH), F32)]
            + [shape_of((quarter, NET_WIDTH), BF16)] * 3,
            compiler_params=limits(48),
            cost_estimate=cost(6.0),
            name="backward",
        )((position + turns) % copies, arrived, acts[h], cot_in, weights)

    def collect(shares):
        share = shares[0]
        for k in (2, 1, 3):
            share = share + send(shares[k], k).astype(F32)
        share = share.astype(BF16)
        behind, ahead = send(share, 1), send(share, 3)
        return share, behind, send(ahead, 3), ahead

    def update(h, pieces, earlier):
        return pl.pallas_call(
            functools.partial(adam_kernel, h),
            in_specs=[pl.BlockSpec(memory_space=pltpu.SMEM)]
            + [vmem] * 7
            + [anywhere] * len(earlier),
            out_specs=[anywhere] * 3,
            out_shape=[shape_of(params.shape, F32)] * 3,
            scratch_shapes=[pltpu.VMEM((copies * quarter, NET_WIDTH), F32)]
            + [pltpu.VMEM((PARAM_ROWS, NET_WIDTH), F32)] * 3
            + [pltpu.SemaphoreType.DMA((3, 2))],
            input_output_aliases={8 + i: i for i in range(len(earlier))},
            compiler_params=limits(12),
            cost_estimate=cost(2.0),
            name="adam",
        )(
            (position - turns) % copies,
            *pieces,
            params,
            first_moment,
            second_moment,
            *earlier,
        )

    pieces = [collect(gradient(h)) for h in range(2)]
    updated = update(0, pieces[0], ())
    new_params, new_first, new_second = update(1, pieces[1], updated)
    return (
        loss.reshape(RAYS),
        new_params,
        new_first,
        new_second,
        new_table,
        new_table_first,
        new_table_second,
    )


def solution(mesh):
    rays = ("expert", "dp")
    table = P(rays, None)
    block = P("expert", None, None)
    return jax.shard_map(
        shards,
        mesh=mesh,
        in_specs=(
            P(rays, None, None),
            P(rays, None),
            P(None, rays),
            P(rays),
            P(rays, None),
            P(rays, None),
            P(rays),
            block,
            block,
            block,
            table,
            table,
            table,
        ),
        out_specs=(P(rays), block, block, block, table, table, table),
        check_vma=False,
    )
```

```python
import functools

import jax
import jax.numpy as jnp
from jax import lax
from jax.experimental import pallas as pl
from jax.experimental.pallas import tpu as pltpu
from jax.sharding import PartitionSpec as P

NET_WIDTH = 256
CODE_WIDTH = 64
ENC_WIDTH = 64
LAYERS = 4
SAMPLES = 32
RAYS = 128
IMAGES_DEV = 16
CAPACITY = 48
DEPTH = 16
THIRDS = CAPACITY // DEPTH
PARTS = 2
HEAD_ROW = ENC_WIDTH + (LAYERS - 1) * NET_WIDTH
PARAM_ROWS = HEAD_ROW + 16

F32 = jnp.float32
BF16 = jnp.bfloat16

BETA_ONE = 0.9
BETA_TWO = 0.999
LEARN_RATE = 0.001
ADAM_EPS = 1e-08
CORRECT_ONE = 1.0 - 0.9**10
CORRECT_TWO = 1.0 - 0.999**10

NN = (((1,), (0,)), ((), ()))
NT = (((1,), (1,)), ((), ()))
TN = (((0,), (0,)), ((), ()))


def mul(left, right, dims=NN):
    return lax.dot_general(left, right, dims, preferred_element_type=F32)


def iota(shape, dim):
    return lax.broadcasted_iota(jnp.int32, shape, dim)


def three_parts(value):
    high = value.astype(BF16)
    rest = value - high.astype(F32)
    middle = rest.astype(BF16)
    low = (rest - middle.astype(F32)).astype(BF16)
    return [high, middle, low]


def adam_update(param_now, gradient, moment_one, moment_two):
    new_one = BETA_ONE * moment_one + (1.0 - BETA_ONE) * gradient
    new_two = BETA_TWO * moment_two + (1.0 - BETA_TWO) * gradient * gradient
    update = LEARN_RATE * (new_one / CORRECT_ONE) / (jnp.sqrt(new_two / CORRECT_TWO) + ADAM_EPS)
    return (param_now - update, new_one, new_two)


def dispatch_kernel(
    feat_in, cell_in, rank_in, out_ref, hot_ref, rows_ref, feat_ref, cell_ref, rank_ref, sems
):
    places = out_ref.shape[0]
    moves = [
        pltpu.make_async_copy(source, target, sems.at[i])
        for i, (source, target) in enumerate(
            ((cell_in, cell_ref), (rank_in, rank_ref), (feat_in, feat_ref))
        )
    ]
    for move in moves:
        move.start()
    for move in moves:
        move.wait()
    for i in range(SAMPLES):
        cell = cell_ref[i : i + 1, :]
        rank = rank_ref[i : i + 1, :]
        place = jnp.where(rank >= 0, (cell >> 1) * DEPTH + (rank & (DEPTH - 1)), -1)
        inner = (rank >> 4) * 2 + (cell & 1)
        span = slice(i * RAYS, (i + 1) * RAYS)
        hot_ref[:, span] = jnp.where(iota((places, RAYS), 0) == place, 1.0, 0.0).astype(BF16)
        feat = feat_ref[i].astype(F32)
        for q in range(THIRDS * 2):
            rows_ref[q * ENC_WIDTH : (q + 1) * ENC_WIDTH, span] = jnp.where(
                inner == q, feat, 0.0
            ).astype(BF16)
    out_ref[...] = mul(hot_ref[...], rows_ref[...], NT).astype(BF16)


def depth_match(rows):
    return (iota((rows, 128), 0) & (DEPTH - 1)) == (iota((rows, 128), 1) & (DEPTH - 1))


def first_matrix(weights_ref, held):
    matrix = weights_ref[held, 0:ENC_WIDTH, :]
    blank = jnp.zeros_like(matrix)
    return jnp.concatenate([matrix, blank] if held == 0 else [blank, matrix], axis=0)


def hidden_matrix(weights_ref, held, layer):
    start = ENC_WIDTH + (layer - 1) * NET_WIDTH
    return weights_ref[held, start : start + NET_WIDTH, :]


def head_tile(head, held):
    rows = jnp.concatenate(
        [jnp.broadcast_to(head[c : c + 1, :], (DEPTH, NET_WIDTH)) for c in range(4)], axis=0
    )
    blank = jnp.zeros_like(rows)
    return jnp.concatenate([rows, blank] if held == 0 else [blank, rows], axis=0).astype(BF16)


def slot_rows(x_ref):
    return jnp.concatenate([x_ref[:, j * 128 : (j + 1) * 128] for j in range(THIRDS)], axis=0)


def forward_kernel(
    x_ref, params_ref, acts0_ref, acts1_ref, out_ref, weights_ref, lines_ref, held_ref, sems
):
    groups = out_ref.shape[0]
    rows = held_ref.shape[1]
    moves = []
    weights_ref[...] = params_ref[...].astype(BF16)
    heads = [weights_ref[h, HEAD_ROW:PARAM_ROWS, :].astype(F32) for h in range(2)]
    for j in range(4):
        h, c = j // 2, (j % 2) * 2
        pair = jnp.concatenate(
            [heads[h][4 + c : 5 + c, :CODE_WIDTH], heads[h][5 + c : 6 + c, :CODE_WIDTH]], axis=1
        )
        lines_ref[:, 3 + j, :] = jnp.broadcast_to(pair, (groups, 128))
    lane = iota((1, 128), 1)
    shift = jnp.zeros((1, 128), F32)
    total = jnp.zeros((rows, 128), F32)
    for h, acts_ref in enumerate((acts0_ref, acts1_ref)):
        current = slot_rows(x_ref)
        for k in range(LAYERS):
            matrix = first_matrix(weights_ref, h) if k == 0 else hidden_matrix(weights_ref, h, k)
            preact = mul(current, matrix) + heads[h][9 + k : 10 + k, :]
            current = jnp.maximum(preact, 0.0).astype(BF16)
            place = h * LAYERS + k
            held_ref[place] = current
            move = pltpu.make_async_copy(held_ref.at[place], acts_ref.at[k], sems.at[place])
            move.start()
            moves.append(move)
        total = total + mul(current, head_tile(heads[h], h), NT)
        for c in range(4):
            shift = shift + jnp.where((lane >> 4) == h * 4 + c, heads[h][8:9, c : c + 1], 0.0)
    total = jnp.where(depth_match(rows), total + shift, 0.0)
    raw = jnp.sum(total.reshape(THIRDS * groups, DEPTH, 128), axis=1)
    low = raw - raw.astype(BF16).astype(F32)
    density = []
    for j in range(THIRDS):
        span = slice(j * groups, (j + 1) * groups)
        lines_ref[:, j, :] = raw[span]
        density += [low[span, 0:DEPTH], low[span, 64 : 64 + DEPTH]]
    lines_ref[:, 7, :] = jnp.concatenate(density + [jnp.zeros((groups, 32), F32)], axis=1)
    out_ref[...] = lines_ref[...].astype(BF16)
    for move in moves:
        move.wait()


def one_sample_row(cell_ref, rank_ref, image, i, owners):
    cell = cell_ref[pl.ds(i, 1), :]
    rank = rank_ref[pl.ds(i, 1), :]
    live = rank >= 0
    owner = jnp.where(live, cell >> 1, -1)
    hot = jnp.where(iota((owners, RAYS), 0) == owner, 1.0, 0.0).astype(BF16)
    held = cell & 1
    slot = jnp.where(live, ((rank >> 4) * 2 + held) * DEPTH + (rank & (DEPTH - 1)), -1)
    code = jnp.where(live, held * IMAGES_DEV + image, -1)
    slot_mask = iota((THIRDS * 2 * DEPTH, RAYS), 0) == slot
    code_mask = iota((2 * IMAGES_DEV, RAYS), 0) == code
    masks = [slot_mask[q * DEPTH : (q + 1) * DEPTH] for q in range(THIRDS * 2)]
    masks += [code_mask[h * IMAGES_DEV : (h + 1) * IMAGES_DEV] for h in range(2)]
    return hot, masks


def running_sum(value):
    step = 1
    while step < SAMPLES:
        value = value + jnp.concatenate(
            [jnp.zeros((step, RAYS), F32), value[: SAMPLES - step]], axis=0
        )
        step *= 2
    return value


def running_sum_back(value):
    step = 1
    while step < SAMPLES:
        value = value + jnp.concatenate([value[step:], jnp.zeros((step, RAYS), F32)], axis=0)
        step *= 2
    return value


def ray_kernel(
    back_ref,
    cell_ref,
    rank_ref,
    image_ref,
    length_ref,
    spacing_ref,
    targets_ref,
    code_ref,
    first_ref,
    second_ref,
    out_ref,
    loss_ref,
    new_code_ref,
    new_first_ref,
    new_second_ref,
    table_ref,
    raw_ref,
    lines_ref,
):
    owners = back_ref.shape[0]
    image = image_ref[...] & (IMAGES_DEV - 1)
    code = code_ref[...].astype(BF16).astype(F32)
    tile = jnp.concatenate([code] * 8, axis=0)
    tile = jnp.concatenate([tile, tile], axis=1)
    block_row = iota((128, 128), 0) >> 4
    block_lane = iota((128, 128), 1) >> 6
    code_blocks = [
        jnp.where(block_row == 2 * j + block_lane, tile, 0.0).astype(BF16) for j in range(4)
    ]
    lines_ref[...] = back_ref[...].astype(F32)
    queries = [lines_ref[:, 3 + j, :].astype(BF16) for j in range(4)]
    code_part = mul(queries[0], code_blocks[0], NT)
    for j in range(1, 4):
        code_part = code_part + mul(queries[j], code_blocks[j], NT)
    code_parts = three_parts(code_part.T)
    lows = lines_ref[:, 7, :]
    blank = jnp.zeros((owners, 64 - DEPTH), F32)
    highs, rests = [], []
    for j in range(THIRDS):
        start = j * 2 * DEPTH
        rest = [lows[:, start : start + DEPTH], blank]
        rest += [lows[:, start + DEPTH : start + 2 * DEPTH], blank]
        highs.append(lines_ref[:, j, :].T.astype(BF16))
        rests.append(jnp.concatenate(rest, axis=1).T.astype(BF16))
    table_ref[...] = jnp.concatenate(
        [
            jnp.concatenate(highs + code_parts[0:1], axis=0),
            jnp.concatenate(rests + code_parts[1:2], axis=0),
        ],
        axis=1,
    )

    def pick(i, carry):
        sides = [one_sample_row(cell_ref, rank_ref, image, 2 * i + half, owners) for half in range(2)]
        hots = jnp.concatenate([side[0] for side in sides], axis=1)
        found = mul(table_ref[...], jnp.concatenate([hots] * PARTS, axis=0))
        for half in range(2):
            masks = sides[half][1]
            for c in range(4):
                total = jnp.zeros((DEPTH, RAYS), F32)
                for q in range(THIRDS * 2 + 2):
                    start = q * 64 + c * DEPTH
                    total = total + jnp.where(
                        masks[q], found[start : start + DEPTH, half * RAYS : (half + 1) * RAYS], 0.0
                    )
                raw_ref[c, pl.ds(2 * i + half, 1), :] = jnp.sum(total, axis=0, keepdims=True)
        return carry

    lax.fori_loop(0, SAMPLES // 2, pick, 0, unroll=4)

    spacing = spacing_ref[...]
    live = jnp.where(iota((SAMPLES, RAYS), 0) < length_ref[...], 1.0, 0.0)
    raw_density = raw_ref[0]
    small = jnp.exp(-jnp.abs(raw_density))
    density = jnp.maximum(raw_density, 0.0) + jnp.log1p(small)
    slope = jnp.where(raw_density >= 0, 1.0, small) / (1.0 + small)
    colors = []
    for c in range(3):
        raw_color = raw_ref[1 + c]
        tail = jnp.exp(-jnp.abs(raw_color))
        colors.append(jnp.where(raw_color >= 0, 1.0, tail) / (1.0 + tail))
    reach = spacing * live
    tau = density * reach
    before = running_sum(tau) - tau
    passed = jnp.exp(-before)
    kept = jnp.exp(-tau)
    weight = passed * (1.0 - kept)
    gaps = []
    loss = jnp.zeros((1, RAYS), F32)
    for c in range(3):
        gap = jnp.sum(weight * colors[c], axis=0, keepdims=True) - targets_ref[c : c + 1, :]
        gaps.append(gap)
        loss = loss + gap * gap
    loss_ref[...] = 0.5 * loss
    pull = gaps[0] * colors[0] + gaps[1] * colors[1] + gaps[2] * colors[2]
    behind = weight * pull
    tau_grad = pull * passed * kept - (running_sum_back(behind) - behind)
    raw_ref[0] = (tau_grad * reach * slope).astype(BF16).astype(F32)
    for c in range(3):
        raw_ref[1 + c] = (
            (weight * gaps[c] * (colors[c] * (1.0 - colors[c]))).astype(BF16).astype(F32)
        )

    def put(i, total):
        hots, rows = [], []
        for half in range(2):
            hot, masks = one_sample_row(cell_ref, rank_ref, image, 2 * i + half, owners)
            cots = [raw_ref[c, pl.ds(2 * i + half, 1), :] for c in range(4)]
            hots.append(hot)
            rows.append(
                jnp.concatenate(
                    [
                        jnp.where(masks[q], cots[c], 0.0)
                        for q in range(THIRDS * 2 + 2)
                        for c in range(4)
                    ],
                    axis=0,
                ).astype(BF16)
            )
        return total + mul(
            jnp.concatenate(rows, axis=1), jnp.concatenate(hots, axis=1), NT
        )

    placed = lax.fori_loop(
        0, SAMPLES // 2, put, jnp.zeros((512, owners), F32), unroll=4
    )
    for j in range(THIRDS):
        lines_ref[:, j, :] = placed[j * 128 : (j + 1) * 128].T
    image_sums = placed[384:512]
    sums_parts = three_parts(image_sums)
    sums_wide = jnp.concatenate(sums_parts, axis=1)
    sums_flip = jnp.concatenate(three_parts(image_sums.T), axis=1)
    table_grad = jnp.zeros((IMAGES_DEV, CODE_WIDTH), F32)
    for j in range(4):
        lines_ref[:, 3 + j, :] = mul(sums_flip, jnp.concatenate([code_blocks[j]] * 3, axis=0))
        product = mul(sums_wide, jnp.concatenate([queries[j]] * 3, axis=0))
        low = 2 * j * IMAGES_DEV
        table_grad = table_grad + product[low : low + IMAGES_DEV, :CODE_WIDTH]
        table_grad = table_grad + product[low + IMAGES_DEV : low + 2 * IMAGES_DEV, CODE_WIDTH:]
    lines_ref[:, 7, :] = jnp.zeros((owners, 128), F32)
    out_ref[...] = lines_ref[...].astype(BF16)
    new_code, new_first, new_second = adam_update(
        code_ref[...], table_grad, first_ref[...], second_ref[...]
    )
    new_code_ref[...] = new_code
    new_first_ref[...] = new_first
    new_second_ref[...] = new_second


def backward_kernel(
    h,
    order_ref,
    x_ref,
    acts_ref,
    cot_in_ref,
    weights_ref,
    own_ref,
    first_ref,
    second_ref,
    third_ref,
    total_ref,
    cot_ref,
):
    third = pl.program_id(0)
    groups = cot_ref.shape[0]
    rows = x_ref.shape[0]

    @pl.when(third == 0)
    def _():
        cot_ref[...] = cot_in_ref[...].astype(F32)
        total_ref[...] = jnp.zeros_like(total_ref)
        lines = []
        for c in range(4):
            sums = jnp.sum(cot_ref[:, 3 + h * 2 + c // 2, :], axis=0, keepdims=True)
            start = (c % 2) * CODE_WIDTH
            line = sums[:, start : start + CODE_WIDTH]
            lines.append(
                jnp.concatenate([line, jnp.zeros((1, NET_WIDTH - CODE_WIDTH), F32)], axis=1)
            )
        total_ref[HEAD_ROW:PARAM_ROWS, :] = jnp.concatenate(
            [jnp.zeros((4, NET_WIDTH), F32)] + lines + [jnp.zeros((8, NET_WIDTH), F32)], axis=0
        )

    cot = jnp.where(
        third == 0, cot_ref[:, 0, :], jnp.where(third == 1, cot_ref[:, 1, :], cot_ref[:, 2, :])
    )
    sums = jnp.sum(cot, axis=0, keepdims=True)
    spread = jnp.broadcast_to(cot[:, None, :], (groups, DEPTH, 128)).reshape(rows, 128)
    spread = jnp.where(depth_match(rows), spread, 0.0).astype(BF16)
    lane = iota((1, 128), 1)
    wide_lane = iota((1, NET_WIDTH), 1)
    head = weights_ref[0, HEAD_ROW:PARAM_ROWS, :].astype(F32)
    outer = mul(spread, acts_ref[LAYERS - 1], TN)[h * 64 : (h + 1) * 64]
    head_grad = jnp.sum(outer.reshape(4, DEPTH, NET_WIDTH), axis=1)
    bias_head = jnp.zeros((1, NET_WIDTH), F32)
    for c in range(4):
        value = jnp.sum(jnp.where((lane >> 4) == h * 4 + c, sums, 0.0), axis=1, keepdims=True)
        bias_head = bias_head + jnp.where(wide_lane == c, value, 0.0)
    up = mul(spread, head_tile(head, h))
    bias_lines = [None] * LAYERS
    for k in reversed(range(LAYERS)):
        pre_grad = jnp.where(acts_ref[k].astype(F32) > 0, up, 0.0).astype(BF16)
        bias_lines[k] = jnp.sum(pre_grad.astype(F32), axis=0, keepdims=True)
        if k > 0:
            start = ENC_WIDTH + (k - 1) * NET_WIDTH
            total_ref[start : start + NET_WIDTH, :] += mul(acts_ref[k - 1], pre_grad, TN)
            up = mul(pre_grad, weights_ref[0, start : start + NET_WIDTH, :], NT)
        else:
            total_ref[0:ENC_WIDTH, :] += mul(x_ref[...], pre_grad, TN)[
                h * ENC_WIDTH : (h + 1) * ENC_WIDTH
            ]
    total_ref[HEAD_ROW:PARAM_ROWS, :] += jnp.concatenate(
        [head_grad, jnp.zeros((4, NET_WIDTH), F32), bias_head]
        + bias_lines
        + [jnp.zeros((3, NET_WIDTH), F32)],
        axis=0,
    )

    @pl.when(third == THIRDS - 1)
    def _():
        quarter = own_ref.shape[0]
        for k, share_ref in enumerate((own_ref, first_ref, second_ref, third_ref)):
            start = pl.multiple_of(order_ref[k] * quarter, 8)
            share_ref[...] = total_ref[pl.ds(start, quarter), :].astype(share_ref.dtype)


def adam_kernel(count, order_ref, *refs):
    step = pl.program_id(0)
    param_ref, one_ref, two_ref = refs[count : count + 3]
    new_param_ref, new_one_ref, new_two_ref = refs[-3:]
    for k in range(count):

        @pl.when(step == k)
        def _():
            new_param, new_one, new_two = adam_update(
                param_ref[0], refs[k][...].astype(F32), one_ref[0], two_ref[0]
            )
            new_param_ref[0] = new_param
            new_one_ref[0] = new_one
            new_two_ref[0] = new_two


def cost(micros):
    return pl.CostEstimate(
        flops=int(micros * 1e9), bytes_accessed=int(micros * 3e6), transcendentals=0
    )


def limits(mib=48):
    return pltpu.CompilerParams(vmem_limit_bytes=mib * 1024 * 1024)


def shape_of(dims, kind):
    return jax.ShapeDtypeStruct(dims, kind)


def shards(
    features,
    spacing,
    targets,
    ray_length,
    cell_id,
    slot_rank,
    image_id,
    params,
    first_moment,
    second_moment,
    code_table,
    table_first,
    table_second,
):
    groups = lax.axis_size("expert")
    places = groups * DEPTH
    cell_rows = cell_id.T
    rank_rows = slot_rank.T
    outgoing = pl.pallas_call(
        dispatch_kernel,
        out_shape=shape_of((places, THIRDS * 128), BF16),
        in_specs=[pl.BlockSpec(memory_space=pl.ANY)] * 3,
        scratch_shapes=[
            pltpu.VMEM((places, SAMPLES * RAYS), BF16),
            pltpu.VMEM((THIRDS * 128, SAMPLES * RAYS), BF16),
            pltpu.VMEM((SAMPLES, ENC_WIDTH, RAYS), BF16),
            pltpu.VMEM((SAMPLES, RAYS), jnp.int32),
            pltpu.VMEM((SAMPLES, RAYS), jnp.int32),
            pltpu.SemaphoreType.DMA((3,)),
        ],
        compiler_params=limits(59),
        name="dispatch",
    )(jnp.transpose(features, (1, 2, 0)), cell_rows, rank_rows)
    arrived = lax.all_to_all(outgoing, "expert", split_axis=0, concat_axis=0, tiled=True)

    slots = THIRDS * places
    vmem = pl.BlockSpec(memory_space=pltpu.VMEM)
    anywhere = pl.BlockSpec(memory_space=pl.ANY)
    acts_shape = shape_of((LAYERS, slots, NET_WIDTH), BF16)
    *acts, raw_out, weights = pl.pallas_call(
        forward_kernel,
        out_shape=[
            acts_shape,
            acts_shape,
            shape_of((groups, 8, 128), BF16),
            shape_of((2, PARAM_ROWS, NET_WIDTH), BF16),
        ],
        out_specs=[anywhere, anywhere, vmem, vmem],
        scratch_shapes=[
            pltpu.VMEM((groups, 8, 128), F32),
            pltpu.VMEM((2 * LAYERS, slots, NET_WIDTH), BF16),
            pltpu.SemaphoreType.DMA((2 * LAYERS,)),
        ],
        compiler_params=limits(48),
        name="forward",
    )(arrived, params)
    returned = lax.all_to_all(raw_out, "expert", split_axis=0, concat_axis=0, tiled=True)

    table_shape = shape_of(code_table.shape, F32)
    cot_out, loss, new_table, new_table_first, new_table_second = pl.pallas_call(
        ray_kernel,
        out_shape=[
            shape_of((groups, 8, 128), BF16),
            shape_of((1, RAYS), F32),
            table_shape,
            table_shape,
            table_shape,
        ],
        scratch_shapes=[
            pltpu.VMEM((512, PARTS * groups), BF16),
            pltpu.VMEM((4, SAMPLES, RAYS), F32),
            pltpu.VMEM((groups, 8, 128), F32),
        ],
        compiler_params=limits(16),
        name="rays",
    )(
        returned,
        cell_rows,
        rank_rows,
        image_id.reshape(1, RAYS),
        ray_length.reshape(1, RAYS),
        spacing.T,
        targets,
        code_table,
        table_first,
        table_second,
    )
    cot_in = lax.all_to_all(cot_out, "expert", split_axis=0, concat_axis=0, tiled=True)

    copies = lax.axis_size("dp")
    quarter = -(-PARAM_ROWS // (8 * copies)) * 8
    turns = jnp.arange(copies, dtype=jnp.int32)
    position = lax.axis_index("dp")
    lent = lambda *dims: pl.BlockSpec(dims, lambda i, order: (0,) * len(dims))

    def send(value, distance):
        return lax.ppermute(value, "dp", [(i, (i + distance) % copies) for i in range(copies)])

    def gradient(h):
        return pl.pallas_call(
            functools.partial(backward_kernel, h),
            grid_spec=pltpu.PrefetchScalarGridSpec(
                num_scalar_prefetch=1,
                grid=(THIRDS,),
                in_specs=[
                    pl.BlockSpec((places, 128), lambda i, order: (0, i)),
                    pl.BlockSpec((LAYERS, places, NET_WIDTH), lambda i, order: (0, i, 0)),
                    lent(groups, 8, 128),
                    pl.BlockSpec((1, PARAM_ROWS, NET_WIDTH), lambda i, order: (h, 0, 0)),
                ],
                out_specs=[lent(quarter, NET_WIDTH)] * 4,
                scratch_shapes=[
                    pltpu.VMEM((copies * quarter, NET_WIDTH), F32),
                    pltpu.VMEM((groups, 8, 128), F32),
                ],
            ),
            out_shape=[shape_of((quarter, NET_WIDTH), F32)]
            + [shape_of((quarter, NET_WIDTH), BF16)] * 3,
            compiler_params=limits(48),
            cost_estimate=cost(6.0),
            name="backward",
        )((position + turns) % copies, arrived, acts[h], cot_in, weights)

    def collect(shares):
        share = shares[0]
        for k in (2, 1, 3):
            share = share + send(shares[k], k).astype(F32)
        share = share.astype(BF16)
        behind, ahead = send(share, 1), send(share, 3)
        return share, behind, ahead, send(ahead, 3)

    def update(pieces, turns, micros, earlier):
        count, each = len(pieces), len(turns)
        block = pl.BlockSpec(
            (1, quarter, NET_WIDTH), lambda i, order: (i // each, order[i % each], 0)
        )
        return pl.pallas_call(
            functools.partial(adam_kernel, count),
            grid_spec=pltpu.PrefetchScalarGridSpec(
                num_scalar_prefetch=1,
                grid=(count,),
                in_specs=[lent(quarter, NET_WIDTH)] * count
                + [block] * 3
                + [anywhere] * len(earlier),
                out_specs=[block] * 3,
            ),
            out_shape=[shape_of(params.shape, F32)] * 3,
            input_output_aliases={count + 4 + i: i for i in range(len(earlier))},
            compiler_params=limits(58),
            cost_estimate=cost(micros),
            name="adam",
        )(
            (position + jnp.array(turns, jnp.int32)) % copies,
            *pieces,
            params,
            first_moment,
            second_moment,
            *earlier,
        )

    pieces = [collect(gradient(h)) for h in range(2)]
    near = pieces[0][:3] + pieces[1][:3]
    updated = update(near, (0, copies - 1, 1), 4.0, ())
    new_params, new_first, new_second = update(
        (pieces[0][3], pieces[1][3]), (2,), 1.5, updated
    )
    return (
        loss.reshape(RAYS),
        new_params,
        new_first,
        new_second,
        new_table,
        new_table_first,
        new_table_second,
    )


def solution(mesh):
    rays = ("expert", "dp")
    table = P(rays, None)
    block = P("expert", None, None)
    return jax.shard_map(
        shards,
        mesh=mesh,
        in_specs=(
            P(rays, None, None),
            P(rays, None),
            P(None, rays),
            P(rays),
            P(rays, None),
            P(rays, None),
            P(rays),
            block,
            block,
            block,
            table,
            table,
            table,
        ),
        out_specs=(P(rays), block, block, block, table, table, table),
        check_vma=False,
    )
```

```python
import functools

import jax
import jax.numpy as jnp
from jax import lax
from jax.experimental import pallas as pl
from jax.experimental.pallas import tpu as pltpu
from jax.sharding import PartitionSpec as P

NET_WIDTH = 256
CODE_WIDTH = 64
ENC_WIDTH = 64
LAYERS = 4
SAMPLES = 32
RAYS = 128
IMAGES_DEV = 16
CAPACITY = 48
DEPTH = 16
THIRDS = CAPACITY // DEPTH
PARTS = 2
HEAD_ROW = ENC_WIDTH + (LAYERS - 1) * NET_WIDTH
PARAM_ROWS = HEAD_ROW + 16

F32 = jnp.float32
BF16 = jnp.bfloat16

BETA_ONE = 0.9
BETA_TWO = 0.999
LEARN_RATE = 0.001
ADAM_EPS = 1e-08
CORRECT_ONE = 1.0 - 0.9**10
CORRECT_TWO = 1.0 - 0.999**10

NN = (((1,), (0,)), ((), ()))
NT = (((1,), (1,)), ((), ()))
TN = (((0,), (0,)), ((), ()))


def mul(left, right, dims=NN):
    return lax.dot_general(left, right, dims, preferred_element_type=F32)


def iota(shape, dim):
    return lax.broadcasted_iota(jnp.int32, shape, dim)


def three_parts(value):
    high = value.astype(BF16)
    rest = value - high.astype(F32)
    middle = rest.astype(BF16)
    low = (rest - middle.astype(F32)).astype(BF16)
    return [high, middle, low]


def adam_update(param_now, gradient, moment_one, moment_two):
    new_one = BETA_ONE * moment_one + (1.0 - BETA_ONE) * gradient
    new_two = BETA_TWO * moment_two + (1.0 - BETA_TWO) * gradient * gradient
    update = LEARN_RATE * (new_one / CORRECT_ONE) / (jnp.sqrt(new_two / CORRECT_TWO) + ADAM_EPS)
    return (param_now - update, new_one, new_two)


def dispatch_kernel(
    feat_in, cell_in, rank_in, out_ref, hot_ref, rows_ref, feat_ref, cell_ref, rank_ref, sems
):
    places = out_ref.shape[0]
    moves = [
        pltpu.make_async_copy(source, target, sems.at[i])
        for i, (source, target) in enumerate(
            ((cell_in, cell_ref), (rank_in, rank_ref), (feat_in, feat_ref))
        )
    ]
    for move in moves:
        move.start()
    for move in moves:
        move.wait()
    for i in range(SAMPLES):
        cell = cell_ref[i : i + 1, :]
        rank = rank_ref[i : i + 1, :]
        place = jnp.where(rank >= 0, (cell >> 1) * DEPTH + (rank & (DEPTH - 1)), -1)
        inner = (rank >> 4) * 2 + (cell & 1)
        span = slice(i * RAYS, (i + 1) * RAYS)
        hot_ref[:, span] = jnp.where(iota((places, RAYS), 0) == place, 1.0, 0.0).astype(BF16)
        feat = feat_ref[i].astype(F32)
        for q in range(THIRDS * 2):
            rows_ref[q * ENC_WIDTH : (q + 1) * ENC_WIDTH, span] = jnp.where(
                inner == q, feat, 0.0
            ).astype(BF16)
    out_ref[...] = mul(hot_ref[...], rows_ref[...], NT).astype(BF16)


def depth_match(rows):
    return (iota((rows, 128), 0) & (DEPTH - 1)) == (iota((rows, 128), 1) & (DEPTH - 1))


def first_matrix(weights_ref, held):
    matrix = weights_ref[held, 0:ENC_WIDTH, :]
    blank = jnp.zeros_like(matrix)
    return jnp.concatenate([matrix, blank] if held == 0 else [blank, matrix], axis=0)


def hidden_matrix(weights_ref, held, layer):
    start = ENC_WIDTH + (layer - 1) * NET_WIDTH
    return weights_ref[held, start : start + NET_WIDTH, :]


def head_tile(head, held):
    rows = jnp.concatenate(
        [jnp.broadcast_to(head[c : c + 1, :], (DEPTH, NET_WIDTH)) for c in range(4)], axis=0
    )
    blank = jnp.zeros_like(rows)
    return jnp.concatenate([rows, blank] if held == 0 else [blank, rows], axis=0).astype(BF16)


def slot_rows(x_ref):
    return jnp.concatenate([x_ref[:, j * 128 : (j + 1) * 128] for j in range(THIRDS)], axis=0)


def forward_kernel(
    x_ref, params_ref, acts0_ref, acts1_ref, out_ref, weights_ref, lines_ref, held_ref, sems
):
    groups = out_ref.shape[0]
    rows = held_ref.shape[1]
    moves = []
    weights_ref[...] = params_ref[...].astype(BF16)
    heads = [weights_ref[h, HEAD_ROW:PARAM_ROWS, :].astype(F32) for h in range(2)]
    for j in range(4):
        h, c = j // 2, (j % 2) * 2
        pair = jnp.concatenate(
            [heads[h][4 + c : 5 + c, :CODE_WIDTH], heads[h][5 + c : 6 + c, :CODE_WIDTH]], axis=1
        )
        lines_ref[:, 3 + j, :] = jnp.broadcast_to(pair, (groups, 128))
    lane = iota((1, 128), 1)
    shift = jnp.zeros((1, 128), F32)
    total = jnp.zeros((rows, 128), F32)
    for h, acts_ref in enumerate((acts0_ref, acts1_ref)):
        current = slot_rows(x_ref)
        for k in range(LAYERS):
            matrix = first_matrix(weights_ref, h) if k == 0 else hidden_matrix(weights_ref, h, k)
            preact = mul(current, matrix) + heads[h][9 + k : 10 + k, :]
            current = jnp.maximum(preact, 0.0).astype(BF16)
            place = h * LAYERS + k
            held_ref[place] = current
            move = pltpu.make_async_copy(held_ref.at[place], acts_ref.at[k], sems.at[place])
            move.start()
            moves.append(move)
        total = total + mul(current, head_tile(heads[h], h), NT)
        for c in range(4):
            shift = shift + jnp.where((lane >> 4) == h * 4 + c, heads[h][8:9, c : c + 1], 0.0)
    total = jnp.where(depth_match(rows), total + shift, 0.0)
    raw = jnp.sum(total.reshape(THIRDS * groups, DEPTH, 128), axis=1)
    low = raw - raw.astype(BF16).astype(F32)
    density = []
    for j in range(THIRDS):
        span = slice(j * groups, (j + 1) * groups)
        lines_ref[:, j, :] = raw[span]
        density += [low[span, 0:DEPTH], low[span, 64 : 64 + DEPTH]]
    lines_ref[:, 7, :] = jnp.concatenate(density + [jnp.zeros((groups, 32), F32)], axis=1)
    out_ref[...] = lines_ref[...].astype(BF16)
    for move in moves:
        move.wait()


def one_sample_row(cell_ref, rank_ref, image, i, owners):
    cell = cell_ref[pl.ds(i, 1), :]
    rank = rank_ref[pl.ds(i, 1), :]
    live = rank >= 0
    owner = jnp.where(live, cell >> 1, -1)
    hot = jnp.where(iota((owners, RAYS), 0) == owner, 1.0, 0.0).astype(BF16)
    held = cell & 1
    slot = jnp.where(live, ((rank >> 4) * 2 + held) * DEPTH + (rank & (DEPTH - 1)), -1)
    code = jnp.where(live, held * IMAGES_DEV + image, -1)
    slot_mask = iota((THIRDS * 2 * DEPTH, RAYS), 0) == slot
    code_mask = iota((2 * IMAGES_DEV, RAYS), 0) == code
    masks = [slot_mask[q * DEPTH : (q + 1) * DEPTH] for q in range(THIRDS * 2)]
    masks += [code_mask[h * IMAGES_DEV : (h + 1) * IMAGES_DEV] for h in range(2)]
    return hot, masks


def running_sum(value):
    step = 1
    while step < SAMPLES:
        value = value + jnp.concatenate(
            [jnp.zeros((step, RAYS), F32), value[: SAMPLES - step]], axis=0
        )
        step *= 2
    return value


def running_sum_back(value):
    step = 1
    while step < SAMPLES:
        value = value + jnp.concatenate([value[step:], jnp.zeros((step, RAYS), F32)], axis=0)
        step *= 2
    return value


def ray_kernel(
    back_ref,
    cell_ref,
    rank_ref,
    image_ref,
    length_ref,
    spacing_ref,
    targets_ref,
    code_ref,
    first_ref,
    second_ref,
    out_ref,
    loss_ref,
    new_code_ref,
    new_first_ref,
    new_second_ref,
    table_ref,
    raw_ref,
    lines_ref,
):
    owners = back_ref.shape[0]
    image = image_ref[...] & (IMAGES_DEV - 1)
    code = code_ref[...].astype(BF16).astype(F32)
    tile = jnp.concatenate([code] * 8, axis=0)
    tile = jnp.concatenate([tile, tile], axis=1)
    block_row = iota((128, 128), 0) >> 4
    block_lane = iota((128, 128), 1) >> 6
    code_blocks = [
        jnp.where(block_row == 2 * j + block_lane, tile, 0.0).astype(BF16) for j in range(4)
    ]
    lines_ref[...] = back_ref[...].astype(F32)
    queries = [lines_ref[:, 3 + j, :].astype(BF16) for j in range(4)]
    code_part = mul(queries[0], code_blocks[0], NT)
    for j in range(1, 4):
        code_part = code_part + mul(queries[j], code_blocks[j], NT)
    code_parts = three_parts(code_part.T)
    lows = lines_ref[:, 7, :]
    blank = jnp.zeros((owners, 64 - DEPTH), F32)
    highs, rests = [], []
    for j in range(THIRDS):
        start = j * 2 * DEPTH
        rest = [lows[:, start : start + DEPTH], blank]
        rest += [lows[:, start + DEPTH : start + 2 * DEPTH], blank]
        highs.append(lines_ref[:, j, :].T.astype(BF16))
        rests.append(jnp.concatenate(rest, axis=1).T.astype(BF16))
    table_ref[...] = jnp.concatenate(
        [
            jnp.concatenate(highs + code_parts[0:1], axis=0),
            jnp.concatenate(rests + code_parts[1:2], axis=0),
        ],
        axis=1,
    )

    def pick(i, carry):
        sides = [one_sample_row(cell_ref, rank_ref, image, 2 * i + half, owners) for half in range(2)]
        hots = jnp.concatenate([side[0] for side in sides], axis=1)
        found = mul(table_ref[...], jnp.concatenate([hots] * PARTS, axis=0))
        for half in range(2):
            masks = sides[half][1]
            for c in range(4):
                total = jnp.zeros((DEPTH, RAYS), F32)
                for q in range(THIRDS * 2 + 2):
                    start = q * 64 + c * DEPTH
                    total = total + jnp.where(
                        masks[q], found[start : start + DEPTH, half * RAYS : (half + 1) * RAYS], 0.0
                    )
                raw_ref[c, pl.ds(2 * i + half, 1), :] = jnp.sum(total, axis=0, keepdims=True)
        return carry

    lax.fori_loop(0, SAMPLES // 2, pick, 0, unroll=4)

    spacing = spacing_ref[...]
    live = jnp.where(iota((SAMPLES, RAYS), 0) < length_ref[...], 1.0, 0.0)
    raw_density = raw_ref[0]
    small = jnp.exp(-jnp.abs(raw_density))
    density = jnp.maximum(raw_density, 0.0) + jnp.log1p(small)
    slope = jnp.where(raw_density >= 0, 1.0, small) / (1.0 + small)
    colors = []
    for c in range(3):
        raw_color = raw_ref[1 + c]
        tail = jnp.exp(-jnp.abs(raw_color))
        colors.append(jnp.where(raw_color >= 0, 1.0, tail) / (1.0 + tail))
    reach = spacing * live
    tau = density * reach
    before = running_sum(tau) - tau
    passed = jnp.exp(-before)
    kept = jnp.exp(-tau)
    weight = passed * (1.0 - kept)
    gaps = []
    loss = jnp.zeros((1, RAYS), F32)
    for c in range(3):
        gap = jnp.sum(weight * colors[c], axis=0, keepdims=True) - targets_ref[c : c + 1, :]
        gaps.append(gap)
        loss = loss + gap * gap
    loss_ref[...] = 0.5 * loss
    pull = gaps[0] * colors[0] + gaps[1] * colors[1] + gaps[2] * colors[2]
    behind = weight * pull
    tau_grad = pull * passed * kept - (running_sum_back(behind) - behind)
    raw_ref[0] = (tau_grad * reach * slope).astype(BF16).astype(F32)
    for c in range(3):
        raw_ref[1 + c] = (
            (weight * gaps[c] * (colors[c] * (1.0 - colors[c]))).astype(BF16).astype(F32)
        )

    def put(i, total):
        hots, rows = [], []
        for half in range(2):
            hot, masks = one_sample_row(cell_ref, rank_ref, image, 2 * i + half, owners)
            cots = [raw_ref[c, pl.ds(2 * i + half, 1), :] for c in range(4)]
            hots.append(hot)
            rows.append(
                jnp.concatenate(
                    [
                        jnp.where(masks[q], cots[c], 0.0)
                        for q in range(THIRDS * 2 + 2)
                        for c in range(4)
                    ],
                    axis=0,
                ).astype(BF16)
            )
        return total + mul(
            jnp.concatenate(rows, axis=1), jnp.concatenate(hots, axis=1), NT
        )

    placed = lax.fori_loop(
        0, SAMPLES // 2, put, jnp.zeros((512, owners), F32), unroll=4
    )
    for j in range(THIRDS):
        lines_ref[:, j, :] = placed[j * 128 : (j + 1) * 128].T
    image_sums = placed[384:512]
    sums_parts = three_parts(image_sums)
    sums_wide = jnp.concatenate(sums_parts, axis=1)
    sums_flip = jnp.concatenate(three_parts(image_sums.T), axis=1)
    table_grad = jnp.zeros((IMAGES_DEV, CODE_WIDTH), F32)
    for j in range(4):
        lines_ref[:, 3 + j, :] = mul(sums_flip, jnp.concatenate([code_blocks[j]] * 3, axis=0))
        product = mul(sums_wide, jnp.concatenate([queries[j]] * 3, axis=0))
        low = 2 * j * IMAGES_DEV
        table_grad = table_grad + product[low : low + IMAGES_DEV, :CODE_WIDTH]
        table_grad = table_grad + product[low + IMAGES_DEV : low + 2 * IMAGES_DEV, CODE_WIDTH:]
    lines_ref[:, 7, :] = jnp.zeros((owners, 128), F32)
    out_ref[...] = lines_ref[...].astype(BF16)
    new_code, new_first, new_second = adam_update(
        code_ref[...], table_grad, first_ref[...], second_ref[...]
    )
    new_code_ref[...] = new_code
    new_first_ref[...] = new_first
    new_second_ref[...] = new_second


def backward_kernel(
    h,
    order_ref,
    x_ref,
    acts_ref,
    cot_in_ref,
    weights_ref,
    own_ref,
    first_ref,
    second_ref,
    third_ref,
    total_ref,
    cot_ref,
):
    third = pl.program_id(0)
    groups = cot_ref.shape[0]
    rows = x_ref.shape[0]

    @pl.when(third == 0)
    def _():
        cot_ref[...] = cot_in_ref[...].astype(F32)
        total_ref[...] = jnp.zeros_like(total_ref)
        lines = []
        for c in range(4):
            sums = jnp.sum(cot_ref[:, 3 + h * 2 + c // 2, :], axis=0, keepdims=True)
            start = (c % 2) * CODE_WIDTH
            line = sums[:, start : start + CODE_WIDTH]
            lines.append(
                jnp.concatenate([line, jnp.zeros((1, NET_WIDTH - CODE_WIDTH), F32)], axis=1)
            )
        total_ref[HEAD_ROW:PARAM_ROWS, :] = jnp.concatenate(
            [jnp.zeros((4, NET_WIDTH), F32)] + lines + [jnp.zeros((8, NET_WIDTH), F32)], axis=0
        )

    cot = jnp.where(
        third == 0, cot_ref[:, 0, :], jnp.where(third == 1, cot_ref[:, 1, :], cot_ref[:, 2, :])
    )
    sums = jnp.sum(cot, axis=0, keepdims=True)
    spread = jnp.broadcast_to(cot[:, None, :], (groups, DEPTH, 128)).reshape(rows, 128)
    spread = jnp.where(depth_match(rows), spread, 0.0).astype(BF16)
    lane = iota((1, 128), 1)
    wide_lane = iota((1, NET_WIDTH), 1)
    head = weights_ref[0, HEAD_ROW:PARAM_ROWS, :].astype(F32)
    outer = mul(spread, acts_ref[LAYERS - 1], TN)[h * 64 : (h + 1) * 64]
    head_grad = jnp.sum(outer.reshape(4, DEPTH, NET_WIDTH), axis=1)
    bias_head = jnp.zeros((1, NET_WIDTH), F32)
    for c in range(4):
        value = jnp.sum(jnp.where((lane >> 4) == h * 4 + c, sums, 0.0), axis=1, keepdims=True)
        bias_head = bias_head + jnp.where(wide_lane == c, value, 0.0)
    up = mul(spread, head_tile(head, h))
    bias_lines = [None] * LAYERS
    for k in reversed(range(LAYERS)):
        pre_grad = jnp.where(acts_ref[k].astype(F32) > 0, up, 0.0).astype(BF16)
        bias_lines[k] = jnp.sum(pre_grad.astype(F32), axis=0, keepdims=True)
        if k > 0:
            start = ENC_WIDTH + (k - 1) * NET_WIDTH
            total_ref[start : start + NET_WIDTH, :] += mul(acts_ref[k - 1], pre_grad, TN)
            up = mul(pre_grad, weights_ref[0, start : start + NET_WIDTH, :], NT)
        else:
            total_ref[0:ENC_WIDTH, :] += mul(x_ref[...], pre_grad, TN)[
                h * ENC_WIDTH : (h + 1) * ENC_WIDTH
            ]
    total_ref[HEAD_ROW:PARAM_ROWS, :] += jnp.concatenate(
        [head_grad, jnp.zeros((4, NET_WIDTH), F32), bias_head]
        + bias_lines
        + [jnp.zeros((3, NET_WIDTH), F32)],
        axis=0,
    )

    @pl.when(third == THIRDS - 1)
    def _():
        quarter = own_ref.shape[0]
        for k, share_ref in enumerate((own_ref, first_ref, second_ref, third_ref)):
            start = pl.multiple_of(order_ref[k] * quarter, 8)
            share_ref[...] = total_ref[pl.ds(start, quarter), :].astype(share_ref.dtype)


def adam_kernel(
    order_ref,
    own_ref,
    first_ref,
    second_ref,
    third_ref,
    param_ref,
    one_ref,
    two_ref,
    *refs,
):
    step = pl.program_id(0)
    new_param_ref, new_one_ref, new_two_ref = refs[-3:]
    for k, share_ref in enumerate((own_ref, first_ref, second_ref, third_ref)):

        @pl.when(step == k)
        def _():
            new_param, new_one, new_two = adam_update(
                param_ref[0], share_ref[...].astype(F32), one_ref[0], two_ref[0]
            )
            new_param_ref[0] = new_param
            new_one_ref[0] = new_one
            new_two_ref[0] = new_two


def cost(micros):
    return pl.CostEstimate(
        flops=int(micros * 1e9), bytes_accessed=int(micros * 3e6), transcendentals=0
    )


def limits(mib=48):
    return pltpu.CompilerParams(vmem_limit_bytes=mib * 1024 * 1024)


def shape_of(dims, kind):
    return jax.ShapeDtypeStruct(dims, kind)


def shards(
    features,
    spacing,
    targets,
    ray_length,
    cell_id,
    slot_rank,
    image_id,
    params,
    first_moment,
    second_moment,
    code_table,
    table_first,
    table_second,
):
    groups = lax.axis_size("expert")
    places = groups * DEPTH
    cell_rows = cell_id.T
    rank_rows = slot_rank.T
    outgoing = pl.pallas_call(
        dispatch_kernel,
        out_shape=shape_of((places, THIRDS * 128), BF16),
        in_specs=[pl.BlockSpec(memory_space=pl.ANY)] * 3,
        scratch_shapes=[
            pltpu.VMEM((places, SAMPLES * RAYS), BF16),
            pltpu.VMEM((THIRDS * 128, SAMPLES * RAYS), BF16),
            pltpu.VMEM((SAMPLES, ENC_WIDTH, RAYS), BF16),
            pltpu.VMEM((SAMPLES, RAYS), jnp.int32),
            pltpu.VMEM((SAMPLES, RAYS), jnp.int32),
            pltpu.SemaphoreType.DMA((3,)),
        ],
        compiler_params=limits(59),
        name="dispatch",
    )(jnp.transpose(features, (1, 2, 0)), cell_rows, rank_rows)
    arrived = lax.all_to_all(outgoing, "expert", split_axis=0, concat_axis=0, tiled=True)

    slots = THIRDS * places
    vmem = pl.BlockSpec(memory_space=pltpu.VMEM)
    anywhere = pl.BlockSpec(memory_space=pl.ANY)
    acts_shape = shape_of((LAYERS, slots, NET_WIDTH), BF16)
    *acts, raw_out, weights = pl.pallas_call(
        forward_kernel,
        out_shape=[
            acts_shape,
            acts_shape,
            shape_of((groups, 8, 128), BF16),
            shape_of((2, PARAM_ROWS, NET_WIDTH), BF16),
        ],
        out_specs=[anywhere, anywhere, vmem, vmem],
        scratch_shapes=[
            pltpu.VMEM((groups, 8, 128), F32),
            pltpu.VMEM((2 * LAYERS, slots, NET_WIDTH), BF16),
            pltpu.SemaphoreType.DMA((2 * LAYERS,)),
        ],
        compiler_params=limits(48),
        name="forward",
    )(arrived, params)
    returned = lax.all_to_all(raw_out, "expert", split_axis=0, concat_axis=0, tiled=True)

    table_shape = shape_of(code_table.shape, F32)
    cot_out, loss, new_table, new_table_first, new_table_second = pl.pallas_call(
        ray_kernel,
        out_shape=[
            shape_of((groups, 8, 128), BF16),
            shape_of((1, RAYS), F32),
            table_shape,
            table_shape,
            table_shape,
        ],
        scratch_shapes=[
            pltpu.VMEM((512, PARTS * groups), BF16),
            pltpu.VMEM((4, SAMPLES, RAYS), F32),
            pltpu.VMEM((groups, 8, 128), F32),
        ],
        compiler_params=limits(16),
        name="rays",
    )(
        returned,
        cell_rows,
        rank_rows,
        image_id.reshape(1, RAYS),
        ray_length.reshape(1, RAYS),
        spacing.T,
        targets,
        code_table,
        table_first,
        table_second,
    )
    cot_in = lax.all_to_all(cot_out, "expert", split_axis=0, concat_axis=0, tiled=True)

    copies = lax.axis_size("dp")
    quarter = -(-PARAM_ROWS // (8 * copies)) * 8
    turns = jnp.arange(copies, dtype=jnp.int32)
    position = lax.axis_index("dp")
    lent = lambda *dims: pl.BlockSpec(dims, lambda i, order: (0,) * len(dims))

    def send(value, distance):
        return lax.ppermute(value, "dp", [(i, (i + distance) % copies) for i in range(copies)])

    def gradient(h):
        return pl.pallas_call(
            functools.partial(backward_kernel, h),
            grid_spec=pltpu.PrefetchScalarGridSpec(
                num_scalar_prefetch=1,
                grid=(THIRDS,),
                in_specs=[
                    pl.BlockSpec((places, 128), lambda i, order: (0, i)),
                    pl.BlockSpec((LAYERS, places, NET_WIDTH), lambda i, order: (0, i, 0)),
                    lent(groups, 8, 128),
                    pl.BlockSpec((1, PARAM_ROWS, NET_WIDTH), lambda i, order: (h, 0, 0)),
                ],
                out_specs=[lent(quarter, NET_WIDTH)] * 4,
                scratch_shapes=[
                    pltpu.VMEM((copies * quarter, NET_WIDTH), F32),
                    pltpu.VMEM((groups, 8, 128), F32),
                ],
            ),
            out_shape=[shape_of((quarter, NET_WIDTH), F32)]
            + [shape_of((quarter, NET_WIDTH), BF16)] * 3,
            compiler_params=limits(48),
            cost_estimate=cost(6.0),
            name="backward",
        )((position + turns) % copies, arrived, acts[h], cot_in, weights)

    def collect(shares, forwarded):
        share = shares[0]
        for k in (2, 1, 3):
            share = share + send(shares[k], k).astype(F32)
        share = share.astype(BF16)
        behind, ahead = send(share, 1), send(share, 3)
        far = send(ahead, 3) if forwarded else send(share, 2)
        return share, behind, far, ahead

    def update(h, pieces, earlier):
        block = pl.BlockSpec((1, quarter, NET_WIDTH), lambda i, order: (h, order[i], 0))
        return pl.pallas_call(
            adam_kernel,
            grid_spec=pltpu.PrefetchScalarGridSpec(
                num_scalar_prefetch=1,
                grid=(copies,),
                in_specs=[lent(quarter, NET_WIDTH)] * 4
                + [block] * 3
                + [pl.BlockSpec(memory_space=pl.ANY)] * len(earlier),
                out_specs=[block] * 3,
            ),
            out_shape=[shape_of(params.shape, F32)] * 3,
            input_output_aliases={8 + i: i for i in range(len(earlier))},
            compiler_params=limits(12),
            cost_estimate=cost(2.0),
            name="adam",
        )(
            (position - turns) % copies,
            *pieces,
            params,
            first_moment,
            second_moment,
            *earlier,
        )

    pieces = [collect(gradient(h), h == 1) for h in range(2)]
    updated = update(0, pieces[0], ())
    new_params, new_first, new_second = update(1, pieces[1], updated)
    return (
        loss.reshape(RAYS),
        new_params,
        new_first,
        new_second,
        new_table,
        new_table_first,
        new_table_second,
    )


def solution(mesh):
    rays = ("expert", "dp")
    table = P(rays, None)
    block = P("expert", None, None)
    return jax.shard_map(
        shards,
        mesh=mesh,
        in_specs=(
            P(rays, None, None),
            P(rays, None),
            P(None, rays),
            P(rays),
            P(rays, None),
            P(rays, None),
            P(rays),
            block,
            block,
            block,
            table,
            table,
            table,
        ),
        out_specs=(P(rays), block, block, block, table, table, table),
        check_vma=False,
    )
```

```python
import functools

import jax
import jax.numpy as jnp
from jax import lax
from jax.experimental import pallas as pl
from jax.experimental.pallas import tpu as pltpu
from jax.sharding import PartitionSpec as P

NET_WIDTH = 256
CODE_WIDTH = 64
ENC_WIDTH = 64
LAYERS = 4
SAMPLES = 32
RAYS = 128
IMAGES_DEV = 16
CAPACITY = 48
DEPTH = 16
THIRDS = CAPACITY // DEPTH
PARTS = 2
HEAD_ROW = ENC_WIDTH + (LAYERS - 1) * NET_WIDTH
PARAM_ROWS = HEAD_ROW + 16

F32 = jnp.float32
BF16 = jnp.bfloat16

BETA_ONE = 0.9
BETA_TWO = 0.999
LEARN_RATE = 0.001
ADAM_EPS = 1e-08
CORRECT_ONE = 1.0 - 0.9**10
CORRECT_TWO = 1.0 - 0.999**10

NN = (((1,), (0,)), ((), ()))
NT = (((1,), (1,)), ((), ()))
TN = (((0,), (0,)), ((), ()))


def mul(left, right, dims=NN):
    return lax.dot_general(left, right, dims, preferred_element_type=F32)


def iota(shape, dim):
    return lax.broadcasted_iota(jnp.int32, shape, dim)


def three_parts(value):
    high = value.astype(BF16)
    rest = value - high.astype(F32)
    middle = rest.astype(BF16)
    low = (rest - middle.astype(F32)).astype(BF16)
    return [high, middle, low]


def adam_update(param_now, gradient, moment_one, moment_two):
    new_one = BETA_ONE * moment_one + (1.0 - BETA_ONE) * gradient
    new_two = BETA_TWO * moment_two + (1.0 - BETA_TWO) * gradient * gradient
    update = LEARN_RATE * (new_one / CORRECT_ONE) / (jnp.sqrt(new_two / CORRECT_TWO) + ADAM_EPS)
    return (param_now - update, new_one, new_two)


def dispatch_kernel(
    feat_in, cell_in, rank_in, out_ref, hot_ref, rows_ref, feat_ref, cell_ref, rank_ref, sems
):
    places = out_ref.shape[0]
    moves = [
        pltpu.make_async_copy(source, target, sems.at[i])
        for i, (source, target) in enumerate(
            ((cell_in, cell_ref), (rank_in, rank_ref), (feat_in, feat_ref))
        )
    ]
    for move in moves:
        move.start()
    for move in moves:
        move.wait()
    for i in range(SAMPLES):
        cell = cell_ref[i : i + 1, :]
        rank = rank_ref[i : i + 1, :]
        place = jnp.where(rank >= 0, (cell >> 1) * DEPTH + (rank & (DEPTH - 1)), -1)
        inner = (rank >> 4) * 2 + (cell & 1)
        span = slice(i * RAYS, (i + 1) * RAYS)
        hot_ref[:, span] = jnp.where(iota((places, RAYS), 0) == place, 1.0, 0.0).astype(BF16)
        feat = feat_ref[i].astype(F32)
        for q in range(THIRDS * 2):
            rows_ref[q * ENC_WIDTH : (q + 1) * ENC_WIDTH, span] = jnp.where(
                inner == q, feat, 0.0
            ).astype(BF16)
    out_ref[...] = mul(hot_ref[...], rows_ref[...], NT).astype(BF16)


def depth_match(rows):
    return (iota((rows, 128), 0) & (DEPTH - 1)) == (iota((rows, 128), 1) & (DEPTH - 1))


def first_matrix(weights_ref, held):
    matrix = weights_ref[held, 0:ENC_WIDTH, :]
    blank = jnp.zeros_like(matrix)
    return jnp.concatenate([matrix, blank] if held == 0 else [blank, matrix], axis=0)


def hidden_matrix(weights_ref, held, layer):
    start = ENC_WIDTH + (layer - 1) * NET_WIDTH
    return weights_ref[held, start : start + NET_WIDTH, :]


def head_tile(head, held):
    rows = jnp.concatenate(
        [jnp.broadcast_to(head[c : c + 1, :], (DEPTH, NET_WIDTH)) for c in range(4)], axis=0
    )
    blank = jnp.zeros_like(rows)
    return jnp.concatenate([rows, blank] if held == 0 else [blank, rows], axis=0).astype(BF16)


def slot_rows(x_ref):
    return jnp.concatenate([x_ref[:, j * 128 : (j + 1) * 128] for j in range(THIRDS)], axis=0)


def forward_kernel(
    x_ref, params_ref, acts0_ref, acts1_ref, out_ref, weights_ref, lines_ref, held_ref, sems
):
    groups = out_ref.shape[0]
    rows = held_ref.shape[1]
    moves = []
    weights_ref[...] = params_ref[...].astype(BF16)
    heads = [weights_ref[h, HEAD_ROW:PARAM_ROWS, :].astype(F32) for h in range(2)]
    for j in range(4):
        h, c = j // 2, (j % 2) * 2
        pair = jnp.concatenate(
            [heads[h][4 + c : 5 + c, :CODE_WIDTH], heads[h][5 + c : 6 + c, :CODE_WIDTH]], axis=1
        )
        lines_ref[:, 3 + j, :] = jnp.broadcast_to(pair, (groups, 128))
    lane = iota((1, 128), 1)
    shift = jnp.zeros((1, 128), F32)
    total = jnp.zeros((rows, 128), F32)
    for h, acts_ref in enumerate((acts0_ref, acts1_ref)):
        current = slot_rows(x_ref)
        for k in range(LAYERS):
            matrix = first_matrix(weights_ref, h) if k == 0 else hidden_matrix(weights_ref, h, k)
            preact = mul(current, matrix) + heads[h][9 + k : 10 + k, :]
            current = jnp.maximum(preact, 0.0).astype(BF16)
            place = h * LAYERS + k
            held_ref[place] = current
            move = pltpu.make_async_copy(held_ref.at[place], acts_ref.at[k], sems.at[place])
            move.start()
            moves.append(move)
        total = total + mul(current, head_tile(heads[h], h), NT)
        for c in range(4):
            shift = shift + jnp.where((lane >> 4) == h * 4 + c, heads[h][8:9, c : c + 1], 0.0)
    total = jnp.where(depth_match(rows), total + shift, 0.0)
    raw = jnp.sum(total.reshape(THIRDS * groups, DEPTH, 128), axis=1)
    low = raw - raw.astype(BF16).astype(F32)
    density = []
    for j in range(THIRDS):
        span = slice(j * groups, (j + 1) * groups)
        lines_ref[:, j, :] = raw[span]
        density += [low[span, 0:DEPTH], low[span, 64 : 64 + DEPTH]]
    lines_ref[:, 7, :] = jnp.concatenate(density + [jnp.zeros((groups, 32), F32)], axis=1)
    out_ref[...] = lines_ref[...].astype(BF16)
    for move in moves:
        move.wait()


def one_sample_row(cell_ref, rank_ref, image, i, owners):
    cell = cell_ref[pl.ds(i, 1), :]
    rank = rank_ref[pl.ds(i, 1), :]
    live = rank >= 0
    owner = jnp.where(live, cell >> 1, -1)
    hot = jnp.where(iota((owners, RAYS), 0) == owner, 1.0, 0.0).astype(BF16)
    held = cell & 1
    slot = jnp.where(live, ((rank >> 4) * 2 + held) * DEPTH + (rank & (DEPTH - 1)), -1)
    code = jnp.where(live, held * IMAGES_DEV + image, -1)
    slot_mask = iota((THIRDS * 2 * DEPTH, RAYS), 0) == slot
    code_mask = iota((2 * IMAGES_DEV, RAYS), 0) == code
    masks = [slot_mask[q * DEPTH : (q + 1) * DEPTH] for q in range(THIRDS * 2)]
    masks += [code_mask[h * IMAGES_DEV : (h + 1) * IMAGES_DEV] for h in range(2)]
    return hot, masks


def running_sum(value):
    step = 1
    while step < SAMPLES:
        value = value + jnp.concatenate(
            [jnp.zeros((step, RAYS), F32), value[: SAMPLES - step]], axis=0
        )
        step *= 2
    return value


def running_sum_back(value):
    step = 1
    while step < SAMPLES:
        value = value + jnp.concatenate([value[step:], jnp.zeros((step, RAYS), F32)], axis=0)
        step *= 2
    return value


def ray_kernel(
    back_ref,
    cell_ref,
    rank_ref,
    image_ref,
    length_ref,
    spacing_ref,
    targets_ref,
    code_ref,
    first_ref,
    second_ref,
    out_ref,
    loss_ref,
    new_code_ref,
    new_first_ref,
    new_second_ref,
    table_ref,
    raw_ref,
    lines_ref,
):
    owners = back_ref.shape[0]
    image = image_ref[...] & (IMAGES_DEV - 1)
    code = code_ref[...].astype(BF16).astype(F32)
    tile = jnp.concatenate([code] * 8, axis=0)
    tile = jnp.concatenate([tile, tile], axis=1)
    block_row = iota((128, 128), 0) >> 4
    block_lane = iota((128, 128), 1) >> 6
    code_blocks = [
        jnp.where(block_row == 2 * j + block_lane, tile, 0.0).astype(BF16) for j in range(4)
    ]
    lines_ref[...] = back_ref[...].astype(F32)
    queries = [lines_ref[:, 3 + j, :].astype(BF16) for j in range(4)]
    code_part = mul(queries[0], code_blocks[0], NT)
    for j in range(1, 4):
        code_part = code_part + mul(queries[j], code_blocks[j], NT)
    code_parts = three_parts(code_part.T)
    lows = lines_ref[:, 7, :]
    blank = jnp.zeros((owners, 64 - DEPTH), F32)
    highs, rests = [], []
    for j in range(THIRDS):
        start = j * 2 * DEPTH
        rest = [lows[:, start : start + DEPTH], blank]
        rest += [lows[:, start + DEPTH : start + 2 * DEPTH], blank]
        highs.append(lines_ref[:, j, :].T.astype(BF16))
        rests.append(jnp.concatenate(rest, axis=1).T.astype(BF16))
    table_ref[...] = jnp.concatenate(
        [
            jnp.concatenate(highs + code_parts[0:1], axis=0),
            jnp.concatenate(rests + code_parts[1:2], axis=0),
        ],
        axis=1,
    )

    def pick(i, carry):
        sides = [one_sample_row(cell_ref, rank_ref, image, 2 * i + half, owners) for half in range(2)]
        hots = jnp.concatenate([side[0] for side in sides], axis=1)
        found = mul(table_ref[...], jnp.concatenate([hots] * PARTS, axis=0))
        for half in range(2):
            masks = sides[half][1]
            for c in range(4):
                total = jnp.zeros((DEPTH, RAYS), F32)
                for q in range(THIRDS * 2 + 2):
                    start = q * 64 + c * DEPTH
                    total = total + jnp.where(
                        masks[q], found[start : start + DEPTH, half * RAYS : (half + 1) * RAYS], 0.0
                    )
                raw_ref[c, pl.ds(2 * i + half, 1), :] = jnp.sum(total, axis=0, keepdims=True)
        return carry

    lax.fori_loop(0, SAMPLES // 2, pick, 0, unroll=4)

    spacing = spacing_ref[...]
    live = jnp.where(iota((SAMPLES, RAYS), 0) < length_ref[...], 1.0, 0.0)
    raw_density = raw_ref[0]
    small = jnp.exp(-jnp.abs(raw_density))
    density = jnp.maximum(raw_density, 0.0) + jnp.log1p(small)
    slope = jnp.where(raw_density >= 0, 1.0, small) / (1.0 + small)
    colors = []
    for c in range(3):
        raw_color = raw_ref[1 + c]
        tail = jnp.exp(-jnp.abs(raw_color))
        colors.append(jnp.where(raw_color >= 0, 1.0, tail) / (1.0 + tail))
    reach = spacing * live
    tau = density * reach
    before = running_sum(tau) - tau
    passed = jnp.exp(-before)
    kept = jnp.exp(-tau)
    weight = passed * (1.0 - kept)
    gaps = []
    loss = jnp.zeros((1, RAYS), F32)
    for c in range(3):
        gap = jnp.sum(weight * colors[c], axis=0, keepdims=True) - targets_ref[c : c + 1, :]
        gaps.append(gap)
        loss = loss + gap * gap
    loss_ref[...] = 0.5 * loss
    pull = gaps[0] * colors[0] + gaps[1] * colors[1] + gaps[2] * colors[2]
    behind = weight * pull
    tau_grad = pull * passed * kept - (running_sum_back(behind) - behind)
    raw_ref[0] = (tau_grad * reach * slope).astype(BF16).astype(F32)
    for c in range(3):
        raw_ref[1 + c] = (
            (weight * gaps[c] * (colors[c] * (1.0 - colors[c]))).astype(BF16).astype(F32)
        )

    def put(i, total):
        hots, rows = [], []
        for half in range(2):
            hot, masks = one_sample_row(cell_ref, rank_ref, image, 2 * i + half, owners)
            cots = [raw_ref[c, pl.ds(2 * i + half, 1), :] for c in range(4)]
            hots.append(hot)
            rows.append(
                jnp.concatenate(
                    [
                        jnp.where(masks[q], cots[c], 0.0)
                        for q in range(THIRDS * 2 + 2)
                        for c in range(4)
                    ],
                    axis=0,
                ).astype(BF16)
            )
        return total + mul(
            jnp.concatenate(rows, axis=1), jnp.concatenate(hots, axis=1), NT
        )

    placed = lax.fori_loop(
        0, SAMPLES // 2, put, jnp.zeros((512, owners), F32), unroll=4
    )
    for j in range(THIRDS):
        lines_ref[:, j, :] = placed[j * 128 : (j + 1) * 128].T
    image_sums = placed[384:512]
    sums_parts = three_parts(image_sums)
    sums_wide = jnp.concatenate(sums_parts, axis=1)
    sums_flip = jnp.concatenate(three_parts(image_sums.T), axis=1)
    table_grad = jnp.zeros((IMAGES_DEV, CODE_WIDTH), F32)
    for j in range(4):
        lines_ref[:, 3 + j, :] = mul(sums_flip, jnp.concatenate([code_blocks[j]] * 3, axis=0))
        product = mul(sums_wide, jnp.concatenate([queries[j]] * 3, axis=0))
        low = 2 * j * IMAGES_DEV
        table_grad = table_grad + product[low : low + IMAGES_DEV, :CODE_WIDTH]
        table_grad = table_grad + product[low + IMAGES_DEV : low + 2 * IMAGES_DEV, CODE_WIDTH:]
    lines_ref[:, 7, :] = jnp.zeros((owners, 128), F32)
    out_ref[...] = lines_ref[...].astype(BF16)
    new_code, new_first, new_second = adam_update(
        code_ref[...], table_grad, first_ref[...], second_ref[...]
    )
    new_code_ref[...] = new_code
    new_first_ref[...] = new_first
    new_second_ref[...] = new_second


def backward_kernel(
    h,
    order_ref,
    x_ref,
    acts_ref,
    cot_in_ref,
    weights_ref,
    own_ref,
    first_ref,
    second_ref,
    third_ref,
    total_ref,
    cot_ref,
):
    third = pl.program_id(0)
    groups = cot_ref.shape[0]
    rows = x_ref.shape[0]

    @pl.when(third == 0)
    def _():
        cot_ref[...] = cot_in_ref[...].astype(F32)
        total_ref[...] = jnp.zeros_like(total_ref)
        lines = []
        for c in range(4):
            sums = jnp.sum(cot_ref[:, 3 + h * 2 + c // 2, :], axis=0, keepdims=True)
            start = (c % 2) * CODE_WIDTH
            line = sums[:, start : start + CODE_WIDTH]
            lines.append(
                jnp.concatenate([line, jnp.zeros((1, NET_WIDTH - CODE_WIDTH), F32)], axis=1)
            )
        total_ref[HEAD_ROW:PARAM_ROWS, :] = jnp.concatenate(
            [jnp.zeros((4, NET_WIDTH), F32)] + lines + [jnp.zeros((8, NET_WIDTH), F32)], axis=0
        )

    cot = jnp.where(
        third == 0, cot_ref[:, 0, :], jnp.where(third == 1, cot_ref[:, 1, :], cot_ref[:, 2, :])
    )
    sums = jnp.sum(cot, axis=0, keepdims=True)
    spread = jnp.broadcast_to(cot[:, None, :], (groups, DEPTH, 128)).reshape(rows, 128)
    spread = jnp.where(depth_match(rows), spread, 0.0).astype(BF16)
    lane = iota((1, 128), 1)
    wide_lane = iota((1, NET_WIDTH), 1)
    head = weights_ref[0, HEAD_ROW:PARAM_ROWS, :].astype(F32)
    outer = mul(spread, acts_ref[LAYERS - 1], TN)[h * 64 : (h + 1) * 64]
    head_grad = jnp.sum(outer.reshape(4, DEPTH, NET_WIDTH), axis=1)
    bias_head = jnp.zeros((1, NET_WIDTH), F32)
    for c in range(4):
        value = jnp.sum(jnp.where((lane >> 4) == h * 4 + c, sums, 0.0), axis=1, keepdims=True)
        bias_head = bias_head + jnp.where(wide_lane == c, value, 0.0)
    up = mul(spread, head_tile(head, h))
    bias_lines = [None] * LAYERS
    for k in reversed(range(LAYERS)):
        pre_grad = jnp.where(acts_ref[k] > 0, up.astype(BF16), jnp.zeros((), BF16))
        bias_lines[k] = jnp.sum(pre_grad.astype(F32), axis=0, keepdims=True)
        if k > 0:
            start = ENC_WIDTH + (k - 1) * NET_WIDTH
            total_ref[start : start + NET_WIDTH, :] += mul(acts_ref[k - 1], pre_grad, TN)
            up = mul(pre_grad, weights_ref[0, start : start + NET_WIDTH, :], NT)
        else:
            total_ref[0:ENC_WIDTH, :] += mul(x_ref[...], pre_grad, TN)[
                h * ENC_WIDTH : (h + 1) * ENC_WIDTH
            ]
    total_ref[HEAD_ROW:PARAM_ROWS, :] += jnp.concatenate(
        [head_grad, jnp.zeros((4, NET_WIDTH), F32), bias_head]
        + bias_lines
        + [jnp.zeros((3, NET_WIDTH), F32)],
        axis=0,
    )

    @pl.when(third == THIRDS - 1)
    def _():
        quarter = own_ref.shape[0]
        for k, share_ref in enumerate((own_ref, first_ref, second_ref, third_ref)):
            start = pl.multiple_of(order_ref[k] * quarter, 8)
            share_ref[...] = total_ref[pl.ds(start, quarter), :].astype(share_ref.dtype)


def adam_kernel(
    order_ref,
    own_ref,
    first_ref,
    second_ref,
    third_ref,
    param_ref,
    one_ref,
    two_ref,
    *refs,
):
    step = pl.program_id(0)
    new_param_ref, new_one_ref, new_two_ref = refs[-3:]
    for k, share_ref in enumerate((own_ref, first_ref, second_ref, third_ref)):

        @pl.when(step == k)
        def _():
            new_param, new_one, new_two = adam_update(
                param_ref[0], share_ref[...].astype(F32), one_ref[0], two_ref[0]
            )
            new_param_ref[0] = new_param
            new_one_ref[0] = new_one
            new_two_ref[0] = new_two


def cost(micros):
    return pl.CostEstimate(
        flops=int(micros * 1e9), bytes_accessed=int(micros * 3e6), transcendentals=0
    )


def limits(mib=48):
    return pltpu.CompilerParams(vmem_limit_bytes=mib * 1024 * 1024)


def shape_of(dims, kind):
    return jax.ShapeDtypeStruct(dims, kind)


def shards(
    features,
    spacing,
    targets,
    ray_length,
    cell_id,
    slot_rank,
    image_id,
    params,
    first_moment,
    second_moment,
    code_table,
    table_first,
    table_second,
):
    groups = lax.axis_size("expert")
    places = groups * DEPTH
    cell_rows = cell_id.T
    rank_rows = slot_rank.T
    outgoing = pl.pallas_call(
        dispatch_kernel,
        out_shape=shape_of((places, THIRDS * 128), BF16),
        in_specs=[pl.BlockSpec(memory_space=pl.ANY)] * 3,
        scratch_shapes=[
            pltpu.VMEM((places, SAMPLES * RAYS), BF16),
            pltpu.VMEM((THIRDS * 128, SAMPLES * RAYS), BF16),
            pltpu.VMEM((SAMPLES, ENC_WIDTH, RAYS), BF16),
            pltpu.VMEM((SAMPLES, RAYS), jnp.int32),
            pltpu.VMEM((SAMPLES, RAYS), jnp.int32),
            pltpu.SemaphoreType.DMA((3,)),
        ],
        compiler_params=limits(59),
        name="dispatch",
    )(jnp.transpose(features, (1, 2, 0)), cell_rows, rank_rows)
    arrived = lax.all_to_all(outgoing, "expert", split_axis=0, concat_axis=0, tiled=True)

    slots = THIRDS * places
    vmem = pl.BlockSpec(memory_space=pltpu.VMEM)
    anywhere = pl.BlockSpec(memory_space=pl.ANY)
    acts_shape = shape_of((LAYERS, slots, NET_WIDTH), BF16)
    *acts, raw_out, weights = pl.pallas_call(
        forward_kernel,
        out_shape=[
            acts_shape,
            acts_shape,
            shape_of((groups, 8, 128), BF16),
            shape_of((2, PARAM_ROWS, NET_WIDTH), BF16),
        ],
        out_specs=[anywhere, anywhere, vmem, vmem],
        scratch_shapes=[
            pltpu.VMEM((groups, 8, 128), F32),
            pltpu.VMEM((2 * LAYERS, slots, NET_WIDTH), BF16),
            pltpu.SemaphoreType.DMA((2 * LAYERS,)),
        ],
        compiler_params=limits(48),
        name="forward",
    )(arrived, params)
    returned = lax.all_to_all(raw_out, "expert", split_axis=0, concat_axis=0, tiled=True)

    table_shape = shape_of(code_table.shape, F32)
    cot_out, loss, new_table, new_table_first, new_table_second = pl.pallas_call(
        ray_kernel,
        out_shape=[
            shape_of((groups, 8, 128), BF16),
            shape_of((1, RAYS), F32),
            table_shape,
            table_shape,
            table_shape,
        ],
        scratch_shapes=[
            pltpu.VMEM((512, PARTS * groups), BF16),
            pltpu.VMEM((4, SAMPLES, RAYS), F32),
            pltpu.VMEM((groups, 8, 128), F32),
        ],
        compiler_params=limits(16),
        name="rays",
    )(
        returned,
        cell_rows,
        rank_rows,
        image_id.reshape(1, RAYS),
        ray_length.reshape(1, RAYS),
        spacing.T,
        targets,
        code_table,
        table_first,
        table_second,
    )
    cot_in = lax.all_to_all(cot_out, "expert", split_axis=0, concat_axis=0, tiled=True)

    copies = lax.axis_size("dp")
    quarter = -(-PARAM_ROWS // (8 * copies)) * 8
    turns = jnp.arange(copies, dtype=jnp.int32)
    position = lax.axis_index("dp")
    lent = lambda *dims: pl.BlockSpec(dims, lambda i, order: (0,) * len(dims))

    def send(value, distance):
        return lax.ppermute(value, "dp", [(i, (i + distance) % copies) for i in range(copies)])

    def gradient(h):
        return pl.pallas_call(
            functools.partial(backward_kernel, h),
            grid_spec=pltpu.PrefetchScalarGridSpec(
                num_scalar_prefetch=1,
                grid=(THIRDS,),
                in_specs=[
                    pl.BlockSpec((places, 128), lambda i, order: (0, i)),
                    pl.BlockSpec((LAYERS, places, NET_WIDTH), lambda i, order: (0, i, 0)),
                    lent(groups, 8, 128),
                    pl.BlockSpec((1, PARAM_ROWS, NET_WIDTH), lambda i, order: (h, 0, 0)),
                ],
                out_specs=[lent(quarter, NET_WIDTH)] * 4,
                scratch_shapes=[
                    pltpu.VMEM((copies * quarter, NET_WIDTH), F32),
                    pltpu.VMEM((groups, 8, 128), F32),
                ],
            ),
            out_shape=[shape_of((quarter, NET_WIDTH), F32)]
            + [shape_of((quarter, NET_WIDTH), BF16)] * 3,
            compiler_params=limits(48),
            cost_estimate=cost(6.0),
            name="backward",
        )((position + turns) % copies, arrived, acts[h], cot_in, weights)

    def collect(shares):
        share = shares[0]
        for k in (2, 1, 3):
            share = share + send(shares[k], k).astype(F32)
        share = share.astype(BF16)
        behind, ahead = send(share, 1), send(share, 3)
        return share, behind, send(ahead, 3), ahead

    def update(h, pieces, earlier):
        block = pl.BlockSpec((1, quarter, NET_WIDTH), lambda i, order: (h, order[i], 0))
        return pl.pallas_call(
            adam_kernel,
            grid_spec=pltpu.PrefetchScalarGridSpec(
                num_scalar_prefetch=1,
                grid=(copies,),
                in_specs=[lent(quarter, NET_WIDTH)] * 4
                + [block] * 3
                + [pl.BlockSpec(memory_space=pl.ANY)] * len(earlier),
                out_specs=[block] * 3,
            ),
            out_shape=[shape_of(params.shape, F32)] * 3,
            input_output_aliases={8 + i: i for i in range(len(earlier))},
            compiler_params=limits(12),
            cost_estimate=cost(2.0),
            name="adam",
        )(
            (position - turns) % copies,
            *pieces,
            params,
            first_moment,
            second_moment,
            *earlier,
        )

    pieces = [collect(gradient(h)) for h in range(2)]
    updated = update(0, pieces[0], ())
    new_params, new_first, new_second = update(1, pieces[1], updated)
    return (
        loss.reshape(RAYS),
        new_params,
        new_first,
        new_second,
        new_table,
        new_table_first,
        new_table_second,
    )


def solution(mesh):
    rays = ("expert", "dp")
    table = P(rays, None)
    block = P("expert", None, None)
    return jax.shard_map(
        shards,
        mesh=mesh,
        in_specs=(
            P(rays, None, None),
            P(rays, None),
            P(None, rays),
            P(rays),
            P(rays, None),
            P(rays, None),
            P(rays),
            block,
            block,
            block,
            table,
            table,
            table,
        ),
        out_specs=(P(rays), block, block, block, table, table, table),
        check_vma=False,
    )
```
